256 devices in a mesh: tr: 64 (over z, x, core), fq: 4 (over y).
Axes of the slice: x: 4, y: 4, z: 8, core: 2. Of those that a mesh axis runs over, the one named last changes fastest.
Arguments:
- traces: bfloat16 [524288, 1024], P('tr', 'fq'), may hold values from -6 to 6
- shot_index: int32 [524288], P('tr'), may hold values from 0 to 8191, as said below
- receiver_index: int32 [524288], P('tr'), may hold values from 0 to 8191
- live_counts: int32 [64], P('tr'), may hold values from 1 to 8192, 393216 in all
- shot_terms: float32 [8192, 512], P('tr', 'fq'), may hold values from 1 to 2.2
- receiver_terms: float32 [8192, 512], P('tr', 'fq'), may hold values from 1 to 2.2
Outputs:
- shot_sums: float32 [8192, 512], P('tr', 'fq')
- receiver_sums: float32 [8192, 512], P('tr', 'fq')
The draws below stay inside these ranges and needn't reach their ends.
Inputs may be any that keep to these rules, and one draw needn't show every extreme that they name: `shot_index`: A trace slot of block b (slots b * 8192 to (b + 1) * 8192 - 1) has a shot among (b - 1) * 128 to (b + 2) * 128 - 1.
All inputs are finite; a program needn't handle non-finite values. No bound on the sum of `live_counts` on one device may be relied on, other than what follows from the above.
Results may differ from the reference program's by a relative error of at most 0.0017.
Values may be sent and summed in bfloat16 or wider, within the bound.
No kernel may reach another device: no remote copies, remote signals or barrier semaphores. Data moves between devices by JAX's collectives and lax.ppermute only.
A program may use at most 128 MiB of HBM per device.

```python
import math
import jax
import jax.numpy as jnp
import numpy as np
from jax import lax

NT = 1024
F = 512
TR_DEV = 8192
SHOT_DEV = 128
TRACES = 524288
NSHOT = 8192
NREC = 8192
N_TR = 64


def draw_shot_index(key, part):
    key = jax.random.fold_in(key, 11)
    owner = jnp.arange(TRACES, dtype=jnp.int32) // TR_DEV
    offset = jax.random.randint(key, (TRACES,), -SHOT_DEV, 2 * SHOT_DEV, dtype=jnp.int32)
    return jnp.clip(owner * SHOT_DEV + offset, 0, NSHOT - 1).astype(jnp.int32)


def set_ends(drawn, key, smallest, top_value):
    dims = drawn.shape
    spot = [jax.random.randint(jax.random.fold_in(key, axis), (), 0, dims[axis]) for axis in range(len(dims))]
    drawn = drawn.at[tuple(spot)].set(smallest)
    longest = dims.index(max(dims))
    spot[longest] = (spot[longest] + 1) % dims[longest]
    return drawn.at[tuple(spot)].set(top_value)


def levels(rng, dims, split, least, top_value):
    gain, own = 1.0, jax.random.fold_in(rng, 6)
    for axis_at, blocks in split:
        heights = jnp.exp(jax.random.uniform(jax.random.fold_in(own, axis_at), (blocks,), jnp.float32, least / len(split), top_value / len(split)))
        gain = gain * jnp.repeat(heights, dims[axis_at] // blocks).reshape([-1 if axis == axis_at else 1 for axis in range(len(dims))])
    return gain


def split_up(count, total, bound, lean):
    weights = [(1 << 20) // math.isqrt(grade ** lean) + 1 for grade in range(2, count + 1)]
    surplus, given = total - bound - (count - 1), [1] * (count - 1)
    while surplus > 0:
        free = [i for i in range(count - 1) if given[i] < bound]
        whole, budget = sum([weights[i] for i in free]), surplus
        for i in free:
            extra = min(bound - given[i], max(1, budget * weights[i] // whole), surplus)
            given[i] = given[i] + extra
            surplus = surplus - extra
    return np.array([bound] + given)


def ragged_sizes(rng, count, total, most, lean):
    if count == 2:
        one = jax.random.randint(rng, (), max(1, total - most), min(most, total - 1) + 1)
        return jnp.stack([one, total - one])
    tallies = jnp.asarray(split_up(count, total, most, lean), jnp.int32)
    twos = (count - 1) // 2
    source_of, sink = tallies[1:1 + 2 * twos:2], tallies[2:2 + 2 * twos:2]
    slack = jnp.minimum(source_of - 1, most - sink)
    moved = jax.random.randint(jax.random.fold_in(rng, 1), (twos,), 0, 1 << 20) % (slack + 1)
    tallies = tallies.at[1:1 + 2 * twos:2].set(source_of - moved).at[2:2 + 2 * twos:2].set(sink + moved)
    return tallies[jax.random.permutation(jax.random.fold_in(rng, 2), count)]


def centred(key, dims, scale, reach, pieces=(), kind=jnp.bfloat16):
    gain = levels(key, dims, pieces, -0.22, 0.18) if pieces else 1.0
    entries = jax.random.normal(key, dims, jnp.float32) * scale * gain
    return jnp.minimum(jnp.maximum(entries, -reach), reach).astype(kind)


def setup_inputs(seed: int = 0) -> dict:
    streams_of = jax.random.split(jax.random.key(seed), 7)
    return {
        "traces": centred(streams_of[0], (TRACES, NT), 1.0, 6.0, ((0, 64), (1, 4))),
        "shot_index": draw_shot_index(jax.random.fold_in(streams_of[6], 71), 0),
        "receiver_index": set_ends(jax.random.randint(streams_of[2], (TRACES,), 0, NREC), jax.random.fold_in(streams_of[2], 1), 0, NREC - 1).astype(jnp.int32),
        "live_counts": ragged_sizes(streams_of[3], N_TR, N_TR * TR_DEV * 3 // 4, TR_DEV, 0).astype(jnp.int32),
        "shot_terms": jnp.clip(1.0 + 1.2 * jax.random.uniform(streams_of[4], (NSHOT, F), jnp.float32) ** levels(streams_of[4], (NSHOT, F), ((0, 64), (1, 4)), -0.2, 0.2), 1.0, 2.2),
        "receiver_terms": jnp.clip(1.0 + 1.2 * jax.random.uniform(streams_of[5], (NREC, F), jnp.float32) ** levels(streams_of[5], (NREC, F), ((0, 64), (1, 4)), -0.2, 0.2), 1.0, 2.2),
    }


def make_table(samples, first, count):
    times = jnp.arange(samples, dtype=jnp.int32)[:, None]
    freqs = first + jnp.arange(count, dtype=jnp.int32)[None, :]
    phase = (times * freqs) % samples
    angle = phase.astype(jnp.float32) * (2.0 * math.pi / samples)
    return jnp.concatenate([jnp.cos(angle), -jnp.sin(angle)], axis=1).astype(jnp.bfloat16)


def reference(traces, shot_index, receiver_index, live_counts, shot_terms, receiver_terms):
    table = make_table(NT, 0, F).astype(jnp.float32)
    blocks = traces.reshape(N_TR, TR_DEV, NT)
    shot_blocks = shot_index.reshape(N_TR, TR_DEV)
    rec_blocks = receiver_index.reshape(N_TR, TR_DEV)

    def step(carry, inputs):
        shot_acc, rec_acc = carry
        block, shots, recs, count = inputs
        spectrum = jnp.dot(block.astype(jnp.float32), table, precision=lax.Precision.HIGHEST)
        real_part = spectrum[:, :F]
        imag_part = spectrum[:, F:]
        logamp = 0.5 * jnp.log(real_part * real_part + imag_part * imag_part + 1.0)
        live = (jnp.arange(TR_DEV, dtype=jnp.int32) < count).astype(jnp.float32)[:, None]
        model = jnp.take(shot_terms, shots, axis=0) + jnp.take(receiver_terms, recs, axis=0)
        resid = live * (logamp - model)
        shot_acc = shot_acc + jax.ops.segment_sum(resid, shots, num_segments=NSHOT)
        rec_acc = rec_acc + jax.ops.segment_sum(resid, recs, num_segments=NREC)
        return (shot_acc, rec_acc), None

    start = (jnp.zeros((NSHOT, F), jnp.float32), jnp.zeros((NREC, F), jnp.float32))
    (shot_sums, receiver_sums), unused = lax.scan(step, start, (blocks, shot_blocks, rec_blocks, live_counts))
    return shot_sums, receiver_sums
```

```python
import math

import jax
import jax.numpy as jnp
from jax import lax
from jax.experimental import pallas as pl
from jax.experimental.pallas import tpu as pltpu
from jax.sharding import PartitionSpec as P

NZ, NX, NC, NY = 8, 4, 2, 4
LA_TOP = 9.1
LA_SCALE = 65535.0 / LA_TOP
REC_LOW, REC_HIGH = 1.0, 2.2
REC_SCALE = 65535.0 / (REC_HIGH - REC_LOW)
SUM_SCALE = 1.0 / 32.0
CHUNKS = 2
VMEM = pltpu.CompilerParams(vmem_limit_bytes=56 * 2**20)


def tr_of(z, x, c):
    return (z * NX + x) * NC + c


def sites():
    return [(z, x, c) for z in range(NZ) for x in range(NX) for c in range(NC)]


def send_x(value, k):
    return lax.ppermute(value, "tr", [(tr_of(z, x, c), tr_of(z, (x + k) % NX, c)) for z, x, c in sites()])


def send_z(value, k):
    return lax.ppermute(value, "tr", [(tr_of(z, x, c), tr_of((z + k) % NZ, x, c)) for z, x, c in sites()])


def swap_z(value):
    return lax.ppermute(value, "tr", [(tr_of(z, x, c), tr_of(z ^ 1, x, c)) for z, x, c in sites()])


def swap_core(value):
    return lax.ppermute(value, "tr", [(tr_of(z, x, c), tr_of(z, x, c ^ 1)) for z, x, c in sites()])


def send_y(value, k):
    return lax.ppermute(value, "fq", [(i, (i + k) % NY) for i in range(NY)])


def make_table(samples, y, width):
    part = samples // NY
    steps = jnp.arange(NY, dtype=jnp.int32)
    times = (((y - steps) % NY) * part)[:, None] + jnp.arange(part, dtype=jnp.int32)[None, :]
    times = times.reshape(samples, 1)
    freqs = (((y + steps) % NY) * width)[:, None] + jnp.arange(width, dtype=jnp.int32)[None, :]
    freqs = jnp.stack([freqs, freqs], axis=1).reshape(1, NY * 2 * width)
    imag = (jnp.arange(NY * 2 * width, dtype=jnp.int32) // width % 2 == 1)[None, :]
    phase = times * freqs % samples
    angle = phase.astype(jnp.float32) * (2.0 * math.pi / samples)
    return jnp.where(imag, -jnp.sin(angle), jnp.cos(angle)).astype(jnp.bfloat16)


def spectra(blocks, table, width):
    rows, part = blocks[0].shape
    tile = 512

    def body(b0, b1, b2, b3, t, o0, o1, o2, o3):
        for k, out in enumerate((o0, o1, o2, o3)):
            cols = pl.ds(k * 2 * width, 2 * width)
            acc = None
            for j, b in enumerate((b0, b1, b2, b3)):
                one = jnp.dot(b[...], t[pl.ds(j * part, part), cols], preferred_element_type=jnp.float32)
                acc = one if acc is None else acc + one
            re, im = acc[:, :width], acc[:, width:]
            logamp = 0.5 * jnp.log(re * re + im * im + 1.0)
            code = jnp.minimum(logamp * LA_SCALE + 0.5, 65535.0).astype(jnp.int32) - 32768
            out[...] = code.astype(jnp.int16)

    return pl.pallas_call(
        body,
        grid=(rows // tile,),
        in_specs=[pl.BlockSpec((tile, part), lambda i: (i, 0))] * 4
        + [pl.BlockSpec(table.shape, lambda i: (0, 0))],
        out_specs=[pl.BlockSpec((tile, width), lambda i: (i, 0))] * 4,
        out_shape=[jax.ShapeDtypeStruct((rows, width), jnp.int16)] * 4,
        compiler_params=VMEM,
        cost_estimate=pl.CostEstimate(flops=2 * rows * 1024 * 1024, bytes_accessed=rows * 3072 + 2**21, transcendentals=rows * 512),
        name="spectra",
    )(*blocks, table)


def gather_terms(own, other, shot_near, rec_at, shot_at):
    rows, width = rec_at.shape[0], own.shape[1]
    half = own.shape[0]

    def body(rec_at, shot_at, own, other, shot, out, rec):
        rec[pl.ds(0, half), :] = (own[...].astype(jnp.float32) + 32768.0) * (1.0 / REC_SCALE) + REC_LOW
        rec[pl.ds(half, half), :] = (other[...].astype(jnp.float32) + 32768.0) * (1.0 / REC_SCALE) + REC_LOW

        def step(b, _):
            for u in range(16):
                i = b * 16 + u
                out[pl.ds(i, 1), :] = rec[pl.ds(rec_at[i], 1), :] + shot[pl.ds(shot_at[i], 1), :]
            return 0

        lax.fori_loop(0, rows // 16, step, 0)

    vm, sm = pl.BlockSpec(memory_space=pltpu.VMEM), pl.BlockSpec(memory_space=pltpu.SMEM)
    return pl.pallas_call(
        body,
        in_specs=[sm, sm, vm, vm, vm],
        out_specs=vm,
        out_shape=jax.ShapeDtypeStruct((rows, width), jnp.float32),
        scratch_shapes=[pltpu.VMEM((2 * half, width), jnp.float32)],
        compiler_params=VMEM,
        cost_estimate=pl.CostEstimate(flops=rows * width, bytes_accessed=48 * 2**20, transcendentals=0),
        name="gather_terms",
    )(rec_at, shot_at, own, other, shot_near)


def residual(code, model, live):
    logamp = (code.astype(jnp.float32) + 32768.0) * (1.0 / LA_SCALE)
    alive = lax.broadcasted_iota(jnp.int32, code.shape, 0) < live
    return jnp.where(alive, logamp - model, 0.0)


def sum_receivers(codes, model, live, rec_at, count):
    rows, width = model.shape
    piece = codes[0].shape[0]
    parts = len(codes)
    banks, depth = 4, 2

    def body(*refs):
        rec_at, live, model = refs[:3]
        codes = refs[3 : 3 + parts]
        out, res = refs[3 + parts : 5 + parts]
        sums = (out,) + refs[5 + parts :]
        for s in sums:
            s[...] = jnp.zeros_like(s)
        for k, code in enumerate(codes):
            at = pl.ds(k * piece, piece)
            res[at, :] = residual(code[...], model[at, :], live[k])

        def step(b, _):
            group = banks * depth
            at = [rec_at[b * group + u] for u in range(group)]
            row = [res[pl.ds(b * group + u, 1), :] for u in range(group)]
            for u in range(banks):
                v = u + banks
                s = sums[u]
                first = s[pl.ds(at[u], 1), :]
                second = s[pl.ds(at[v], 1), :]
                again = (at[u] == at[v]).astype(jnp.float32)
                s[pl.ds(at[u], 1), :] = first + row[u]
                s[pl.ds(at[v], 1), :] = second + (row[v] + again * row[u])
            return 0

        lax.fori_loop(0, rows // (banks * depth), step, 0)
        out[...] = (sums[0][...] + sums[1][...]) + (sums[2][...] + sums[3][...])

    vm, sm = pl.BlockSpec(memory_space=pltpu.VMEM), pl.BlockSpec(memory_space=pltpu.SMEM)
    return pl.pallas_call(
        body,
        in_specs=[sm, sm] + [vm] * (1 + parts),
        out_specs=vm,
        out_shape=jax.ShapeDtypeStruct((count, width), jnp.float32),
        scratch_shapes=[pltpu.VMEM((rows, width), jnp.float32)] + [pltpu.VMEM((count, width), jnp.float32)] * (banks - 1),
        compiler_params=VMEM,
        cost_estimate=pl.CostEstimate(flops=rows * width, bytes_accessed=48 * 2**20, transcendentals=0),
        name="sum_receivers",
    )(rec_at, live, model, *codes)


def sum_shots(codes, model, live, shot_at, count):
    rows, width = model.shape
    piece = codes[0].shape[0]
    parts = len(codes)

    def body(*refs):
        shot_at, live, model = refs[:3]
        codes, out = refs[3 : 3 + parts], refs[3 + parts]
        acc = jnp.zeros((count, 2 * width), jnp.float32)
        for k, code in enumerate(codes):
            at = pl.ds(k * piece, piece)
            res = residual(code[...], model[at, :], live[k])
            high = res.astype(jnp.bfloat16)
            low = (res - high.astype(jnp.float32)).astype(jnp.bfloat16)
            both = jnp.concatenate([high, low], axis=1)
            hot = lax.broadcasted_iota(jnp.int32, (count, piece), 0) == shot_at[:, at]
            acc = acc + jnp.dot(hot.astype(jnp.bfloat16), both, preferred_element_type=jnp.float32)
        out[...] = acc[:, :width] + acc[:, width:]

    vm, sm = pl.BlockSpec(memory_space=pltpu.VMEM), pl.BlockSpec(memory_space=pltpu.SMEM)
    return pl.pallas_call(
        body,
        in_specs=[vm, sm] + [vm] * (1 + parts),
        out_specs=vm,
        out_shape=jax.ShapeDtypeStruct((count, width), jnp.float32),
        compiler_params=VMEM,
        cost_estimate=pl.CostEstimate(flops=4 * rows * width * count, bytes_accessed=12 * 2**20, transcendentals=0),
        name="sum_shots",
    )(shot_at[None, :], live, model, *codes)


def neighbour(value, by):
    size = NZ * NX * NC
    return lax.ppermute(value, "tr", [(i, i + by) for i in range(size) if 0 <= i + by < size])


def per_device(traces, shot_index, receiver_index, live_counts, shot_terms, receiver_terms):
    rows, part = traces.shape
    block, width = shot_terms.shape
    share, piece = rows // NY, rows // NY // CHUNKS
    owner, y = lax.axis_index("tr"), lax.axis_index("fq")
    z, x, c = owner // (NX * NC), owner // NC % NX, owner % NC

    parts = [lax.dynamic_slice_in_dim(traces, (y + k) % NY * share, share, 0) for k in range(NY)]
    got = [[None] * NY for _ in range(CHUNKS)]
    for h in range(CHUNKS):
        for k in (0, 1, 3, 2):
            mine = parts[k][h * piece : (h + 1) * piece]
            got[h][k] = send_y(mine, k) if k else mine

    code = jnp.clip(jnp.round((receiver_terms - REC_LOW) * REC_SCALE), 0.0, 65535.0).astype(jnp.int32) - 32768
    terms = code.astype(jnp.int16)
    terms = jnp.concatenate([terms] + [send_z(terms, -2 * k) for k in range(1, NZ // 2)])
    terms = jnp.concatenate([terms, swap_z(terms)])
    terms = jnp.concatenate([terms] + [send_x(terms, -k) for k in range(1, NX)])
    far_terms = swap_core(terms)

    def ordered(v):
        v = v.reshape(NY, CHUNKS, piece)
        v = jnp.stack([lax.dynamic_index_in_dim(v, (y - k) % NY, 0, keepdims=False) for k in range(NY)], axis=1)
        return v.reshape(rows)

    near = receiver_index // block
    rz, rx, rc = near // (NX * NC), near // NC % NX, near % NC
    odd = (rz ^ z) & 1
    place = (((rc ^ c) * NX + (rx - x) % NX) * 2 + odd) * (NZ // 2) + (rz - (z ^ odd)) % NZ // 2
    rec_at = ordered(place * block + receiver_index % block)
    shot_at = ordered(shot_index - (owner - 1) * block)
    live = live_counts[0] - jnp.stack([(y - k) % NY * share + h * piece for h in range(CHUNKS) for k in range(NY)])

    shot_near = jnp.concatenate([neighbour(shot_terms, 1), shot_terms, neighbour(shot_terms, -1)])

    table = make_table(part * NY, y, width)
    codes = []
    for h in range(CHUNKS):
        outs = spectra(got[h], table, width)
        codes += [send_y(outs[k], k) if k else outs[k] for k in range(NY)]
    model = gather_terms(terms, far_terms, shot_near, rec_at, shot_at)

    sums = sum_receivers(codes, model, live, rec_at, block * NZ * NX * NC)
    half = sums.shape[0] // 2
    sums = sums[:half] + swap_core(sums[half:])
    sums = sums.reshape(NX, NZ * block, width)
    sent = (sums * SUM_SCALE).astype(jnp.float16)
    come = [send_x(sent[k], k).astype(jnp.float32) for k in (1, 3, 2)]
    sums = sums[0] + (come[0] + come[1] + come[2]) * (1.0 / SUM_SCALE)
    half = sums.shape[0] // 2
    sent = (sums[half:] * SUM_SCALE).astype(jnp.float16)
    sums = sums[:half] + swap_z(sent).astype(jnp.float32) * (1.0 / SUM_SCALE)
    sums = sums.reshape(NZ // 2, block, width)
    sent = (sums * SUM_SCALE).astype(jnp.float16)
    come = [send_z(sent[k], 2 * k).astype(jnp.float32) for k in (1, 3, 2)]
    receiver_sums = sums[0] + (come[0] + come[1] + come[2]) * (1.0 / SUM_SCALE)

    shots = sum_shots(codes, model, live, shot_at, 3 * block)
    shot_sums = shots[block : 2 * block] + neighbour(shots[2 * block :], 1) + neighbour(shots[:block], -1)
    return (shot_sums, receiver_sums)


def solution(mesh):
    return jax.shard_map(
        per_device,
        mesh=mesh,
        in_specs=(P("tr", "fq"), P("tr"), P("tr"), P("tr"), P("tr", "fq"), P("tr", "fq")),
        out_specs=(P("tr", "fq"), P("tr", "fq")),
        check_vma=False,
    )
```

```python
import math

import jax
import jax.numpy as jnp
from jax import lax
from jax.experimental import pallas as pl
from jax.experimental.pallas import tpu as pltpu
from jax.sharding import PartitionSpec as P

NZ, NX, NC, NY = 8, 4, 2, 4
LA_TOP = 9.1
LA_SCALE = 65535.0 / LA_TOP
REC_LOW, REC_HIGH = 1.0, 2.2
REC_SCALE = 65535.0 / (REC_HIGH - REC_LOW)
SUM_SCALE = 1.0 / 32.0
CHUNKS = 2
SMALL = pltpu.CompilerParams(vmem_limit_bytes=12 * 2**20)
COST = pl.CostEstimate(flops=1000, bytes_accessed=1000, transcendentals=0)
VMEM = pltpu.CompilerParams(vmem_limit_bytes=56 * 2**20)


def tr_of(z, x, c):
    return (z * NX + x) * NC + c


def sites():
    return [(z, x, c) for z in range(NZ) for x in range(NX) for c in range(NC)]


def send_x(value, k):
    return lax.ppermute(value, "tr", [(tr_of(z, x, c), tr_of(z, (x + k) % NX, c)) for z, x, c in sites()])


def send_z(value, k):
    return lax.ppermute(value, "tr", [(tr_of(z, x, c), tr_of((z + k) % NZ, x, c)) for z, x, c in sites()])


def swap_z(value):
    return lax.ppermute(value, "tr", [(tr_of(z, x, c), tr_of(z ^ 1, x, c)) for z, x, c in sites()])


def swap_core(value):
    return lax.ppermute(value, "tr", [(tr_of(z, x, c), tr_of(z, x, c ^ 1)) for z, x, c in sites()])


def send_y(value, k):
    return lax.ppermute(value, "fq", [(i, (i + k) % NY) for i in range(NY)])


def make_table(samples, y, width):
    part, cols = samples // NY, NY * 2 * width
    tile = 128
    quarter = samples // 4

    def body(y_ref, out):
        y = y_ref[0]
        row = pl.program_id(0) * tile
        time = (y - row // part) % NY * part + row % part + lax.broadcasted_iota(jnp.int32, (tile, 1), 0)
        for k in range(NY):
            first = (y + k) % NY * width
            for half in range(2):
                freq = first + lax.broadcasted_iota(jnp.int32, (1, width), 1)
                phase = (time * freq + half * quarter) % samples
                turn = (phase + quarter // 2) // quarter
                rest = (phase - turn * quarter).astype(jnp.float32) * (2.0 * math.pi / samples)
                sq = rest * rest
                cos = 1.0 + sq * (-0.5 + sq * (1 / 24 + sq * (-1 / 720 + sq * (1 / 40320 - sq * (1 / 3628800)))))
                sin = rest * (1.0 + sq * (-1 / 6 + sq * (1 / 120 + sq * (-1 / 5040 + sq * (1 / 362880)))))
                value = jnp.where(turn % 2 == 1, sin, cos)
                value = jnp.where((turn % 4 == 1) | (turn % 4 == 2), -value, value)
                out[:, pl.ds((2 * k + half) * width, width)] = value.astype(jnp.bfloat16)

    return pl.pallas_call(
        body,
        grid=(samples // tile,),
        in_specs=[pl.BlockSpec(memory_space=pltpu.SMEM)],
        out_specs=pl.BlockSpec((tile, cols), lambda i: (i, 0)),
        out_shape=jax.ShapeDtypeStruct((samples, cols), jnp.bfloat16),
        compiler_params=SMALL,
        cost_estimate=COST,
        name="make_table",
    )(y[None])


def join(parts, after=()):
    size = parts[0].shape[0]

    def body(*refs):
        out = refs[-1]
        for k in range(len(parts)):
            out[pl.ds(k * size, size), :] = refs[k][...]

    vm = pl.BlockSpec(memory_space=pltpu.VMEM)
    return pl.pallas_call(
        body,
        in_specs=[vm] * len(parts) + [pl.BlockSpec(memory_space=pl.ANY)] * len(after),
        out_specs=vm,
        out_shape=jax.ShapeDtypeStruct((size * len(parts),) + parts[0].shape[1:], parts[0].dtype),
        compiler_params=SMALL,
        cost_estimate=COST,
        name="join",
    )(*parts, *after)


def take_rows(traces, y, chunk, after=()):
    rows, part = traces.shape
    piece = rows // NY // CHUNKS
    tile = min(piece, 256)
    steps = piece // tile

    def body(y_ref, *refs):
        for a, b in zip(refs[:3], refs[3 + len(after) :]):
            b[...] = a[...]

    def spot(k):
        return pl.BlockSpec((tile, part), lambda i, y: (((y[0] + k) % NY * CHUNKS + chunk) * steps + i, 0))

    return pl.pallas_call(
        body,
        grid_spec=pltpu.PrefetchScalarGridSpec(
            num_scalar_prefetch=1,
            grid=(steps,),
            in_specs=[spot(k) for k in range(1, NY)] + [pl.BlockSpec(memory_space=pl.ANY)] * len(after),
            out_specs=[pl.BlockSpec((tile, part), lambda i, y: (i, 0))] * 3,
        ),
        out_shape=[jax.ShapeDtypeStruct((piece, part), traces.dtype)] * 3,
        compiler_params=SMALL,
        cost_estimate=COST,
        name="take_rows",
    )(y[None], traces, traces, traces, *after)


def encode_terms(terms, after):
    def body(a, *refs):
        b = refs[-1]
        code = jnp.clip((a[...] - REC_LOW) * REC_SCALE + 0.5, 0.0, 65535.0).astype(jnp.int32) - 32768
        b[...] = code.astype(jnp.int16)

    vm = pl.BlockSpec(memory_space=pltpu.VMEM)
    return pl.pallas_call(
        body,
        in_specs=[vm] + [pl.BlockSpec(memory_space=pl.ANY)] * len(after),
        out_specs=vm,
        out_shape=jax.ShapeDtypeStruct(terms.shape, jnp.int16),
        compiler_params=SMALL,
        cost_estimate=COST,
        name="encode_terms",
    )(terms, *after)


def spectra(traces, y, chunk, blocks, table, width):
    rows, part = blocks[0].shape
    tile = min(rows, 512)
    steps = rows // tile

    def body(y_ref, b0, b1, b2, b3, t, o0, o1, o2, o3):
        for k, out in enumerate((o0, o1, o2, o3)):
            cols = pl.ds(k * 2 * width, 2 * width)
            acc = None
            for j, b in enumerate((b0, b1, b2, b3)):
                one = jnp.dot(b[...], t[pl.ds(j * part, part), cols], preferred_element_type=jnp.float32)
                acc = one if acc is None else acc + one
            re, im = acc[:, :width], acc[:, width:]
            logamp = 0.5 * jnp.log(re * re + im * im + 1.0)
            code = jnp.minimum(logamp * LA_SCALE + 0.5, 65535.0).astype(jnp.int32) - 32768
            out[...] = code.astype(jnp.int16)

    return pl.pallas_call(
        body,
        grid_spec=pltpu.PrefetchScalarGridSpec(
            num_scalar_prefetch=1,
            grid=(steps,),
            in_specs=[pl.BlockSpec((tile, part), lambda i, y: ((y[0] * CHUNKS + chunk) * steps + i, 0))]
            + [pl.BlockSpec((tile, part), lambda i, y: (i, 0))] * 3
            + [pl.BlockSpec(table.shape, lambda i, y: (0, 0))],
            out_specs=[pl.BlockSpec((tile, width), lambda i, y: (i, 0))] * 4,
        ),
        out_shape=[jax.ShapeDtypeStruct((rows, width), jnp.int16)] * 4,
        compiler_params=VMEM,
        cost_estimate=COST,
        name="spectra",
    )(y[None], traces, *blocks, table)


def gather_terms(own, other, shot_near, rec_at, shot_at):
    rows, width = rec_at.shape[0], own.shape[1]
    half = own.shape[0]

    def body(rec_at, shot_at, own, other, shot, out, rec):
        rec[pl.ds(0, half), :] = (own[...].astype(jnp.float32) + 32768.0) * (1.0 / REC_SCALE) + REC_LOW
        rec[pl.ds(half, half), :] = (other[...].astype(jnp.float32) + 32768.0) * (1.0 / REC_SCALE) + REC_LOW

        def step(b, _):
            at = [b * 32 + u for u in range(32)]
            row = [rec[pl.ds(rec_at[i], 1), :] + shot[pl.ds(shot_at[i], 1), :] for i in at]
            for i, value in zip(at, row):
                out[pl.ds(i, 1), :] = value
            return 0

        lax.fori_loop(0, rows // 32, step, 0)

    vm, sm = pl.BlockSpec(memory_space=pltpu.VMEM), pl.BlockSpec(memory_space=pltpu.SMEM)
    return pl.pallas_call(
        body,
        in_specs=[sm, sm, vm, vm, vm],
        out_specs=vm,
        out_shape=jax.ShapeDtypeStruct((rows, width), jnp.float32),
        scratch_shapes=[pltpu.VMEM((2 * half, width), jnp.float32)],
        compiler_params=VMEM,
        cost_estimate=COST,
        name="gather_terms",
    )(rec_at, shot_at, own, other, shot_near)


def residual(code, model, live):
    logamp = (code.astype(jnp.float32) + 32768.0) * (1.0 / LA_SCALE)
    alive = lax.broadcasted_iota(jnp.int32, code.shape, 0) < live
    return jnp.where(alive, logamp - model, 0.0)


def sum_receivers(codes, model, live, rec_at, count):
    rows, width = model.shape
    piece = codes[0].shape[0]
    parts = len(codes)
    banks, group = 8, 32

    def body(*refs):
        rec_at, live, model = refs[:3]
        codes = refs[3 : 3 + parts]
        out, res = refs[3 + parts : 5 + parts]
        sums = (out,) + refs[5 + parts :]
        for s in sums:
            s[...] = jnp.zeros_like(s)
        for k, code in enumerate(codes):
            at = pl.ds(k * piece, piece)
            res[at, :] = residual(code[...], model[at, :], live[k])

        def step(b, _):
            for u in range(group):
                s, at = sums[u % banks], pl.ds(rec_at[b * group + u], 1)
                s[at, :] = s[at, :] + res[pl.ds(b * group + u, 1), :]
            return 0

        lax.fori_loop(0, rows // group, step, 0)
        out[...] = ((sums[0][...] + sums[1][...]) + (sums[2][...] + sums[3][...])) + (
            (sums[4][...] + sums[5][...]) + (sums[6][...] + sums[7][...])
        )

    vm, sm = pl.BlockSpec(memory_space=pltpu.VMEM), pl.BlockSpec(memory_space=pltpu.SMEM)
    return pl.pallas_call(
        body,
        in_specs=[sm, sm] + [vm] * (1 + parts),
        out_specs=vm,
        out_shape=jax.ShapeDtypeStruct((count, width), jnp.float32),
        scratch_shapes=[pltpu.VMEM((rows, width), jnp.float32)] + [pltpu.VMEM((count, width), jnp.float32)] * (banks - 1),
        compiler_params=VMEM,
        cost_estimate=COST,
        name="sum_receivers",
    )(rec_at, live, model, *codes)


def sum_shots(codes, model, live, shot_at, count):
    rows, width = model.shape
    piece = codes[0].shape[0]
    parts = len(codes)

    def body(*refs):
        shot_at, live, model = refs[:3]
        codes, out = refs[3 : 3 + parts], refs[3 + parts]
        acc = jnp.zeros((count, 2 * width), jnp.float32)
        for k, code in enumerate(codes):
            at = pl.ds(k * piece, piece)
            res = residual(code[...], model[at, :], live[k])
            high = res.astype(jnp.bfloat16)
            low = (res - high.astype(jnp.float32)).astype(jnp.bfloat16)
            both = jnp.concatenate([high, low], axis=1)
            hot = lax.broadcasted_iota(jnp.int32, (count, piece), 0) == shot_at[:, at]
            acc = acc + jnp.dot(hot.astype(jnp.bfloat16), both, preferred_element_type=jnp.float32)
        out[...] = acc[:, :width] + acc[:, width:]

    vm, sm = pl.BlockSpec(memory_space=pltpu.VMEM), pl.BlockSpec(memory_space=pltpu.SMEM)
    return pl.pallas_call(
        body,
        in_specs=[vm, sm] + [vm] * (1 + parts),
        out_specs=vm,
        out_shape=jax.ShapeDtypeStruct((count, width), jnp.float32),
        compiler_params=VMEM,
        cost_estimate=COST,
        name="sum_shots",
    )(shot_at[None, :], live, model, *codes)


def neighbour(value, by):
    size = NZ * NX * NC
    return lax.ppermute(value, "tr", [(i, i + by) for i in range(size) if 0 <= i + by < size])


def per_device(traces, shot_index, receiver_index, live_counts, shot_terms, receiver_terms):
    rows, part = traces.shape
    block, width = shot_terms.shape
    share, piece = rows // NY, rows // NY // CHUNKS
    owner, y = lax.axis_index("tr"), lax.axis_index("fq")
    z, x, c = owner // (NX * NC), owner // NC % NX, owner % NC

    got, after = [], ()
    for h in range(CHUNKS):
        mine = take_rows(traces, y, h, after)
        come = {k: send_y(mine[k - 1], k) for k in (1, 3, 2)}
        got.append([come[k] for k in range(1, NY)])
        after = (come[1], come[3])
    table = make_table(part * NY, y, width)
    coded = [spectra(traces, y, h, got[h], table, width) for h in range(CHUNKS)]
    codes = [send_y(outs[k], k) if k else outs[k] for outs in coded for k in range(NY)]

    terms = encode_terms(receiver_terms, (got[0][0], got[0][2], table))
    terms = join([terms] + [send_z(terms, -2 * k) for k in range(1, NZ // 2)], (got[0][1],))
    terms = join([terms, swap_z(terms)], (got[1][0], got[1][2], coded[0][0]))
    terms = join([terms] + [send_x(terms, -k) for k in range(1, NX)], (codes[1], codes[3], coded[1][0]))
    far_terms = swap_core(terms)

    def ordered(v):
        v = v.reshape(NY, CHUNKS, piece)
        v = jnp.stack([lax.dynamic_index_in_dim(v, (y - k) % NY, 0, keepdims=False) for k in range(NY)], axis=1)
        return v.reshape(rows)

    near = receiver_index // block
    rz, rx, rc = near // (NX * NC), near // NC % NX, near % NC
    odd = (rz ^ z) & 1
    place = (((rc ^ c) * NX + (rx - x) % NX) * 2 + odd) * (NZ // 2) + (rz - (z ^ odd)) % NZ // 2
    rec_at = ordered(place * block + receiver_index % block)
    shot_at = ordered(shot_index - (owner - 1) * block)
    live = live_counts[0] - jnp.stack([(y - k) % NY * share + h * piece for h in range(CHUNKS) for k in range(NY)])

    shot_near = jnp.concatenate([neighbour(shot_terms, 1), shot_terms, neighbour(shot_terms, -1)])

    model = gather_terms(terms, far_terms, shot_near, rec_at, shot_at)

    sums = sum_receivers(codes, model, live, rec_at, block * NZ * NX * NC)
    half = sums.shape[0] // 2
    sums = sums[:half] + swap_core(sums[half:])
    sums = sums.reshape(NX, NZ * block, width)
    sent = (sums * SUM_SCALE).astype(jnp.float16)
    come = [send_x(sent[k], k).astype(jnp.float32) for k in (1, 3, 2)]
    sums = sums[0] + (come[0] + come[1] + come[2]) * (1.0 / SUM_SCALE)
    half = sums.shape[0] // 2
    sent = (sums[half:] * SUM_SCALE).astype(jnp.float16)
    sums = sums[:half] + swap_z(sent).astype(jnp.float32) * (1.0 / SUM_SCALE)
    sums = sums.reshape(NZ // 2, block, width)
    sent = (sums * SUM_SCALE).astype(jnp.float16)
    come = [send_z(sent[k], 2 * k).astype(jnp.float32) for k in (1, 3, 2)]
    receiver_sums = sums[0] + (come[0] + come[1] + come[2]) * (1.0 / SUM_SCALE)

    shots = sum_shots(codes, model, live, shot_at, 3 * block)
    shot_sums = shots[block : 2 * block] + neighbour(shots[2 * block :], 1) + neighbour(shots[:block], -1)
    return (shot_sums, receiver_sums)


def solution(mesh):
    return jax.shard_map(
        per_device,
        mesh=mesh,
        in_specs=(P("tr", "fq"), P("tr"), P("tr"), P("tr"), P("tr", "fq"), P("tr", "fq")),
        out_specs=(P("tr", "fq"), P("tr", "fq")),
        check_vma=False,
    )
```

```python
import math

import jax
import jax.numpy as jnp
from jax import lax
from jax.experimental import pallas as pl
from jax.experimental.pallas import tpu as pltpu
from jax.sharding import PartitionSpec as P

NZ, NX, NC, NY = 8, 4, 2, 4
LA_TOP = 9.1
LA_SCALE = 65535.0 / LA_TOP
REC_LOW, REC_HIGH = 1.0, 2.2
REC_SCALE = 65535.0 / (REC_HIGH - REC_LOW)
SUM_SCALE = 1.0 / 32.0
SENT = (1024, 1024)
BACK = ((0, 0, 1024), (1, 0, 1024))
SMALL = pltpu.CompilerParams(vmem_limit_bytes=12 * 2**20)
COST = pl.CostEstimate(flops=1000, bytes_accessed=1000, transcendentals=0)
VMEM = pltpu.CompilerParams(vmem_limit_bytes=56 * 2**20)


def tr_of(z, x, c):
    return (z * NX + x) * NC + c


def sites():
    return [(z, x, c) for z in range(NZ) for x in range(NX) for c in range(NC)]


def swap(value, dz, dx, dc):
    return lax.ppermute(value, "tr", [(tr_of(z, x, c), tr_of(z ^ dz, x ^ dx, c ^ dc)) for z, x, c in sites()])


def send_y(value, k):
    return lax.ppermute(value, "fq", [(i, (i + k) % NY) for i in range(NY)])


def make_table(samples, y, width):
    part, cols = samples // NY, NY * 2 * width
    tile = 128
    quarter = samples // 4
    shift = quarter.bit_length() - 1

    def body(y_ref, out):
        y = y_ref[0]
        row = pl.program_id(0) * tile
        time = (y - row // part) % NY * part + row % part + lax.broadcasted_iota(jnp.int32, (tile, 1), 0)
        for k in range(NY):
            first = (y + k) % NY * width
            for half in range(2):
                freq = first + lax.broadcasted_iota(jnp.int32, (1, width), 1)
                phase = (time * freq + half * quarter) & (samples - 1)
                turn = lax.shift_right_logical(phase + quarter // 2, shift)
                rest = (phase - turn * quarter).astype(jnp.float32) * (2.0 * math.pi / samples)
                sq = rest * rest
                cos = 1.0 + sq * (-0.5 + sq * (1 / 24 + sq * (-1 / 720 + sq * (1 / 40320 - sq * (1 / 3628800)))))
                sin = rest * (1.0 + sq * (-1 / 6 + sq * (1 / 120 + sq * (-1 / 5040 + sq * (1 / 362880)))))
                value = jnp.where((turn & 1) == 1, sin, cos)
                value = jnp.where(((turn + 1) & 2) == 2, -value, value)
                out[:, pl.ds((2 * k + half) * width, width)] = value.astype(jnp.bfloat16)

    return pl.pallas_call(
        body,
        grid=(samples // tile,),
        in_specs=[pl.BlockSpec(memory_space=pltpu.SMEM)],
        out_specs=pl.BlockSpec((tile, cols), lambda i: (i, 0)),
        out_shape=jax.ShapeDtypeStruct((samples, cols), jnp.bfloat16),
        compiler_params=SMALL,
        cost_estimate=pl.CostEstimate(flops=2**30, bytes_accessed=2**25, transcendentals=0),
        name="make_table",
    )(y[None])


def join(parts, after=()):
    size = parts[0].shape[0]

    def body(*refs):
        out = refs[-1]
        for k in range(len(parts)):
            out[pl.ds(k * size, size), :] = refs[k][...]

    vm = pl.BlockSpec(memory_space=pltpu.VMEM)
    return pl.pallas_call(
        body,
        in_specs=[vm] * len(parts) + [pl.BlockSpec(memory_space=pl.ANY)] * len(after),
        out_specs=vm,
        out_shape=jax.ShapeDtypeStruct((size * len(parts),) + parts[0].shape[1:], parts[0].dtype),
        compiler_params=SMALL,
        cost_estimate=COST,
        name="join",
    )(*parts, *after)


def take_rows(traces, y, first, piece, after=()):
    rows, part = traces.shape
    tile = 256
    share, start, steps = rows // NY // tile, first // tile, piece // tile

    def body(y_ref, *refs):
        for a, b in zip(refs[:3], refs[3 + len(after) :]):
            b[...] = a[...]

    def spot(k):
        return pl.BlockSpec((tile, part), lambda i, y: ((y[0] + k) % NY * share + start + i, 0))

    return pl.pallas_call(
        body,
        grid_spec=pltpu.PrefetchScalarGridSpec(
            num_scalar_prefetch=1,
            grid=(steps,),
            in_specs=[spot(k) for k in range(1, NY)] + [pl.BlockSpec(memory_space=pl.ANY)] * len(after),
            out_specs=[pl.BlockSpec((tile, part), lambda i, y: (i, 0))] * 3,
        ),
        out_shape=[jax.ShapeDtypeStruct((piece, part), traces.dtype)] * 3,
        compiler_params=SMALL,
        cost_estimate=COST,
        name="take_rows",
    )(y[None], traces, traces, traces, *after)


def encode_terms(terms, after):
    def body(a, *refs):
        b = refs[-1]
        code = jnp.clip((a[...] - REC_LOW) * REC_SCALE + 0.5, 0.0, 65535.0).astype(jnp.int32) - 32768
        b[...] = code.astype(jnp.int16)

    vm = pl.BlockSpec(memory_space=pltpu.VMEM)
    return pl.pallas_call(
        body,
        in_specs=[vm] + [pl.BlockSpec(memory_space=pl.ANY)] * len(after),
        out_specs=vm,
        out_shape=jax.ShapeDtypeStruct(terms.shape, jnp.int16),
        compiler_params=SMALL,
        cost_estimate=COST,
        name="encode_terms",
    )(terms, *after)


def spectra(traces, y, first, inner, rows, blocks, table, width, after=()):
    part, tile = traces.shape[1], 256
    share, start, steps = traces.shape[0] // NY // tile, first // tile, rows // tile

    def body(y_ref, b0, b1, b2, b3, t, *refs):
        for k, out in enumerate(refs[len(after) :]):
            cols = pl.ds(k * 2 * width, 2 * width)
            acc = None
            for j, b in enumerate((b0, b1, b2, b3)):
                one = jnp.dot(b[...], t[pl.ds(j * part, part), cols], preferred_element_type=jnp.float32)
                acc = one if acc is None else acc + one
            re, im = acc[:, :width], acc[:, width:]
            logamp = 0.5 * jnp.log(re * re + im * im + 1.0)
            code = jnp.minimum(logamp * LA_SCALE + 0.5, 65535.0).astype(jnp.int32) - 32768
            out[...] = code.astype(jnp.int16)

    return pl.pallas_call(
        body,
        grid_spec=pltpu.PrefetchScalarGridSpec(
            num_scalar_prefetch=1,
            grid=(steps,),
            in_specs=[pl.BlockSpec((tile, part), lambda i, y: (y[0] * share + start + i, 0))]
            + [pl.BlockSpec((tile, part), lambda i, y: (inner // tile + i, 0))] * 3
            + [pl.BlockSpec(table.shape, lambda i, y: (0, 0))]
            + [pl.BlockSpec(memory_space=pl.ANY)] * len(after),
            out_specs=[pl.BlockSpec((tile, width), lambda i, y: (i, 0))] * 4,
        ),
        out_shape=[jax.ShapeDtypeStruct((rows, width), jnp.int16)] * 4,
        compiler_params=VMEM,
        cost_estimate=COST,
        name="spectra",
    )(y[None], traces, *blocks, table, *after)


def gather_terms(coded, shot_near, rec_at, shot_at):
    rows, width = rec_at.shape[0], shot_near.shape[1]
    parts = len(coded)
    spans = spans_of(coded)

    def body(rec_at, shot_at, shot, *refs):
        out, rec = refs[parts:]
        for code, at in zip(refs, spans):
            rec[at, :] = (code[...].astype(jnp.float32) + 32768.0) * (1.0 / REC_SCALE) + REC_LOW

        def step(b, _):
            at = [b * 32 + u for u in range(32)]
            row = [rec[pl.ds(rec_at[i], 1), :] + shot[pl.ds(shot_at[i], 1), :] for i in at]
            for i, value in zip(at, row):
                out[pl.ds(i, 1), :] = value
            return 0

        lax.fori_loop(0, rows // 32, step, 0)

    vm, sm = pl.BlockSpec(memory_space=pltpu.VMEM), pl.BlockSpec(memory_space=pltpu.SMEM)
    return pl.pallas_call(
        body,
        in_specs=[sm, sm, vm] + [vm] * parts,
        out_specs=vm,
        out_shape=jax.ShapeDtypeStruct((rows, width), jnp.float32),
        scratch_shapes=[pltpu.VMEM((sum(code.shape[0] for code in coded), width), jnp.float32)],
        compiler_params=VMEM,
        cost_estimate=COST,
        name="gather_terms",
    )(rec_at, shot_at, shot_near, *coded)


def residual(code, model, live):
    logamp = (code.astype(jnp.float32) + 32768.0) * (1.0 / LA_SCALE)
    alive = lax.broadcasted_iota(jnp.int32, code.shape, 0) < live
    return jnp.where(alive, logamp - model, 0.0)


def spans_of(codes):
    sizes = [code.shape[0] for code in codes]
    return [pl.ds(sum(sizes[:k]), size) for k, size in enumerate(sizes)]


def sum_receivers(codes, model, live, rec_at, count):
    rows, width = model.shape
    parts = len(codes)
    spans = spans_of(codes)
    banks, group = 8, 32

    def body(*refs):
        rec_at, live, model = refs[:3]
        codes = refs[3 : 3 + parts]
        out, res = refs[3 + parts : 5 + parts]
        sums = (out,) + refs[5 + parts :]
        for s in sums:
            s[...] = jnp.zeros_like(s)
        for k, (code, at) in enumerate(zip(codes, spans)):
            res[at, :] = residual(code[...], model[at, :], live[k])

        def step(b, _):
            for u in range(group):
                s, at = sums[u % banks], pl.ds(rec_at[b * group + u], 1)
                s[at, :] = s[at, :] + res[pl.ds(b * group + u, 1), :]
            return 0

        lax.fori_loop(0, rows // group, step, 0)
        out[...] = ((sums[0][...] + sums[1][...]) + (sums[2][...] + sums[3][...])) + (
            (sums[4][...] + sums[5][...]) + (sums[6][...] + sums[7][...])
        )

    vm, sm = pl.BlockSpec(memory_space=pltpu.VMEM), pl.BlockSpec(memory_space=pltpu.SMEM)
    return pl.pallas_call(
        body,
        in_specs=[sm, sm] + [vm] * (1 + parts),
        out_specs=vm,
        out_shape=jax.ShapeDtypeStruct((count, width), jnp.float32),
        scratch_shapes=[pltpu.VMEM((rows, width), jnp.float32)] + [pltpu.VMEM((count, width), jnp.float32)] * (banks - 1),
        compiler_params=VMEM,
        cost_estimate=COST,
        name="sum_receivers",
    )(rec_at, live, model, *codes)


def sum_shots(codes, model, live, shot_at, count):
    rows, width = model.shape
    parts = len(codes)
    spans = spans_of(codes)

    def body(*refs):
        shot_at, live, model = refs[:3]
        codes, out = refs[3 : 3 + parts], refs[3 + parts]
        acc = jnp.zeros((count, 2 * width), jnp.float32)
        for k, (code, at) in enumerate(zip(codes, spans)):
            res = residual(code[...], model[at, :], live[k])
            high = res.astype(jnp.bfloat16)
            low = (res - high.astype(jnp.float32)).astype(jnp.bfloat16)
            both = jnp.concatenate([high, low], axis=1)
            hot = lax.broadcasted_iota(jnp.int32, (count, at.size), 0) == shot_at[:, at]
            acc = acc + jnp.dot(hot.astype(jnp.bfloat16), both, preferred_element_type=jnp.float32)
        out[...] = acc[:, :width] + acc[:, width:]

    vm, sm = pl.BlockSpec(memory_space=pltpu.VMEM), pl.BlockSpec(memory_space=pltpu.SMEM)
    return pl.pallas_call(
        body,
        in_specs=[vm, sm] + [vm] * (1 + parts),
        out_specs=vm,
        out_shape=jax.ShapeDtypeStruct((count, width), jnp.float32),
        compiler_params=VMEM,
        cost_estimate=COST,
        name="sum_shots",
    )(shot_at[None, :], live, model, *codes)


def neighbour(value, by):
    size = NZ * NX * NC
    return lax.ppermute(value, "tr", [(i, i + by) for i in range(size) if 0 <= i + by < size])


def per_device(traces, shot_index, receiver_index, live_counts, shot_terms, receiver_terms):
    rows, part = traces.shape
    block, width = shot_terms.shape
    share = rows // NY
    starts = [sum(SENT[:t]) for t in range(len(SENT))]
    first = [starts[t] + inner for t, inner, _ in BACK]
    owner, y = lax.axis_index("tr"), lax.axis_index("fq")
    z, x, c = owner // (NX * NC), owner // NC % NX, owner % NC

    got, after = [], ()
    for start, size in zip(starts, SENT):
        mine = take_rows(traces, y, start, size, after)
        come = {k: send_y(mine[k - 1], k) for k in (1, 3, 2)}
        got.append([come[k] for k in range(1, NY)])
        after = got[-1]
        if start == 0:
            mine_first = mine[0]
    table = make_table(part * NY, y, width)
    terms = encode_terms(receiver_terms, (mine_first,))
    terms = join([terms, swap(terms, 1, 0, 0)])
    terms = join([terms, swap(terms, 2, 0, 0)])
    terms = join([terms, swap(terms, 4, 0, 0)], (table,))
    terms = join([terms, swap(terms, 0, 1, 0)])
    terms = join([terms, swap(terms, 0, 2, 0)])
    far_terms = [swap(terms, 0, 0, 1)]

    def ordered(v):
        v = v.reshape(NY, share)
        v = jnp.stack([lax.dynamic_index_in_dim(v, (y - k) % NY, 0, keepdims=False) for k in range(NY)])
        return jnp.concatenate([v[:, at : at + size].reshape(NY * size) for at, (_, _, size) in zip(first, BACK)])

    near = receiver_index // block
    rz, rx, rc = near // (NX * NC), near // NC % NX, near % NC
    place = ((rc ^ c) * NX + (rx ^ x)) * NZ + (rz ^ z)
    rec_at = ordered(place * block + receiver_index % block)
    shot_at = ordered(shot_index - (owner - 1) * block)
    live = live_counts[0] - jnp.stack([(y - k) % NY * share + at for at in first for k in range(NY)])

    shot_terms = join([shot_terms], got[0])
    shot_near = jnp.concatenate([neighbour(shot_terms, 1), shot_terms, neighbour(shot_terms, -1)])

    model = gather_terms([terms] + far_terms, shot_near, rec_at, shot_at)

    codes = []
    for t, inner, size in BACK:
        after = (model,) if t else ()
        outs = spectra(traces, y, starts[t] + inner, inner, size, got[t], table, width, after)
        codes += [send_y(outs[k], k) if k else outs[k] for k in range(NY)]

    sums = sum_receivers(codes, model, live, rec_at, block * NZ * NX * NC)
    half = sums.shape[0] // 2
    sums = sums[:half] + swap(sums[half:], 0, 0, 1)
    sums = sums.reshape(NX, NZ * block, width)
    sent = (sums * SUM_SCALE).astype(jnp.float16)
    come = [swap(sent[k], 0, k, 0).astype(jnp.float32) for k in (1, 3, 2)]
    shots = sum_shots(codes, model, live, shot_at, 3 * block)
    shot_sums = shots[block : 2 * block] + neighbour(shots[2 * block :], 1) + neighbour(shots[:block], -1)
    sums = join([sums[0]], (shot_sums,)) + (come[0] + come[1] + come[2]) * (1.0 / SUM_SCALE)
    sums = sums.reshape(2, NZ // 2 * block, width)
    sent = (sums[1] * SUM_SCALE).astype(jnp.float16)
    sums = sums[0] + swap(sent, 4, 0, 0).astype(jnp.float32) * (1.0 / SUM_SCALE)
    sums = sums.reshape(NZ // 2, block, width)
    sent = (sums * SUM_SCALE).astype(jnp.float16)
    come = [swap(sent[k], k, 0, 0).astype(jnp.float32) for k in (1, 3, 2)]
    receiver_sums = sums[0] + (come[0] + come[1] + come[2]) * (1.0 / SUM_SCALE)
    return (shot_sums, receiver_sums)


def solution(mesh):
    return jax.shard_map(
        per_device,
        mesh=mesh,
        in_specs=(P("tr", "fq"), P("tr"), P("tr"), P("tr"), P("tr", "fq"), P("tr", "fq")),
        out_specs=(P("tr", "fq"), P("tr", "fq")),
        check_vma=False,
    )
```

```python
import math

import jax
import jax.numpy as jnp
from jax import lax
from jax.experimental import pallas as pl
from jax.experimental.pallas import tpu as pltpu
from jax.sharding import PartitionSpec as P

NZ, NX, NC, NY = 8, 4, 2, 4
LA_TOP = 9.1
LA_SCALE = 65535.0 / LA_TOP
REC_LOW, REC_HIGH = 1.0, 2.2
REC_SCALE = 65535.0 / (REC_HIGH - REC_LOW)
SUM_SCALE = 1.0 / 32.0
SENT = (2048,)
BACK = ((0, 0, 768), (0, 768, 1280))
SMALL = pltpu.CompilerParams(vmem_limit_bytes=12 * 2**20)
COST = pl.CostEstimate(flops=1000, bytes_accessed=1000, transcendentals=0)
VMEM = pltpu.CompilerParams(vmem_limit_bytes=56 * 2**20)


def tr_of(z, x, c):
    return (z * NX + x) * NC + c


def sites():
    return [(z, x, c) for z in range(NZ) for x in range(NX) for c in range(NC)]


def swap(value, dz, dx, dc):
    return lax.ppermute(value, "tr", [(tr_of(z, x, c), tr_of(z ^ dz, x ^ dx, c ^ dc)) for z, x, c in sites()])


def send_y(value, k):
    return lax.ppermute(value, "fq", [(i, (i + k) % NY) for i in range(NY)])


def make_table(samples, y, width):
    part, cols = samples // NY, NY * 2 * width
    tile = 128
    quarter = samples // 4
    shift = quarter.bit_length() - 1

    def body(y_ref, out):
        y = y_ref[0]
        row = pl.program_id(0) * tile
        time = (y - row // part) % NY * part + row % part + lax.broadcasted_iota(jnp.int32, (tile, 1), 0)
        for k in range(NY):
            first = (y + k) % NY * width
            for half in range(2):
                freq = first + lax.broadcasted_iota(jnp.int32, (1, width), 1)
                phase = (time * freq + half * quarter) & (samples - 1)
                turn = lax.shift_right_logical(phase + quarter // 2, shift)
                rest = (phase - turn * quarter).astype(jnp.float32) * (2.0 * math.pi / samples)
                sq = rest * rest
                cos = 1.0 + sq * (-0.5 + sq * (1 / 24 + sq * (-1 / 720 + sq * (1 / 40320 - sq * (1 / 3628800)))))
                sin = rest * (1.0 + sq * (-1 / 6 + sq * (1 / 120 + sq * (-1 / 5040 + sq * (1 / 362880)))))
                value = jnp.where((turn & 1) == 1, sin, cos)
                value = jnp.where(((turn + 1) & 2) == 2, -value, value)
                out[:, pl.ds((2 * k + half) * width, width)] = value.astype(jnp.bfloat16)

    return pl.pallas_call(
        body,
        grid=(samples // tile,),
        in_specs=[pl.BlockSpec(memory_space=pltpu.SMEM)],
        out_specs=pl.BlockSpec((tile, cols), lambda i: (i, 0)),
        out_shape=jax.ShapeDtypeStruct((samples, cols), jnp.bfloat16),
        compiler_params=SMALL,
        cost_estimate=pl.CostEstimate(flops=2**30, bytes_accessed=2**25, transcendentals=0),
        name="make_table",
    )(y[None])


def join(parts, after=()):
    size = parts[0].shape[0]

    def body(*refs):
        out = refs[-1]
        for k in range(len(parts)):
            out[pl.ds(k * size, size), :] = refs[k][...]

    vm = pl.BlockSpec(memory_space=pltpu.VMEM)
    return pl.pallas_call(
        body,
        in_specs=[vm] * len(parts) + [pl.BlockSpec(memory_space=pl.ANY)] * len(after),
        out_specs=vm,
        out_shape=jax.ShapeDtypeStruct((size * len(parts),) + parts[0].shape[1:], parts[0].dtype),
        compiler_params=SMALL,
        cost_estimate=COST,
        name="join",
    )(*parts, *after)


def take_rows(traces, y, first, piece, after=()):
    rows, part = traces.shape
    tile = 256
    share, start, steps = rows // NY // tile, first // tile, piece // tile

    def body(y_ref, *refs):
        for a, b in zip(refs[:3], refs[3 + len(after) :]):
            b[...] = a[...]

    def spot(k):
        return pl.BlockSpec((tile, part), lambda i, y: ((y[0] + k) % NY * share + start + i, 0))

    return pl.pallas_call(
        body,
        grid_spec=pltpu.PrefetchScalarGridSpec(
            num_scalar_prefetch=1,
            grid=(steps,),
            in_specs=[spot(k) for k in range(1, NY)] + [pl.BlockSpec(memory_space=pl.ANY)] * len(after),
            out_specs=[pl.BlockSpec((tile, part), lambda i, y: (i, 0))] * 3,
        ),
        out_shape=[jax.ShapeDtypeStruct((piece, part), traces.dtype)] * 3,
        compiler_params=SMALL,
        cost_estimate=COST,
        name="take_rows",
    )(y[None], traces, traces, traces, *after)


def encode_terms(terms, after):
    def body(a, *refs):
        b = refs[-1]
        code = jnp.clip((a[...] - REC_LOW) * REC_SCALE + 0.5, 0.0, 65535.0).astype(jnp.int32) - 32768
        b[...] = code.astype(jnp.int16)

    vm = pl.BlockSpec(memory_space=pltpu.VMEM)
    return pl.pallas_call(
        body,
        in_specs=[vm] + [pl.BlockSpec(memory_space=pl.ANY)] * len(after),
        out_specs=vm,
        out_shape=jax.ShapeDtypeStruct(terms.shape, jnp.int16),
        compiler_params=SMALL,
        cost_estimate=COST,
        name="encode_terms",
    )(terms, *after)


def spectra(traces, y, first, inner, rows, blocks, table, width):
    part, tile = traces.shape[1], 256
    share, start, steps = traces.shape[0] // NY // tile, first // tile, rows // tile

    def body(y_ref, b0, b1, b2, b3, t, *outs):
        for k, out in enumerate(outs):
            cols = pl.ds(k * 2 * width, 2 * width)
            acc = None
            for j, b in enumerate((b0, b1, b2, b3)):
                one = jnp.dot(b[...], t[pl.ds(j * part, part), cols], preferred_element_type=jnp.float32)
                acc = one if acc is None else acc + one
            re, im = acc[:, :width], acc[:, width:]
            logamp = 0.5 * jnp.log(re * re + im * im + 1.0)
            code = jnp.minimum(logamp * LA_SCALE + 0.5, 65535.0).astype(jnp.int32) - 32768
            out[...] = code.astype(jnp.int16)

    return pl.pallas_call(
        body,
        grid_spec=pltpu.PrefetchScalarGridSpec(
            num_scalar_prefetch=1,
            grid=(steps,),
            in_specs=[pl.BlockSpec((tile, part), lambda i, y: (y[0] * share + start + i, 0))]
            + [pl.BlockSpec((tile, part), lambda i, y: (inner // tile + i, 0))] * 3
            + [pl.BlockSpec(table.shape, lambda i, y: (0, 0))],
            out_specs=[pl.BlockSpec((tile, width), lambda i, y: (i, 0))] * 4,
        ),
        out_shape=[jax.ShapeDtypeStruct((rows, width), jnp.int16)] * 4,
        compiler_params=VMEM,
        cost_estimate=COST,
        name="spectra",
    )(y[None], traces, *blocks, table)


def gather_terms(coded, shot_near, rec_at, shot_at, after):
    rows, width = rec_at.shape[0], shot_near.shape[1]
    parts = len(coded)
    spans = spans_of(coded)

    def body(rec_at, shot_at, shot, *refs):
        out, rec = refs[parts + len(after) :]
        for code, at in zip(refs, spans):
            rec[at, :] = (code[...].astype(jnp.float32) + 32768.0) * (1.0 / REC_SCALE) + REC_LOW

        def step(b, _):
            at = [b * 32 + u for u in range(32)]
            row = [rec[pl.ds(rec_at[i], 1), :] + shot[pl.ds(shot_at[i], 1), :] for i in at]
            for i, value in zip(at, row):
                out[pl.ds(i, 1), :] = value
            return 0

        lax.fori_loop(0, rows // 32, step, 0)

    vm, sm = pl.BlockSpec(memory_space=pltpu.VMEM), pl.BlockSpec(memory_space=pltpu.SMEM)
    return pl.pallas_call(
        body,
        in_specs=[sm, sm, vm] + [vm] * parts + [pl.BlockSpec(memory_space=pl.ANY)] * len(after),
        out_specs=vm,
        out_shape=jax.ShapeDtypeStruct((rows, width), jnp.float32),
        scratch_shapes=[pltpu.VMEM((sum(code.shape[0] for code in coded), width), jnp.float32)],
        compiler_params=VMEM,
        cost_estimate=COST,
        name="gather_terms",
    )(rec_at, shot_at, shot_near, *coded, *after)


def residual(code, model, live):
    logamp = (code.astype(jnp.float32) + 32768.0) * (1.0 / LA_SCALE)
    alive = lax.broadcasted_iota(jnp.int32, code.shape, 0) < live
    return jnp.where(alive, logamp - model, 0.0)


def spans_of(codes):
    sizes = [code.shape[0] for code in codes]
    return [pl.ds(sum(sizes[:k]), size) for k, size in enumerate(sizes)]


def sum_receivers(codes, model, live, rec_at, count):
    rows, width = model.shape
    parts = len(codes)
    spans = spans_of(codes)
    banks, group = 8, 32

    def body(*refs):
        rec_at, live, model = refs[:3]
        codes = refs[3 : 3 + parts]
        near, far, res = refs[3 + parts : 6 + parts]
        sums = refs[6 + parts :]
        for s in sums:
            s[...] = jnp.zeros_like(s)
        for k, (code, at) in enumerate(zip(codes, spans)):
            res[at, :] = residual(code[...], model[at, :], live[k])

        def step(b, _):
            for u in range(group):
                s, at = sums[u % banks], pl.ds(rec_at[b * group + u], 1)
                s[at, :] = s[at, :] + res[pl.ds(b * group + u, 1), :]
            return 0

        lax.fori_loop(0, rows // group, step, 0)
        for out, at in ((near, pl.ds(0, count // 2)), (far, pl.ds(count // 2, count // 2))):
            out[...] = ((sums[0][at, :] + sums[1][at, :]) + (sums[2][at, :] + sums[3][at, :])) + (
                (sums[4][at, :] + sums[5][at, :]) + (sums[6][at, :] + sums[7][at, :])
            )

    vm, sm = pl.BlockSpec(memory_space=pltpu.VMEM), pl.BlockSpec(memory_space=pltpu.SMEM)
    return pl.pallas_call(
        body,
        in_specs=[sm, sm] + [vm] * (1 + parts),
        out_specs=[vm, vm],
        out_shape=[jax.ShapeDtypeStruct((count // 2, width), jnp.float32)] * 2,
        scratch_shapes=[pltpu.VMEM((rows, width), jnp.float32)] + [pltpu.VMEM((count, width), jnp.float32)] * banks,
        compiler_params=VMEM,
        cost_estimate=COST,
        name="sum_receivers",
    )(rec_at, live, model, *codes)


def sum_shots(codes, model, live, shot_at, count):
    rows, width = model.shape
    parts = len(codes)
    spans = spans_of(codes)

    def body(*refs):
        shot_at, live, model = refs[:3]
        codes, out = refs[3 : 3 + parts], refs[3 + parts]
        acc = jnp.zeros((count, 2 * width), jnp.float32)
        for k, (code, at) in enumerate(zip(codes, spans)):
            res = residual(code[...], model[at, :], live[k])
            high = res.astype(jnp.bfloat16)
            low = (res - high.astype(jnp.float32)).astype(jnp.bfloat16)
            both = jnp.concatenate([high, low], axis=1)
            hot = lax.broadcasted_iota(jnp.int32, (count, at.size), 0) == shot_at[:, at]
            acc = acc + jnp.dot(hot.astype(jnp.bfloat16), both, preferred_element_type=jnp.float32)
        out[...] = acc[:, :width] + acc[:, width:]

    vm, sm = pl.BlockSpec(memory_space=pltpu.VMEM), pl.BlockSpec(memory_space=pltpu.SMEM)
    return pl.pallas_call(
        body,
        in_specs=[vm, sm] + [vm] * (1 + parts),
        out_specs=vm,
        out_shape=jax.ShapeDtypeStruct((count, width), jnp.float32),
        compiler_params=VMEM,
        cost_estimate=COST,
        name="sum_shots",
    )(shot_at[None, :], live, model, *codes)


def neighbour(value, by):
    size = NZ * NX * NC
    return lax.ppermute(value, "tr", [(i, i + by) for i in range(size) if 0 <= i + by < size])


def per_device(traces, shot_index, receiver_index, live_counts, shot_terms, receiver_terms):
    rows, part = traces.shape
    block, width = shot_terms.shape
    share = rows // NY
    starts = [sum(SENT[:t]) for t in range(len(SENT))]
    first = [starts[t] + inner for t, inner, _ in BACK]
    owner, y = lax.axis_index("tr"), lax.axis_index("fq")
    z, x, c = owner // (NX * NC), owner // NC % NX, owner % NC

    got, after = [], ()
    for start, size in zip(starts, SENT):
        mine = take_rows(traces, y, start, size, after)
        come = {k: send_y(mine[k - 1], k) for k in (1, 3, 2)}
        got.append([come[k] for k in range(1, NY)])
        after = got[-1]
        if start == 0:
            mine_first = mine[0]
    table = make_table(part * NY, y, width)
    codes, coded = [], []
    for t, inner, size in BACK:
        coded.append(spectra(traces, y, starts[t] + inner, inner, size, got[t], table, width))
        codes += [send_y(coded[-1][k], k) if k else coded[-1][k] for k in range(NY)]

    def ordered(v):
        v = v.reshape(NY, share)
        v = jnp.stack([lax.dynamic_index_in_dim(v, (y - k) % NY, 0, keepdims=False) for k in range(NY)])
        return jnp.concatenate([v[:, at : at + size].reshape(NY * size) for at, (_, _, size) in zip(first, BACK)])

    near = receiver_index // block
    rz, rx, rc = near // (NX * NC), near // NC % NX, near % NC
    turn = rz ^ z
    place = (((rc ^ c) * NX + (rx ^ x)) * 2 + (turn & 1)) * (NZ // 2) + turn // 2
    rec_at = ordered(place * block + receiver_index % block)
    shot_at = ordered(shot_index - (owner - 1) * block)
    live = live_counts[0] - jnp.stack([(y - k) % NY * share + at for at in first for k in range(NY)])

    terms = encode_terms(receiver_terms, (mine_first,))
    terms = join([terms, swap(terms, 2, 0, 0)])
    terms = join([terms, swap(terms, 4, 0, 0)])
    terms = join([terms, swap(terms, 1, 0, 0)], (table,))
    shot_terms = join([shot_terms], (terms,))
    shot_near = jnp.concatenate([neighbour(shot_terms, 1), shot_terms, neighbour(shot_terms, -1)])
    terms = join([terms, swap(terms, 0, 1, 0)], got[0] + [shot_near, rec_at, shot_at])
    terms = join([terms, swap(terms, 0, 2, 0)], [coded[1][0]] + codes[1:NY])
    far_terms = [swap(terms, 0, 0, 1)]

    model = gather_terms([terms] + far_terms, shot_near, rec_at, shot_at, (coded[-1][0],))
    sums, far_sums = sum_receivers(codes, model, live, rec_at, block * NZ * NX * NC)
    sums = (sums + swap(far_sums, 0, 0, 1)).reshape(NX, 2, NZ // 2, block, width)
    shots = sum_shots(codes, model, live, shot_at, 3 * block)
    sent = (sums * SUM_SCALE).astype(jnp.float16)
    come = [swap(sent[k], 0, k, 0).astype(jnp.float32) for k in (1, 3, 2)]
    sums = sums[0] + (come[0] + come[1] + come[2]) * (1.0 / SUM_SCALE)
    shots = join([shots], (sums,))
    shot_sums = shots[block : 2 * block] + neighbour(shots[2 * block :], 1) + neighbour(shots[:block], -1)
    sent = (sums[1] * SUM_SCALE).astype(jnp.float16)
    sums = sums[0] + swap(sent, 1, 0, 0).astype(jnp.float32) * (1.0 / SUM_SCALE)
    sent = (sums * SUM_SCALE).astype(jnp.float16)
    come = [swap(sent[k], 2 * k, 0, 0).astype(jnp.float32) for k in (1, 3, 2)]
    receiver_sums = sums[0] + (come[0] + come[1] + come[2]) * (1.0 / SUM_SCALE)
    return (shot_sums, receiver_sums)


def solution(mesh):
    return jax.shard_map(
        per_device,
        mesh=mesh,
        in_specs=(P("tr", "fq"), P("tr"), P("tr"), P("tr"), P("tr", "fq"), P("tr", "fq")),
        out_specs=(P("tr", "fq"), P("tr", "fq")),
        check_vma=False,
    )
```

```python
import math

import jax
import jax.numpy as jnp
from jax import lax
from jax.experimental import pallas as pl
from jax.experimental.pallas import tpu as pltpu
from jax.sharding import PartitionSpec as P

NZ, NX, NC, NY = 8, 4, 2, 4
LA_TOP = 9.1
LA_SCALE = 65535.0 / LA_TOP
REC_LOW, REC_HIGH = 1.0, 2.2
REC_SCALE = 65535.0 / (REC_HIGH - REC_LOW)
SUM_SCALE = 1.0 / 32.0
SENT = (2048,)
BACK = ((0, 0, 1024), (0, 1024, 1024))
LARGE = pltpu.CompilerParams(vmem_limit_bytes=60 * 2**20)
SMALL = pltpu.CompilerParams(vmem_limit_bytes=12 * 2**20)
COST = pl.CostEstimate(flops=1000, bytes_accessed=1000, transcendentals=0)
VMEM = pltpu.CompilerParams(vmem_limit_bytes=56 * 2**20)


def tr_of(z, x, c):
    return (z * NX + x) * NC + c


def sites():
    return [(z, x, c) for z in range(NZ) for x in range(NX) for c in range(NC)]


def swap(value, dz, dx, dc):
    return lax.ppermute(value, "tr", [(tr_of(z, x, c), tr_of(z ^ dz, x ^ dx, c ^ dc)) for z, x, c in sites()])


def send_y(value, k):
    return lax.ppermute(value, "fq", [(i, (i + k) % NY) for i in range(NY)])


def make_table(samples, y, width):
    part, cols = samples // NY, NY * 2 * width
    tile = 128
    quarter = samples // 4
    shift = quarter.bit_length() - 1

    def body(y_ref, out):
        y = y_ref[0]
        row = pl.program_id(0) * tile
        time = (y - row // part) % NY * part + row % part + lax.broadcasted_iota(jnp.int32, (tile, 1), 0)
        for k in range(NY):
            first = (y + k) % NY * width
            for half in range(2):
                freq = first + lax.broadcasted_iota(jnp.int32, (1, width), 1)
                phase = (time * freq + half * quarter) & (samples - 1)
                turn = lax.shift_right_logical(phase + quarter // 2, shift)
                rest = (phase - turn * quarter).astype(jnp.float32) * (2.0 * math.pi / samples)
                sq = rest * rest
                cos = 1.0 + sq * (-0.5 + sq * (1 / 24 + sq * (-1 / 720 + sq * (1 / 40320 - sq * (1 / 3628800)))))
                sin = rest * (1.0 + sq * (-1 / 6 + sq * (1 / 120 + sq * (-1 / 5040 + sq * (1 / 362880)))))
                value = jnp.where((turn & 1) == 1, sin, cos)
                value = jnp.where(((turn + 1) & 2) == 2, -value, value)
                out[:, pl.ds((2 * k + half) * width, width)] = value.astype(jnp.bfloat16)

    return pl.pallas_call(
        body,
        grid=(samples // tile,),
        in_specs=[pl.BlockSpec(memory_space=pltpu.SMEM)],
        out_specs=pl.BlockSpec((tile, cols), lambda i: (i, 0)),
        out_shape=jax.ShapeDtypeStruct((samples, cols), jnp.bfloat16),
        compiler_params=SMALL,
        cost_estimate=pl.CostEstimate(flops=2**30, bytes_accessed=2**25, transcendentals=0),
        name="make_table",
    )(y[None])


def join(parts, after=()):
    size = parts[0].shape[0]

    def body(*refs):
        out = refs[-1]
        for k in range(len(parts)):
            out[pl.ds(k * size, size), :] = refs[k][...]

    vm = pl.BlockSpec(memory_space=pltpu.VMEM)
    return pl.pallas_call(
        body,
        in_specs=[vm] * len(parts) + [pl.BlockSpec(memory_space=pl.ANY)] * len(after),
        out_specs=vm,
        out_shape=jax.ShapeDtypeStruct((size * len(parts),) + parts[0].shape[1:], parts[0].dtype),
        compiler_params=SMALL,
        cost_estimate=COST,
        name="join",
    )(*parts, *after)


def take_rows(traces, y, first, piece, after=()):
    rows, part = traces.shape
    tile = 512
    share, start, steps = rows // NY // tile, first // tile, piece // tile

    def body(y_ref, *refs):
        for a, b in zip(refs[:3], refs[3 + len(after) :]):
            b[...] = a[...]

    def spot(k):
        return pl.BlockSpec((tile, part), lambda i, y: ((y[0] + k) % NY * share + start + i, 0))

    return pl.pallas_call(
        body,
        grid_spec=pltpu.PrefetchScalarGridSpec(
            num_scalar_prefetch=1,
            grid=(steps,),
            in_specs=[spot(k) for k in range(1, NY)] + [pl.BlockSpec(memory_space=pl.ANY)] * len(after),
            out_specs=[pl.BlockSpec((tile, part), lambda i, y: (i, 0))] * 3,
        ),
        out_shape=[jax.ShapeDtypeStruct((piece, part), traces.dtype)] * 3,
        compiler_params=LARGE,
        cost_estimate=COST,
        name="take_rows",
    )(y[None], traces, traces, traces, *after)


def encode_terms(terms, after):
    def body(a, *refs):
        b = refs[-1]
        code = jnp.clip((a[...] - REC_LOW) * REC_SCALE + 0.5, 0.0, 65535.0).astype(jnp.int32) - 32768
        b[...] = code.astype(jnp.int16)

    vm = pl.BlockSpec(memory_space=pltpu.VMEM)
    return pl.pallas_call(
        body,
        in_specs=[vm] + [pl.BlockSpec(memory_space=pl.ANY)] * len(after),
        out_specs=vm,
        out_shape=jax.ShapeDtypeStruct(terms.shape, jnp.int16),
        compiler_params=SMALL,
        cost_estimate=COST,
        name="encode_terms",
    )(terms, *after)


def spectra(traces, y, first, inner, rows, blocks, table, width):
    part, tile = traces.shape[1], 256
    share, start, steps = traces.shape[0] // NY // tile, first // tile, rows // tile

    def body(y_ref, b0, b1, b2, b3, t, *outs):
        for k, out in enumerate(outs):
            cols = pl.ds(k * 2 * width, 2 * width)
            acc = None
            for j, b in enumerate((b0, b1, b2, b3)):
                one = jnp.dot(b[...], t[pl.ds(j * part, part), cols], preferred_element_type=jnp.float32)
                acc = one if acc is None else acc + one
            re, im = acc[:, :width], acc[:, width:]
            logamp = 0.5 * jnp.log(re * re + im * im + 1.0)
            code = jnp.minimum(logamp * LA_SCALE + 0.5, 65535.0).astype(jnp.int32) - 32768
            out[...] = code.astype(jnp.int16)

    return pl.pallas_call(
        body,
        grid_spec=pltpu.PrefetchScalarGridSpec(
            num_scalar_prefetch=1,
            grid=(steps,),
            in_specs=[pl.BlockSpec((tile, part), lambda i, y: (y[0] * share + start + i, 0))]
            + [pl.BlockSpec((tile, part), lambda i, y: (inner // tile + i, 0))] * 3
            + [pl.BlockSpec(table.shape, lambda i, y: (0, 0))],
            out_specs=[pl.BlockSpec((tile, width), lambda i, y: (i, 0))] * 4,
        ),
        out_shape=[jax.ShapeDtypeStruct((rows, width), jnp.int16)] * 4,
        compiler_params=VMEM,
        cost_estimate=COST,
        name="spectra",
    )(y[None], traces, *blocks, table)


def gather_shots(shot_near, shot_at, sizes):
    width = shot_near.shape[1]
    unroll = 64

    def body(shot_at, shot, *outs):
        for k, out in enumerate(outs):

            def step(b, _, out=out, first=sum(sizes[:k])):
                at = [b * unroll + u for u in range(unroll)]
                row = [shot[pl.ds(shot_at[first + i], 1), :] for i in at]
                for i, value in zip(at, row):
                    out[pl.ds(i, 1), :] = value
                return 0

            lax.fori_loop(0, sizes[k] // unroll, step, 0)

    vm, sm = pl.BlockSpec(memory_space=pltpu.VMEM), pl.BlockSpec(memory_space=pltpu.SMEM)
    return pl.pallas_call(
        body,
        in_specs=[sm, vm],
        out_specs=[vm] * len(sizes),
        out_shape=[jax.ShapeDtypeStruct((size, width), jnp.float32) for size in sizes],
        compiler_params=VMEM,
        cost_estimate=COST,
        name="gather_shots",
    )(shot_at, shot_near)


def sum_receivers(codes, shots, coded, live, rec_at, before):
    rows, width = shots.shape
    size, half = codes[0].shape[0], coded[0].shape[0]
    banks, unroll = 4, 32
    parts, held = len(codes), len(before)

    def body(*refs):
        rec_at, live, shots, own, other = refs[:5]
        codes, before = refs[5 : 5 + parts], refs[5 + parts : 5 + parts + held]
        near, far, res, rec = refs[5 + parts + held : 9 + parts + held]
        sums = refs[9 + parts + held :]
        halves = (pl.ds(0, half), pl.ds(half, half))
        for code, at in zip((own, other), halves):
            rec[at, :] = (code[...].astype(jnp.float32) + 32768.0) * (1.0 / REC_SCALE) + REC_LOW
        rec[pl.ds(2 * half, 8), :] = jnp.zeros((8, width), jnp.float32)
        for k, s in enumerate(sums):
            if k or not held:
                s[...] = jnp.zeros_like(s)
        for s, at in zip(before, halves):
            sums[0][at, :] = s[...]
        for k, code in enumerate(codes):
            at = pl.ds(k * size, size)
            logamp = (code[...].astype(jnp.float32) + 32768.0) * (1.0 / LA_SCALE)
            alive = lax.broadcasted_iota(jnp.int32, code.shape, 0) < live[k]
            res[at, :] = jnp.where(alive, logamp - shots[at, :], 0.0)

        def step(b, _):
            for u in range(unroll):
                s, row, at = sums[u % banks], pl.ds(b * unroll + u, 1), pl.ds(rec_at[b * unroll + u], 1)
                value = res[row, :] - rec[at, :]
                s[at, :] = s[at, :] + value
                res[row, :] = value
            return 0

        lax.fori_loop(0, rows // unroll, step, 0)
        for out, at in zip((near, far), halves):
            out[...] = (sums[0][at, :] + sums[1][at, :]) + (sums[2][at, :] + sums[3][at, :])

    vm, sm = pl.BlockSpec(memory_space=pltpu.VMEM), pl.BlockSpec(memory_space=pltpu.SMEM)
    sums = pltpu.VMEM((2 * half + 8, width), jnp.float32)
    return pl.pallas_call(
        body,
        in_specs=[sm, sm] + [vm] * (3 + parts + held),
        out_specs=[vm] * 3,
        out_shape=[jax.ShapeDtypeStruct((n, width), jnp.float32) for n in (half, half, rows)],
        scratch_shapes=[sums] * (1 + banks),
        compiler_params=VMEM,
        cost_estimate=COST,
        name="sum_receivers",
    )(rec_at, live, shots, *coded, *codes, *before)


def sum_shots(residuals, shot_at, count):
    width = residuals[0].shape[1]
    tile = 1024

    def body(shot_at, *refs):
        acc, first = jnp.zeros((count, 2 * width), jnp.float32), 0
        for res in refs[:-1]:
            for k in range(0, res.shape[0], tile):
                value = res[pl.ds(k, tile), :]
                high = value.astype(jnp.bfloat16)
                low = (value - high.astype(jnp.float32)).astype(jnp.bfloat16)
                both = jnp.concatenate([high, low], axis=1)
                hot = lax.broadcasted_iota(jnp.int32, (count, tile), 0) == shot_at[:, pl.ds(first + k, tile)]
                acc = acc + jnp.dot(hot.astype(jnp.bfloat16), both, preferred_element_type=jnp.float32)
            first += res.shape[0]
        refs[-1][...] = acc[:, :width] + acc[:, width:]

    vm = pl.BlockSpec(memory_space=pltpu.VMEM)
    return pl.pallas_call(
        body,
        in_specs=[vm] * (1 + len(residuals)),
        out_specs=vm,
        out_shape=jax.ShapeDtypeStruct((count, width), jnp.float32),
        compiler_params=VMEM,
        cost_estimate=COST,
        name="sum_shots",
    )(shot_at[None, :], *residuals)


def neighbour(value, by):
    size = NZ * NX * NC
    return lax.ppermute(value, "tr", [(i, i + by) for i in range(size) if 0 <= i + by < size])


def per_device(traces, shot_index, receiver_index, live_counts, shot_terms, receiver_terms):
    rows, part = traces.shape
    block, width = shot_terms.shape
    share = rows // NY
    starts = [sum(SENT[:t]) for t in range(len(SENT))]
    first = [starts[t] + inner for t, inner, _ in BACK]
    owner, y = lax.axis_index("tr"), lax.axis_index("fq")
    z, x, c = owner // (NX * NC), owner // NC % NX, owner % NC

    got, after = [], ()
    for start, size in zip(starts, SENT):
        mine = take_rows(traces, y, start, size, after)
        come = {k: send_y(mine[k - 1], k) for k in (1, 3, 2)}
        got.append([come[k] for k in range(1, NY)])
        after = got[-1]
        if start == 0:
            mine_first = mine[0]
    table = make_table(part * NY, y, width)
    codes, coded = [], []
    for t, inner, size in BACK:
        coded.append(spectra(traces, y, starts[t] + inner, inner, size, got[t], table, width))
        codes += [send_y(coded[-1][k], k) if k else coded[-1][k] for k in range(NY)]

    def ordered(v):
        v = v.reshape(NY, share)
        v = jnp.stack([lax.dynamic_index_in_dim(v, (y - k) % NY, 0, keepdims=False) for k in range(NY)])
        return jnp.concatenate([v[:, at : at + size].reshape(NY * size) for at, (_, _, size) in zip(first, BACK)])

    near = receiver_index // block
    rz, rx, rc = near // (NX * NC), near // NC % NX, near % NC
    turn = rz ^ z
    place = (((rc ^ c) * NX + (rx ^ x)) * 2 + (turn & 1)) * (NZ // 2) + turn // 2
    place = place * block + receiver_index % block
    spare = block * NZ * NX * NC
    rec_at = ordered(jnp.where(jnp.arange(rows, dtype=jnp.int32) < live_counts[0], place, spare))
    shot_at = ordered(shot_index - (owner - 1) * block)
    live = live_counts[0] - jnp.stack([(y - k) % NY * share + at for at in first for k in range(NY)])

    terms = encode_terms(receiver_terms, (mine_first,))
    terms = join([terms, swap(terms, 2, 0, 0)])
    terms = join([terms, swap(terms, 4, 0, 0)])
    terms = join([terms, swap(terms, 1, 0, 0)], (table,))
    shot_terms = join([shot_terms], (terms,))
    shot_near = jnp.concatenate([neighbour(shot_terms, 1), shot_terms, neighbour(shot_terms, -1)])
    shots = gather_shots(shot_near, shot_at, [size * NY for _, _, size in BACK])
    terms = join([terms, swap(terms, 0, 1, 0)], got[0] + [shots[0], rec_at, coded[0][0]])
    terms = join([terms, swap(terms, 0, 2, 0)], [coded[1][0]] + codes[1:NY])
    far_terms = swap(terms, 0, 0, 1)

    sums, residuals, done = (), [], 0
    for h, part_shots in enumerate(shots):
        some = slice(h * NY, (h + 1) * NY)
        at = rec_at[done : done + part_shots.shape[0]]
        done += part_shots.shape[0]
        *sums, resid = sum_receivers(codes[some], part_shots, [terms, far_terms], live[some], at, sums)
        residuals.append(resid)
    sums, far_sums = sums
    sums = (sums + swap(far_sums, 0, 0, 1)).reshape(NX, 2, NZ // 2, block, width)
    shots = sum_shots(residuals, shot_at, 3 * block)
    sent = (sums * SUM_SCALE).astype(jnp.float16)
    come = [swap(sent[k], 0, k, 0).astype(jnp.float32) for k in (1, 3, 2)]
    mine = join([sums[0].reshape(-1, width)], (shots,)).reshape(sums.shape[1:])
    sums = mine + (come[0] + come[1] + come[2]) * (1.0 / SUM_SCALE)
    shots = join([shots], (sums,))
    shot_sums = shots[block : 2 * block] + neighbour(shots[2 * block :], 1) + neighbour(shots[:block], -1)
    sent = (sums[1] * SUM_SCALE).astype(jnp.float16)
    sums = sums[0] + swap(sent, 1, 0, 0).astype(jnp.float32) * (1.0 / SUM_SCALE)
    sums = sums.reshape(2, 2, block, width)
    sent = (sums[:, 1] * SUM_SCALE).astype(jnp.float16)
    sums = sums[:, 0] + swap(sent, 2, 0, 0).astype(jnp.float32) * (1.0 / SUM_SCALE)
    sent = (sums[1] * SUM_SCALE).astype(jnp.float16)
    receiver_sums = sums[0] + swap(sent, 4, 0, 0).astype(jnp.float32) * (1.0 / SUM_SCALE)
    return (shot_sums, receiver_sums)


def solution(mesh):
    return jax.shard_map(
        per_device,
        mesh=mesh,
        in_specs=(P("tr", "fq"), P("tr"), P("tr"), P("tr"), P("tr", "fq"), P("tr", "fq")),
        out_specs=(P("tr", "fq"), P("tr", "fq")),
        check_vma=False,
    )
```

```python
import math

import jax
import jax.numpy as jnp
from jax import lax
from jax.experimental import pallas as pl
from jax.experimental.pallas import tpu as pltpu
from jax.sharding import PartitionSpec as P

NZ, NX, NC, NY = 8, 4, 2, 4
LA_TOP = 9.1
LA_SCALE = 65535.0 / LA_TOP
REC_LOW, REC_HIGH = 1.0, 2.2
REC_SCALE = 65535.0 / (REC_HIGH - REC_LOW)
SUM_SCALE = 1.0 / 32.0
BACK = (768, 1280)
LARGE = pltpu.CompilerParams(vmem_limit_bytes=60 * 2**20)
SUMS = pltpu.CompilerParams(vmem_limit_bytes=44 * 2**20)
SMALL = pltpu.CompilerParams(vmem_limit_bytes=12 * 2**20)
COST = pl.CostEstimate(flops=1000, bytes_accessed=1000, transcendentals=0)
MEDIUM = pltpu.CompilerParams(vmem_limit_bytes=18 * 2**20)


def tr_of(z, x, c):
    return (z * NX + x) * NC + c


def sites():
    return [(z, x, c) for z in range(NZ) for x in range(NX) for c in range(NC)]


def swap(value, dz, dx, dc):
    return lax.ppermute(value, "tr", [(tr_of(z, x, c), tr_of(z ^ dz, x ^ dx, c ^ dc)) for z, x, c in sites()])


def send_y(value, k):
    return lax.ppermute(value, "fq", [(i, (i + k) % NY) for i in range(NY)])


def make_table(samples, y, width):
    part, cols = samples // NY, NY * 2 * width
    tile = 128
    quarter = samples // 4
    shift = quarter.bit_length() - 1

    def body(y_ref, out):
        y = y_ref[0]
        row = pl.program_id(0) * tile
        time = (y - row // part) % NY * part + row % part + lax.broadcasted_iota(jnp.int32, (tile, 1), 0)
        for k in range(NY):
            first = (y + k) % NY * width
            for half in range(2):
                freq = first + lax.broadcasted_iota(jnp.int32, (1, width), 1)
                phase = (time * freq + half * quarter) & (samples - 1)
                turn = lax.shift_right_logical(phase + quarter // 2, shift)
                rest = (phase - turn * quarter).astype(jnp.float32) * (2.0 * math.pi / samples)
                sq = rest * rest
                cos = 1.0 + sq * (-0.5 + sq * (1 / 24 + sq * (-1 / 720 + sq * (1 / 40320 - sq * (1 / 3628800)))))
                sin = rest * (1.0 + sq * (-1 / 6 + sq * (1 / 120 + sq * (-1 / 5040 + sq * (1 / 362880)))))
                value = jnp.where((turn & 1) == 1, sin, cos)
                value = jnp.where(((turn + 1) & 2) == 2, -value, value)
                out[:, pl.ds((2 * k + half) * width, width)] = value.astype(jnp.bfloat16)

    return pl.pallas_call(
        body,
        grid=(samples // tile,),
        in_specs=[pl.BlockSpec(memory_space=pltpu.SMEM)],
        out_specs=pl.BlockSpec((tile, cols), lambda i: (i, 0)),
        out_shape=jax.ShapeDtypeStruct((samples, cols), jnp.bfloat16),
        compiler_params=SMALL,
        cost_estimate=pl.CostEstimate(flops=2**30, bytes_accessed=2**25, transcendentals=0),
        name="make_table",
    )(y[None])


def join(parts, after=()):
    size = parts[0].shape[0]

    def body(*refs):
        out = refs[-1]
        for k in range(len(parts)):
            out[pl.ds(k * size, size), :] = refs[k][...]

    vm = pl.BlockSpec(memory_space=pltpu.VMEM)
    return pl.pallas_call(
        body,
        in_specs=[vm] * len(parts) + [pl.BlockSpec(memory_space=pl.ANY)] * len(after),
        out_specs=vm,
        out_shape=jax.ShapeDtypeStruct((size * len(parts),) + parts[0].shape[1:], parts[0].dtype),
        compiler_params=SMALL,
        cost_estimate=COST,
        name="join",
    )(*parts, *after)


def take_rows(traces, y, k):
    rows, part = traces.shape
    tile = 512
    steps = rows // NY // tile

    def body(y_ref, a, b):
        b[...] = a[...]

    return pl.pallas_call(
        body,
        grid_spec=pltpu.PrefetchScalarGridSpec(
            num_scalar_prefetch=1,
            grid=(steps,),
            in_specs=[pl.BlockSpec((tile, part), lambda i, y: ((y[0] + k) % NY * steps + i, 0))],
            out_specs=pl.BlockSpec((tile, part), lambda i, y: (i, 0)),
        ),
        out_shape=jax.ShapeDtypeStruct((rows // NY, part), traces.dtype),
        compiler_params=LARGE,
        cost_estimate=COST,
        name="take_rows",
    )(y[None], traces)


def encode_terms(terms, after):
    def body(a, *refs):
        b = refs[-1]
        code = jnp.clip((a[...] - REC_LOW) * REC_SCALE + 0.5, 0.0, 65535.0).astype(jnp.int32) - 32768
        b[...] = code.astype(jnp.int16)

    vm = pl.BlockSpec(memory_space=pltpu.VMEM)
    return pl.pallas_call(
        body,
        in_specs=[vm] + [pl.BlockSpec(memory_space=pl.ANY)] * len(after),
        out_specs=vm,
        out_shape=jax.ShapeDtypeStruct(terms.shape, jnp.int16),
        compiler_params=SMALL,
        cost_estimate=COST,
        name="encode_terms",
    )(terms, *after)


def spectra(traces, y, first, rows, blocks, table, width):
    part, tile = traces.shape[1], 256
    share, start, steps = traces.shape[0] // NY // tile, first // tile, rows // tile

    def body(y_ref, b0, b1, b2, b3, t, *outs):
        for k, out in enumerate(outs):
            cols = pl.ds(k * 2 * width, 2 * width)
            acc = None
            for j, b in enumerate((b0, b1, b2, b3)):
                one = jnp.dot(b[...], t[pl.ds(j * part, part), cols], preferred_element_type=jnp.float32)
                acc = one if acc is None else acc + one
            re, im = acc[:, :width], acc[:, width:]
            logamp = 0.5 * jnp.log(re * re + im * im + 1.0)
            code = jnp.minimum(logamp * LA_SCALE + 0.5, 65535.0).astype(jnp.int32) - 32768
            out[...] = code.astype(jnp.int16)

    return pl.pallas_call(
        body,
        grid_spec=pltpu.PrefetchScalarGridSpec(
            num_scalar_prefetch=1,
            grid=(steps,),
            in_specs=[pl.BlockSpec((tile, part), lambda i, y: (y[0] * share + start + i, 0))]
            + [pl.BlockSpec((tile, part), lambda i, y: (start + i, 0))] * 3
            + [pl.BlockSpec(table.shape, lambda i, y: (0, 0))],
            out_specs=[pl.BlockSpec((tile, width), lambda i, y: (i, 0))] * 4,
        ),
        out_shape=[jax.ShapeDtypeStruct((rows, width), jnp.int16)] * 4,
        compiler_params=MEDIUM,
        cost_estimate=COST,
        name="spectra",
    )(y[None], traces, *blocks, table)


def gather_shots(shot_near, shot_at, sizes):
    width = shot_near.shape[1]
    unroll = 64

    def body(shot_at, shot, *outs):
        for k, out in enumerate(outs):

            def step(b, _, out=out, first=sum(sizes[:k])):
                at = [b * unroll + u for u in range(unroll)]
                row = [shot[pl.ds(shot_at[first + i], 1), :] for i in at]
                for i, value in zip(at, row):
                    out[pl.ds(i, 1), :] = value
                return 0

            lax.fori_loop(0, sizes[k] // unroll, step, 0)

    vm, sm = pl.BlockSpec(memory_space=pltpu.VMEM), pl.BlockSpec(memory_space=pltpu.SMEM)
    return pl.pallas_call(
        body,
        in_specs=[sm, vm],
        out_specs=[vm] * len(sizes),
        out_shape=[jax.ShapeDtypeStruct((size, width), jnp.float32) for size in sizes],
        compiler_params=MEDIUM,
        cost_estimate=COST,
        name="gather_shots",
    )(shot_at, shot_near)


def sum_receivers(codes, shots, coded, live, rec_at, before):
    rows, width = shots.shape
    size, half = codes[0].shape[0], coded[0].shape[0]
    banks, unroll = 4, 32
    parts, held = len(codes), len(before)

    def body(*refs):
        rec_at, live, shots, own, other = refs[:5]
        codes, before = refs[5 : 5 + parts], refs[5 + parts : 5 + parts + held]
        near, far, res, rec = refs[5 + parts + held : 9 + parts + held]
        sums = refs[9 + parts + held :]
        halves = (pl.ds(0, half), pl.ds(half, half))
        for code, at in zip((own, other), halves):
            rec[at, :] = (code[...].astype(jnp.float32) + 32768.0) * (1.0 / REC_SCALE) + REC_LOW
        rec[pl.ds(2 * half, 8), :] = jnp.zeros((8, width), jnp.float32)
        for k, s in enumerate(sums):
            if k or not held:
                s[...] = jnp.zeros_like(s)
        for s, at in zip(before, halves):
            sums[0][at, :] = s[...]
        for k, code in enumerate(codes):
            at = pl.ds(k * size, size)
            logamp = (code[...].astype(jnp.float32) + 32768.0) * (1.0 / LA_SCALE)
            alive = lax.broadcasted_iota(jnp.int32, code.shape, 0) < live[k]
            res[at, :] = jnp.where(alive, logamp - shots[at, :], 0.0)

        def step(b, _):
            for u in range(unroll):
                s, row, at = sums[u % banks], pl.ds(b * unroll + u, 1), pl.ds(rec_at[b * unroll + u], 1)
                value = res[row, :] - rec[at, :]
                s[at, :] = s[at, :] + value
                res[row, :] = value
            return 0

        lax.fori_loop(0, rows // unroll, step, 0)
        for out, at in zip((near, far), halves):
            out[...] = (sums[0][at, :] + sums[1][at, :]) + (sums[2][at, :] + sums[3][at, :])

    vm, sm = pl.BlockSpec(memory_space=pltpu.VMEM), pl.BlockSpec(memory_space=pltpu.SMEM)
    sums = pltpu.VMEM((2 * half + 8, width), jnp.float32)
    return pl.pallas_call(
        body,
        in_specs=[sm, sm] + [vm] * (3 + parts + held),
        out_specs=[vm] * 3,
        out_shape=[jax.ShapeDtypeStruct((n, width), jnp.float32) for n in (half, half, rows)],
        scratch_shapes=[sums] * (1 + banks),
        compiler_params=SUMS,
        cost_estimate=COST,
        name="sum_receivers",
    )(rec_at, live, shots, *coded, *codes, *before)


def sum_shots(residuals, shot_at, count):
    width = residuals[0].shape[1]
    tile = 1024

    def body(shot_at, *refs):
        acc, first = jnp.zeros((count, 2 * width), jnp.float32), 0
        for res in refs[:-1]:
            for k in range(0, res.shape[0], tile):
                value = res[pl.ds(k, tile), :]
                high = value.astype(jnp.bfloat16)
                low = (value - high.astype(jnp.float32)).astype(jnp.bfloat16)
                both = jnp.concatenate([high, low], axis=1)
                hot = lax.broadcasted_iota(jnp.int32, (count, tile), 0) == shot_at[:, pl.ds(first + k, tile)]
                acc = acc + jnp.dot(hot.astype(jnp.bfloat16), both, preferred_element_type=jnp.float32)
            first += res.shape[0]
        refs[-1][...] = acc[:, :width] + acc[:, width:]

    vm = pl.BlockSpec(memory_space=pltpu.VMEM)
    return pl.pallas_call(
        body,
        in_specs=[vm] * (1 + len(residuals)),
        out_specs=vm,
        out_shape=jax.ShapeDtypeStruct((count, width), jnp.float32),
        compiler_params=MEDIUM,
        cost_estimate=COST,
        name="sum_shots",
    )(shot_at[None, :], *residuals)


def neighbour(value, by):
    size = NZ * NX * NC
    return lax.ppermute(value, "tr", [(i, i + by) for i in range(size) if 0 <= i + by < size])


def per_device(traces, shot_index, receiver_index, live_counts, shot_terms, receiver_terms):
    rows, part = traces.shape
    block, width = shot_terms.shape
    share = rows // NY
    first = [sum(BACK[:h]) for h in range(len(BACK))]
    owner, y = lax.axis_index("tr"), lax.axis_index("fq")
    z, x, c = owner // (NX * NC), owner // NC % NX, owner % NC

    come = {k: send_y(take_rows(traces, y, k), k) for k in (1, 3, 2)}
    got = [come[k] for k in range(1, NY)]
    table = make_table(part * NY, y, width)
    codes, coded = [], []
    for at, size in zip(first, BACK):
        coded.append(spectra(traces, y, at, size, got, table, width))
        codes += [send_y(coded[-1][k], k) if k else coded[-1][k] for k in range(NY)]

    def ordered(v):
        v = v.reshape(NY, share)
        v = jnp.stack([lax.dynamic_index_in_dim(v, (y - k) % NY, 0, keepdims=False) for k in range(NY)])
        return jnp.concatenate([v[:, at : at + size].reshape(NY * size) for at, size in zip(first, BACK)])

    near = receiver_index // block
    rz, rx, rc = near // (NX * NC), near // NC % NX, near % NC
    turn = rz ^ z
    place = (((rc ^ c) * NX + (rx ^ x)) * 2 + (turn & 1)) * (NZ // 2) + turn // 2
    place = place * block + receiver_index % block
    spare = block * NZ * NX * NC
    rec_at = ordered(jnp.where(jnp.arange(rows, dtype=jnp.int32) < live_counts[0], place, spare))
    shot_at = ordered(shot_index - (owner - 1) * block)
    live = live_counts[0] - jnp.stack([(y - k) % NY * share + at for at in first for k in range(NY)])

    terms = encode_terms(receiver_terms, (table,))
    terms = join([terms, swap(terms, 2, 0, 0)])
    terms = join([terms, swap(terms, 4, 0, 0)])
    terms = join([terms, swap(terms, 1, 0, 0)])
    shot_terms = join([shot_terms], (terms,))
    shot_near = jnp.concatenate([neighbour(shot_terms, 1), shot_terms, neighbour(shot_terms, -1)])
    shots = gather_shots(shot_near, shot_at, [size * NY for size in BACK])
    terms = join([terms, swap(terms, 0, 1, 0)], got + [shots[0], rec_at, coded[0][0]])
    terms = join([terms, swap(terms, 0, 2, 0)], [coded[1][0]] + codes[1:NY])
    far_terms = swap(terms, 0, 0, 1)

    sums, residuals, done = (), [], 0
    for h, part_shots in enumerate(shots):
        some = slice(h * NY, (h + 1) * NY)
        at = rec_at[done : done + part_shots.shape[0]]
        done += part_shots.shape[0]
        *sums, resid = sum_receivers(codes[some], part_shots, [terms, far_terms], live[some], at, sums)
        residuals.append(resid)
    sums, far_sums = sums
    sums = (sums + swap(far_sums, 0, 0, 1)).reshape(NX, 2, NZ // 2, block, width)
    shots = sum_shots(residuals, shot_at, 3 * block)
    sent = (sums * SUM_SCALE).astype(jnp.float16)
    come = [swap(sent[k], 0, k, 0).astype(jnp.float32) for k in (1, 3, 2)]
    mine = join([sums[0].reshape(-1, width)], (shots,)).reshape(sums.shape[1:])
    sums = mine + (come[0] + come[1] + come[2]) * (1.0 / SUM_SCALE)
    shot_sums = shots[block : 2 * block] + neighbour(shots[2 * block :], 1) + neighbour(shots[:block], -1)
    sent = (sums[1] * SUM_SCALE).astype(jnp.float16)
    mine = join([sums[0].reshape(-1, width)], (shot_sums,)).reshape(sums.shape[1:])
    sums = mine + swap(sent, 1, 0, 0).astype(jnp.float32) * (1.0 / SUM_SCALE)
    sums = sums.reshape(2, 2, block, width)
    sent = (sums[:, 1] * SUM_SCALE).astype(jnp.float16)
    sums = sums[:, 0] + swap(sent, 2, 0, 0).astype(jnp.float32) * (1.0 / SUM_SCALE)
    sent = (sums[1] * SUM_SCALE).astype(jnp.float16)
    receiver_sums = sums[0] + swap(sent, 4, 0, 0).astype(jnp.float32) * (1.0 / SUM_SCALE)
    return (shot_sums, receiver_sums)


def solution(mesh):
    return jax.shard_map(
        per_device,
        mesh=mesh,
        in_specs=(P("tr", "fq"), P("tr"), P("tr"), P("tr"), P("tr", "fq"), P("tr", "fq")),
        out_specs=(P("tr", "fq"), P("tr", "fq")),
        check_vma=False,
    )
```

```python
import math

import jax
import jax.numpy as jnp
from jax import lax
from jax.experimental import pallas as pl
from jax.experimental.pallas import tpu as pltpu
from jax.sharding import PartitionSpec as P

NZ, NX, NC, NY = 8, 4, 2, 4
LA_TOP = 9.1
LA_SCALE = 65535.0 / LA_TOP
REC_LOW, REC_HIGH = 1.0, 2.2
REC_SCALE = 65535.0 / (REC_HIGH - REC_LOW)
SUM_SCALE = 1.0 / 32.0
PIECES = (1024, 1024)
LARGE = pltpu.CompilerParams(vmem_limit_bytes=60 * 2**20)
SUMS = pltpu.CompilerParams(vmem_limit_bytes=44 * 2**20)
SMALL = pltpu.CompilerParams(vmem_limit_bytes=12 * 2**20)
COST = pl.CostEstimate(flops=1000, bytes_accessed=1000, transcendentals=0)
MEDIUM = pltpu.CompilerParams(vmem_limit_bytes=18 * 2**20)


def tr_of(z, x, c):
    return (z * NX + x) * NC + c


def sites():
    return [(z, x, c) for z in range(NZ) for x in range(NX) for c in range(NC)]


def swap(value, dz, dx, dc):
    return lax.ppermute(value, "tr", [(tr_of(z, x, c), tr_of(z ^ dz, x ^ dx, c ^ dc)) for z, x, c in sites()])


def send_y(value, k):
    return lax.ppermute(value, "fq", [(i, (i + k) % NY) for i in range(NY)])


def make_table(samples, y, width, after):
    part, cols = samples // NY, NY * 2 * width
    tile = 128
    quarter = samples // 4
    shift = quarter.bit_length() - 1

    def body(y_ref, *refs):
        y, out = y_ref[0], refs[-1]
        row = pl.program_id(0) * tile
        time = (y - row // part) % NY * part + row % part + lax.broadcasted_iota(jnp.int32, (tile, 1), 0)
        for k in range(NY):
            first = (y + k) % NY * width
            for half in range(2):
                freq = first + lax.broadcasted_iota(jnp.int32, (1, width), 1)
                phase = (time * freq + half * quarter) & (samples - 1)
                turn = lax.shift_right_logical(phase + quarter // 2, shift)
                rest = (phase - turn * quarter).astype(jnp.float32) * (2.0 * math.pi / samples)
                sq = rest * rest
                cos = 1.0 + sq * (-0.5 + sq * (1 / 24 + sq * (-1 / 720 + sq * (1 / 40320 - sq * (1 / 3628800)))))
                sin = rest * (1.0 + sq * (-1 / 6 + sq * (1 / 120 + sq * (-1 / 5040 + sq * (1 / 362880)))))
                value = jnp.where((turn & 1) == 1, sin, cos)
                value = jnp.where(((turn + 1) & 2) == 2, -value, value)
                out[:, pl.ds((2 * k + half) * width, width)] = value.astype(jnp.bfloat16)

    return pl.pallas_call(
        body,
        grid=(samples // tile,),
        in_specs=[pl.BlockSpec(memory_space=pltpu.SMEM)] + [pl.BlockSpec(memory_space=pl.ANY)] * len(after),
        out_specs=pl.BlockSpec((tile, cols), lambda i: (i, 0)),
        out_shape=jax.ShapeDtypeStruct((samples, cols), jnp.bfloat16),
        compiler_params=SMALL,
        cost_estimate=pl.CostEstimate(flops=2**30, bytes_accessed=2**25, transcendentals=0),
        name="make_table",
    )(y[None], *after)


def join(parts, after=()):
    size = parts[0].shape[0]

    def body(*refs):
        out = refs[-1]
        for k in range(len(parts)):
            out[pl.ds(k * size, size), :] = refs[k][...]

    vm = pl.BlockSpec(memory_space=pltpu.VMEM)
    return pl.pallas_call(
        body,
        in_specs=[vm] * len(parts) + [pl.BlockSpec(memory_space=pl.ANY)] * len(after),
        out_specs=vm,
        out_shape=jax.ShapeDtypeStruct((size * len(parts),) + parts[0].shape[1:], parts[0].dtype),
        compiler_params=SMALL,
        cost_estimate=COST,
        name="join",
    )(*parts, *after)


def take_rows(traces, y, first, size, after=()):
    rows, part = traces.shape

    def body(y_ref, traces, *refs):
        outs, sems = refs[len(after) : len(after) + NY], refs[len(after) + NY :]
        copies = []
        for k in range(NY):
            at = pl.multiple_of((y_ref[0] + k) % NY * (rows // NY) + first, 16)
            copies.append(pltpu.make_async_copy(traces.at[pl.ds(at, size), :], outs[k], sems[k]))
        for copy in copies:
            copy.start()
        for copy in copies:
            copy.wait()

    hbm = pl.BlockSpec(memory_space=pl.ANY)
    return pl.pallas_call(
        body,
        in_specs=[pl.BlockSpec(memory_space=pltpu.SMEM), hbm] + [hbm] * len(after),
        out_specs=[hbm] * NY,
        out_shape=[jax.ShapeDtypeStruct((size, part), traces.dtype)] * NY,
        scratch_shapes=[pltpu.SemaphoreType.DMA] * NY,
        compiler_params=LARGE,
        cost_estimate=COST,
        name="take_rows",
    )(y[None], traces, *after)


def encode_terms(terms, after):
    def body(a, *refs):
        b = refs[-1]
        code = jnp.clip((a[...] - REC_LOW) * REC_SCALE + 0.5, 0.0, 65535.0).astype(jnp.int32) - 32768
        b[...] = code.astype(jnp.int16)

    vm = pl.BlockSpec(memory_space=pltpu.VMEM)
    return pl.pallas_call(
        body,
        in_specs=[vm] + [pl.BlockSpec(memory_space=pl.ANY)] * len(after),
        out_specs=vm,
        out_shape=jax.ShapeDtypeStruct(terms.shape, jnp.int16),
        compiler_params=SMALL,
        cost_estimate=COST,
        name="encode_terms",
    )(terms, *after)


def spectra(blocks, table, width):
    rows, part = blocks[0].shape
    tile = 512

    def body(b0, b1, b2, b3, t, *outs):
        for k, out in enumerate(outs):
            cols = pl.ds(k * 2 * width, 2 * width)
            acc = None
            for j, b in enumerate((b0, b1, b2, b3)):
                one = jnp.dot(b[...], t[pl.ds(j * part, part), cols], preferred_element_type=jnp.float32)
                acc = one if acc is None else acc + one
            re, im = acc[:, :width], acc[:, width:]
            logamp = 0.5 * jnp.log(re * re + im * im + 1.0)
            code = jnp.minimum(logamp * LA_SCALE + 0.5, 65535.0).astype(jnp.int32) - 32768
            out[...] = code.astype(jnp.int16)

    return pl.pallas_call(
        body,
        grid=(rows // tile,),
        in_specs=[pl.BlockSpec((tile, part), lambda i: (i, 0))] * NY + [pl.BlockSpec(table.shape, lambda i: (0, 0))],
        out_specs=[pl.BlockSpec((tile, width), lambda i: (i, 0))] * NY,
        out_shape=[jax.ShapeDtypeStruct((rows, width), jnp.int16)] * NY,
        compiler_params=MEDIUM,
        cost_estimate=COST,
        name="spectra",
    )(*blocks, table)


def gather_shots(shot_near, shot_at, sizes):
    width = shot_near.shape[1]
    unroll = 64

    def body(shot_at, shot, *outs):
        for k, out in enumerate(outs):

            def step(b, _, out=out, first=sum(sizes[:k])):
                at = [b * unroll + u for u in range(unroll)]
                row = [shot[pl.ds(shot_at[first + i], 1), :] for i in at]
                for i, value in zip(at, row):
                    out[pl.ds(i, 1), :] = value
                return 0

            lax.fori_loop(0, sizes[k] // unroll, step, 0)

    vm, sm = pl.BlockSpec(memory_space=pltpu.VMEM), pl.BlockSpec(memory_space=pltpu.SMEM)
    return pl.pallas_call(
        body,
        in_specs=[sm, vm],
        out_specs=[vm] * len(sizes),
        out_shape=[jax.ShapeDtypeStruct((size, width), jnp.float32) for size in sizes],
        compiler_params=MEDIUM,
        cost_estimate=COST,
        name="gather_shots",
    )(shot_at, shot_near)


def sum_receivers(codes, shots, coded, live, rec_at, before):
    rows, width = shots.shape
    size, half = codes[0].shape[0], coded[0].shape[0]
    banks, unroll = 4, 32
    parts, held = len(codes), len(before)

    def body(*refs):
        rec_at, live, shots, own, other = refs[:5]
        codes, before = refs[5 : 5 + parts], refs[5 + parts : 5 + parts + held]
        near, far, res, rec = refs[5 + parts + held : 9 + parts + held]
        sums = refs[9 + parts + held :]
        halves = (pl.ds(0, half), pl.ds(half, half))
        for code, at in zip((own, other), halves):
            rec[at, :] = (code[...].astype(jnp.float32) + 32768.0) * (1.0 / REC_SCALE) + REC_LOW
        rec[pl.ds(2 * half, 8), :] = jnp.zeros((8, width), jnp.float32)
        for k, s in enumerate(sums):
            if k or not held:
                s[...] = jnp.zeros_like(s)
        for s, at in zip(before, halves):
            sums[0][at, :] = s[...]
        for k, code in enumerate(codes):
            at = pl.ds(k * size, size)
            logamp = (code[...].astype(jnp.float32) + 32768.0) * (1.0 / LA_SCALE)
            alive = lax.broadcasted_iota(jnp.int32, code.shape, 0) < live[k]
            res[at, :] = jnp.where(alive, logamp - shots[at, :], 0.0)

        def step(b, _):
            for u in range(unroll):
                s, row, at = sums[u % banks], pl.ds(b * unroll + u, 1), pl.ds(rec_at[b * unroll + u], 1)
                value = res[row, :] - rec[at, :]
                s[at, :] = s[at, :] + value
                res[row, :] = value
            return 0

        lax.fori_loop(0, rows // unroll, step, 0)
        for out, at in zip((near, far), halves):
            out[...] = (sums[0][at, :] + sums[1][at, :]) + (sums[2][at, :] + sums[3][at, :])

    vm, sm = pl.BlockSpec(memory_space=pltpu.VMEM), pl.BlockSpec(memory_space=pltpu.SMEM)
    sums = pltpu.VMEM((2 * half + 8, width), jnp.float32)
    return pl.pallas_call(
        body,
        in_specs=[sm, sm] + [vm] * (3 + parts + held),
        out_specs=[vm] * 3,
        out_shape=[jax.ShapeDtypeStruct((n, width), jnp.float32) for n in (half, half, rows)],
        scratch_shapes=[sums] * (1 + banks),
        compiler_params=SUMS,
        cost_estimate=COST,
        name="sum_receivers",
    )(rec_at, live, shots, *coded, *codes, *before)


def sum_shots(residuals, shot_at, count):
    width = residuals[0].shape[1]
    tile = 1024

    def body(shot_at, *refs):
        acc, first = jnp.zeros((count, 2 * width), jnp.float32), 0
        for res in refs[:-1]:
            for k in range(0, res.shape[0], tile):
                value = res[pl.ds(k, tile), :]
                high = value.astype(jnp.bfloat16)
                low = (value - high.astype(jnp.float32)).astype(jnp.bfloat16)
                both = jnp.concatenate([high, low], axis=1)
                hot = lax.broadcasted_iota(jnp.int32, (count, tile), 0) == shot_at[:, pl.ds(first + k, tile)]
                acc = acc + jnp.dot(hot.astype(jnp.bfloat16), both, preferred_element_type=jnp.float32)
            first += res.shape[0]
        refs[-1][...] = acc[:, :width] + acc[:, width:]

    vm = pl.BlockSpec(memory_space=pltpu.VMEM)
    return pl.pallas_call(
        body,
        in_specs=[vm] * (1 + len(residuals)),
        out_specs=vm,
        out_shape=jax.ShapeDtypeStruct((count, width), jnp.float32),
        compiler_params=MEDIUM,
        cost_estimate=COST,
        name="sum_shots",
    )(shot_at[None, :], *residuals)


def neighbour(value, by):
    size = NZ * NX * NC
    return lax.ppermute(value, "tr", [(i, i + by) for i in range(size) if 0 <= i + by < size])


def per_device(traces, shot_index, receiver_index, live_counts, shot_terms, receiver_terms):
    rows, part = traces.shape
    block, width = shot_terms.shape
    share = rows // NY
    first = [sum(PIECES[:h]) for h in range(len(PIECES))]
    owner, y = lax.axis_index("tr"), lax.axis_index("fq")
    z, x, c = owner // (NX * NC), owner // NC % NX, owner % NC

    got, after = [], ()
    for at, size in zip(first, PIECES):
        mine = take_rows(traces, y, at, size, after)
        come = {k: send_y(mine[k], k) for k in (1, 3, 2)}
        after = [come[k] for k in range(1, NY)]
        got.append([mine[0]] + after)
    table = make_table(part * NY, y, width, got[0][:1])
    codes, coded = [], []
    for blocks in got:
        coded.append(spectra(blocks, table, width))
        codes += [send_y(coded[-1][k], k) if k else coded[-1][k] for k in range(NY)]

    def ordered(v):
        v = v.reshape(NY, share)
        v = jnp.stack([lax.dynamic_index_in_dim(v, (y - k) % NY, 0, keepdims=False) for k in range(NY)])
        return jnp.concatenate([v[:, at : at + size].reshape(NY * size) for at, size in zip(first, PIECES)])

    near = receiver_index // block
    rz, rx, rc = near // (NX * NC), near // NC % NX, near % NC
    turn = rz ^ z
    place = (((rc ^ c) * NX + (rx ^ x)) * 2 + (turn & 1)) * (NZ // 2) + turn // 2
    place = place * block + receiver_index % block
    spare = block * NZ * NX * NC
    rec_at = ordered(jnp.where(jnp.arange(rows, dtype=jnp.int32) < live_counts[0], place, spare))
    shot_at = ordered(shot_index - (owner - 1) * block)
    live = live_counts[0] - jnp.stack([(y - k) % NY * share + at for at in first for k in range(NY)])

    terms = encode_terms(receiver_terms, (table,))
    terms = join([terms, swap(terms, 2, 0, 0)])
    terms = join([terms, swap(terms, 4, 0, 0)], got[0][1:])
    terms = join([terms, swap(terms, 1, 0, 0)], got[1][:1])
    shot_terms = join([shot_terms], (terms,))
    shot_near = jnp.concatenate([neighbour(shot_terms, 1), shot_terms, neighbour(shot_terms, -1)])
    shots = gather_shots(shot_near, shot_at, [size * NY for size in PIECES])
    terms = join([terms, swap(terms, 0, 1, 0)], [coded[0][0]])
    terms = join([terms, swap(terms, 0, 2, 0)], [shots[0], rec_at] + got[1][1:])
    far_terms = swap(terms, 0, 0, 1)

    sums, residuals, done = (), [], 0
    for h, part_shots in enumerate(shots):
        some = slice(h * NY, (h + 1) * NY)
        at = rec_at[done : done + part_shots.shape[0]]
        done += part_shots.shape[0]
        *sums, resid = sum_receivers(codes[some], part_shots, [terms, far_terms], live[some], at, sums)
        residuals.append(resid)
    sums, far_sums = sums
    sums = (sums + swap(far_sums, 0, 0, 1)).reshape(NX, 2, NZ // 2, block, width)
    shots = sum_shots(residuals, shot_at, 3 * block)
    sent = (sums * SUM_SCALE).astype(jnp.float16)
    come = [swap(sent[k], 0, k, 0).astype(jnp.float32) for k in (1, 3, 2)]
    mine = join([sums[0].reshape(-1, width)], (shots,)).reshape(sums.shape[1:])
    sums = mine + (come[0] + come[1] + come[2]) * (1.0 / SUM_SCALE)
    shot_sums = shots[block : 2 * block] + neighbour(shots[2 * block :], 1) + neighbour(shots[:block], -1)
    sent = (sums[1] * SUM_SCALE).astype(jnp.float16)
    mine = join([sums[0].reshape(-1, width)], (shot_sums,)).reshape(sums.shape[1:])
    sums = mine + swap(sent, 1, 0, 0).astype(jnp.float32) * (1.0 / SUM_SCALE)
    sums = sums.reshape(2, 2, block, width)
    sent = (sums[:, 1] * SUM_SCALE).astype(jnp.float16)
    sums = sums[:, 0] + swap(sent, 2, 0, 0).astype(jnp.float32) * (1.0 / SUM_SCALE)
    sent = (sums[1] * SUM_SCALE).astype(jnp.float16)
    receiver_sums = sums[0] + swap(sent, 4, 0, 0).astype(jnp.float32) * (1.0 / SUM_SCALE)
    return (shot_sums, receiver_sums)


def solution(mesh):
    return jax.shard_map(
        per_device,
        mesh=mesh,
        in_specs=(P("tr", "fq"), P("tr"), P("tr"), P("tr"), P("tr", "fq"), P("tr", "fq")),
        out_specs=(P("tr", "fq"), P("tr", "fq")),
        check_vma=False,
    )
```

```python
import math

import jax
import jax.numpy as jnp
from jax import lax
from jax.experimental import pallas as pl
from jax.experimental.pallas import tpu as pltpu
from jax.sharding import PartitionSpec as P

NZ, NX, NC, NY = 8, 4, 2, 4
LA_TOP = 9.1
LA_SCALE = 65535.0 / LA_TOP
REC_LOW, REC_HIGH = 1.0, 2.2
REC_SCALE = 65535.0 / (REC_HIGH - REC_LOW)
SUM_SCALE = 1.0 / 32.0
PIECES = (1024, 1024)
LARGE = pltpu.CompilerParams(vmem_limit_bytes=60 * 2**20)
SUMS = pltpu.CompilerParams(vmem_limit_bytes=32 * 2**20)
SMALL = pltpu.CompilerParams(vmem_limit_bytes=12 * 2**20)
COST = pl.CostEstimate(flops=1000, bytes_accessed=1000, transcendentals=0)
MEDIUM = pltpu.CompilerParams(vmem_limit_bytes=18 * 2**20)


def tr_of(z, x, c):
    return (z * NX + x) * NC + c


def sites():
    return [(z, x, c) for z in range(NZ) for x in range(NX) for c in range(NC)]


def swap(value, dz, dx, dc):
    return lax.ppermute(value, "tr", [(tr_of(z, x, c), tr_of(z ^ dz, x ^ dx, c ^ dc)) for z, x, c in sites()])


def send_y(value, k):
    return lax.ppermute(value, "fq", [(i, (i + k) % NY) for i in range(NY)])


def make_table(samples, y, width, after):
    part, cols = samples // NY, NY * 2 * width
    tile = 128
    quarter = samples // 4
    shift = quarter.bit_length() - 1

    def body(y_ref, *refs):
        y, out = y_ref[0], refs[-1]
        row = pl.program_id(0) * tile
        time = (y - row // part) % NY * part + row % part + lax.broadcasted_iota(jnp.int32, (tile, 1), 0)
        for k in range(NY):
            first = (y + k) % NY * width
            for half in range(2):
                freq = first + lax.broadcasted_iota(jnp.int32, (1, width), 1)
                phase = (time * freq + half * quarter) & (samples - 1)
                turn = lax.shift_right_logical(phase + quarter // 2, shift)
                rest = (phase - turn * quarter).astype(jnp.float32) * (2.0 * math.pi / samples)
                sq = rest * rest
                cos = 1.0 + sq * (-0.5 + sq * (1 / 24 + sq * (-1 / 720 + sq * (1 / 40320 - sq * (1 / 3628800)))))
                sin = rest * (1.0 + sq * (-1 / 6 + sq * (1 / 120 + sq * (-1 / 5040 + sq * (1 / 362880)))))
                value = jnp.where((turn & 1) == 1, sin, cos)
                value = jnp.where(((turn + 1) & 2) == 2, -value, value)
                out[:, pl.ds((2 * k + half) * width, width)] = value.astype(jnp.bfloat16)

    return pl.pallas_call(
        body,
        grid=(samples // tile,),
        in_specs=[pl.BlockSpec(memory_space=pltpu.SMEM)] + [pl.BlockSpec(memory_space=pl.ANY)] * len(after),
        out_specs=pl.BlockSpec((tile, cols), lambda i: (i, 0)),
        out_shape=jax.ShapeDtypeStruct((samples, cols), jnp.bfloat16),
        compiler_params=SMALL,
        cost_estimate=pl.CostEstimate(flops=2**30, bytes_accessed=2**25, transcendentals=0),
        name="make_table",
    )(y[None], *after)


def join(parts, after=()):
    size = parts[0].shape[0]

    def body(*refs):
        out = refs[-1]
        for k in range(len(parts)):
            out[pl.ds(k * size, size), :] = refs[k][...]

    vm = pl.BlockSpec(memory_space=pltpu.VMEM)
    return pl.pallas_call(
        body,
        in_specs=[vm] * len(parts) + [pl.BlockSpec(memory_space=pl.ANY)] * len(after),
        out_specs=vm,
        out_shape=jax.ShapeDtypeStruct((size * len(parts),) + parts[0].shape[1:], parts[0].dtype),
        compiler_params=SMALL,
        cost_estimate=COST,
        name="join",
    )(*parts, *after)


def take_rows(traces, y, first, size, after=()):
    rows, part = traces.shape

    def body(y_ref, traces, *refs):
        outs, sems = refs[len(after) : len(after) + NY], refs[len(after) + NY :]
        copies = []
        for k in range(NY):
            at = pl.multiple_of((y_ref[0] + k) % NY * (rows // NY) + first, 16)
            copies.append(pltpu.make_async_copy(traces.at[pl.ds(at, size), :], outs[k], sems[k]))
        for copy in copies:
            copy.start()
        for copy in copies:
            copy.wait()

    hbm, vm = pl.BlockSpec(memory_space=pl.ANY), pl.BlockSpec(memory_space=pltpu.VMEM)
    return pl.pallas_call(
        body,
        in_specs=[pl.BlockSpec(memory_space=pltpu.SMEM), hbm] + [hbm] * len(after),
        out_specs=[vm] * NY,
        out_shape=[jax.ShapeDtypeStruct((size, part), traces.dtype)] * NY,
        scratch_shapes=[pltpu.SemaphoreType.DMA] * NY,
        compiler_params=SMALL,
        cost_estimate=COST,
        name="take_rows",
    )(y[None], traces, *after)


def encode_terms(terms, after):
    def body(a, *refs):
        b = refs[-1]
        code = jnp.clip((a[...] - REC_LOW) * REC_SCALE + 0.5, 0.0, 65535.0).astype(jnp.int32) - 32768
        b[...] = code.astype(jnp.int16)

    vm = pl.BlockSpec(memory_space=pltpu.VMEM)
    return pl.pallas_call(
        body,
        in_specs=[vm] + [pl.BlockSpec(memory_space=pl.ANY)] * len(after),
        out_specs=vm,
        out_shape=jax.ShapeDtypeStruct(terms.shape, jnp.int16),
        compiler_params=SMALL,
        cost_estimate=COST,
        name="encode_terms",
    )(terms, *after)


def spectra(blocks, table, width):
    rows, part = blocks[0].shape
    tile = 512

    def body(b0, b1, b2, b3, t, *outs):
        for k, out in enumerate(outs):
            cols = pl.ds(k * 2 * width, 2 * width)
            acc = None
            for j, b in enumerate((b0, b1, b2, b3)):
                one = jnp.dot(b[...], t[pl.ds(j * part, part), cols], preferred_element_type=jnp.float32)
                acc = one if acc is None else acc + one
            re, im = acc[:, :width], acc[:, width:]
            logamp = 0.5 * jnp.log(re * re + im * im + 1.0)
            code = jnp.minimum(logamp * LA_SCALE + 0.5, 65535.0).astype(jnp.int32) - 32768
            out[...] = code.astype(jnp.int16)

    return pl.pallas_call(
        body,
        grid=(rows // tile,),
        in_specs=[pl.BlockSpec((tile, part), lambda i: (i, 0))] * NY + [pl.BlockSpec(table.shape, lambda i: (0, 0))],
        out_specs=[pl.BlockSpec((tile, width), lambda i: (i, 0))] * NY,
        out_shape=[jax.ShapeDtypeStruct((rows, width), jnp.int16)] * NY,
        compiler_params=MEDIUM,
        cost_estimate=COST,
        name="spectra",
    )(*blocks, table)


def gather_shots(shot_near, shot_at, sizes):
    width = shot_near.shape[1]
    unroll = 64

    def body(shot_at, shot, *outs):
        for k, out in enumerate(outs):

            def step(b, _, out=out, first=sum(sizes[:k])):
                at = [b * unroll + u for u in range(unroll)]
                row = [shot[pl.ds(shot_at[first + i], 1), :] for i in at]
                for i, value in zip(at, row):
                    out[pl.ds(i, 1), :] = value
                return 0

            lax.fori_loop(0, sizes[k] // unroll, step, 0)

    vm, sm = pl.BlockSpec(memory_space=pltpu.VMEM), pl.BlockSpec(memory_space=pltpu.SMEM)
    return pl.pallas_call(
        body,
        in_specs=[sm, vm],
        out_specs=[vm] * len(sizes),
        out_shape=[jax.ShapeDtypeStruct((size, width), jnp.float32) for size in sizes],
        compiler_params=MEDIUM,
        cost_estimate=COST,
        name="gather_shots",
    )(shot_at, shot_near)


def sum_receivers(codes, shots, coded, live, rec_at, before):
    rows, width = shots.shape
    size, half = codes[0].shape[0], coded[0].shape[0]
    banks, unroll = 4, 32
    parts, held = len(codes), len(before)

    def body(*refs):
        rec_at, live, shots, own, other = refs[:5]
        codes, before = refs[5 : 5 + parts], refs[5 + parts : 5 + parts + held]
        near, far, res, rec = refs[5 + parts + held : 9 + parts + held]
        sums = refs[9 + parts + held :]
        halves = (pl.ds(0, half), pl.ds(half, half))
        for code, at in zip((own, other), halves):
            rec[at, :] = (code[...].astype(jnp.float32) + 32768.0) * (1.0 / REC_SCALE) + REC_LOW
        rec[pl.ds(2 * half, 8), :] = jnp.zeros((8, width), jnp.float32)
        for k, s in enumerate(sums):
            if k or not held:
                s[...] = jnp.zeros_like(s)
        for s, at in zip(before, halves):
            sums[0][at, :] = s[...]
        for k, code in enumerate(codes):
            at = pl.ds(k * size, size)
            logamp = (code[...].astype(jnp.float32) + 32768.0) * (1.0 / LA_SCALE)
            alive = lax.broadcasted_iota(jnp.int32, code.shape, 0) < live[k]
            res[at, :] = jnp.where(alive, logamp - shots[at, :], 0.0)

        def step(b, _):
            for u in range(unroll):
                s, row, at = sums[u % banks], pl.ds(b * unroll + u, 1), pl.ds(rec_at[b * unroll + u], 1)
                value = res[row, :] - rec[at, :]
                s[at, :] = s[at, :] + value
                res[row, :] = value
            return 0

        lax.fori_loop(0, rows // unroll, step, 0)
        for out, at in zip((near, far), halves):
            out[...] = (sums[0][at, :] + sums[1][at, :]) + (sums[2][at, :] + sums[3][at, :])

    vm, sm = pl.BlockSpec(memory_space=pltpu.VMEM), pl.BlockSpec(memory_space=pltpu.SMEM)
    sums = pltpu.VMEM((2 * half + 8, width), jnp.float32)
    return pl.pallas_call(
        body,
        in_specs=[sm, sm] + [vm] * (3 + parts + held),
        out_specs=[vm] * 3,
        out_shape=[jax.ShapeDtypeStruct((n, width), jnp.float32) for n in (half, half, rows)],
        scratch_shapes=[sums] * (1 + banks),
        compiler_params=SUMS,
        cost_estimate=COST,
        name="sum_receivers",
    )(rec_at, live, shots, *coded, *codes, *before)


def sum_shots(residuals, shot_at, count):
    width = residuals[0].shape[1]
    tile = 1024

    def body(shot_at, *refs):
        acc, first = jnp.zeros((count, 2 * width), jnp.float32), 0
        for res in refs[:-1]:
            for k in range(0, res.shape[0], tile):
                value = res[pl.ds(k, tile), :]
                high = value.astype(jnp.bfloat16)
                low = (value - high.astype(jnp.float32)).astype(jnp.bfloat16)
                both = jnp.concatenate([high, low], axis=1)
                hot = lax.broadcasted_iota(jnp.int32, (count, tile), 0) == shot_at[:, pl.ds(first + k, tile)]
                acc = acc + jnp.dot(hot.astype(jnp.bfloat16), both, preferred_element_type=jnp.float32)
            first += res.shape[0]
        refs[-1][...] = acc[:, :width] + acc[:, width:]

    vm = pl.BlockSpec(memory_space=pltpu.VMEM)
    return pl.pallas_call(
        body,
        in_specs=[vm] * (1 + len(residuals)),
        out_specs=vm,
        out_shape=jax.ShapeDtypeStruct((count, width), jnp.float32),
        compiler_params=MEDIUM,
        cost_estimate=COST,
        name="sum_shots",
    )(shot_at[None, :], *residuals)


def neighbour(value, by):
    size = NZ * NX * NC
    return lax.ppermute(value, "tr", [(i, i + by) for i in range(size) if 0 <= i + by < size])


def per_device(traces, shot_index, receiver_index, live_counts, shot_terms, receiver_terms):
    rows, part = traces.shape
    block, width = shot_terms.shape
    share = rows // NY
    first = [sum(PIECES[:h]) for h in range(len(PIECES))]
    owner, y = lax.axis_index("tr"), lax.axis_index("fq")
    z, x, c = owner // (NX * NC), owner // NC % NX, owner % NC

    got, after = [], ()
    for at, size in zip(first, PIECES):
        if after:
            mine = take_rows(traces, y, at, size, after)
        else:
            mine = [lax.dynamic_slice_in_dim(traces, (y + k) % NY * share + at, size, 0) for k in range(NY)]
        come = {k: send_y(mine[k], k) for k in (1, 3, 2)}
        after = [come[k] for k in range(1, NY)]
        got.append([mine[0]] + after)
    table = make_table(part * NY, y, width, got[0][:1])
    codes, coded = [], []
    for blocks in got:
        coded.append(spectra(blocks, table, width))
        codes += [send_y(coded[-1][k], k) if k else coded[-1][k] for k in range(NY)]

    def ordered(v):
        v = v.reshape(NY, share)
        v = jnp.stack([lax.dynamic_index_in_dim(v, (y - k) % NY, 0, keepdims=False) for k in range(NY)])
        return jnp.concatenate([v[:, at : at + size].reshape(NY * size) for at, size in zip(first, PIECES)])

    near = receiver_index // block
    rz, rx, rc = near // (NX * NC), near // NC % NX, near % NC
    turn = rz ^ z
    place = (((rc ^ c) * NX + (rx ^ x)) * 2 + (turn & 1)) * (NZ // 2) + turn // 2
    place = place * block + receiver_index % block
    spare = block * NZ * NX * NC
    rec_at = ordered(jnp.where(jnp.arange(rows, dtype=jnp.int32) < live_counts[0], place, spare))
    shot_at = ordered(shot_index - (owner - 1) * block)
    live = live_counts[0] - jnp.stack([(y - k) % NY * share + at for at in first for k in range(NY)])

    shot_terms = join([shot_terms], (table,))
    shot_near = jnp.concatenate([neighbour(shot_terms, 1), shot_terms, neighbour(shot_terms, -1)])
    terms = encode_terms(receiver_terms, (table,))
    terms = join([terms, swap(terms, 2, 0, 0)])
    terms = join([terms, swap(terms, 4, 0, 0)], got[0][1:] + [shot_near])
    terms = join([terms, swap(terms, 1, 0, 0)], got[1][:1])
    shots = gather_shots(shot_near, shot_at, [size * NY for size in PIECES])
    terms = join([terms, swap(terms, 0, 1, 0)], [coded[0][0]])
    terms = join([terms, swap(terms, 0, 2, 0)], [shots[0], rec_at] + got[1][1:])
    far_terms = swap(terms, 0, 0, 1)

    sums, residuals, done = (), [], 0
    for h, part_shots in enumerate(shots):
        some = slice(h * NY, (h + 1) * NY)
        at = rec_at[done : done + part_shots.shape[0]]
        done += part_shots.shape[0]
        *sums, resid = sum_receivers(codes[some], part_shots, [terms, far_terms], live[some], at, sums)
        residuals.append(resid)
    sums, far_sums = sums
    sums = (sums + swap(far_sums, 0, 0, 1)).reshape(NX, 2, NZ // 2, block, width)
    shots = sum_shots(residuals, shot_at, 3 * block)
    sent = (sums * SUM_SCALE).astype(jnp.float16)
    come = [swap(sent[k], 0, k, 0).astype(jnp.float32) for k in (1, 3, 2)]
    mine = join([sums[0].reshape(-1, width)], (shots,)).reshape(sums.shape[1:])
    sums = mine + (come[0] + come[1] + come[2]) * (1.0 / SUM_SCALE)
    shot_sums = shots[block : 2 * block] + neighbour(shots[2 * block :], 1) + neighbour(shots[:block], -1)
    sent = (sums[1] * SUM_SCALE).astype(jnp.float16)
    mine = join([sums[0].reshape(-1, width)], (shot_sums,)).reshape(sums.shape[1:])
    sums = mine + swap(sent, 1, 0, 0).astype(jnp.float32) * (1.0 / SUM_SCALE)
    sums = sums.reshape(2, 2, block, width)
    sent = (sums[:, 1] * SUM_SCALE).astype(jnp.float16)
    sums = sums[:, 0] + swap(sent, 2, 0, 0).astype(jnp.float32) * (1.0 / SUM_SCALE)
    sent = (sums[1] * SUM_SCALE).astype(jnp.float16)
    receiver_sums = sums[0] + swap(sent, 4, 0, 0).astype(jnp.float32) * (1.0 / SUM_SCALE)
    return (shot_sums, receiver_sums)


def solution(mesh):
    return jax.shard_map(
        per_device,
        mesh=mesh,
        in_specs=(P("tr", "fq"), P("tr"), P("tr"), P("tr"), P("tr", "fq"), P("tr", "fq")),
        out_specs=(P("tr", "fq"), P("tr", "fq")),
        check_vma=False,
    )
```

```python
import math

import jax
import jax.numpy as jnp
from jax import lax
from jax.experimental import pallas as pl
from jax.experimental.pallas import tpu as pltpu
from jax.sharding import PartitionSpec as P

NZ, NX, NC, NY = 8, 4, 2, 4
LA_TOP = 9.1
LA_SCALE = 65535.0 / LA_TOP
REC_LOW, REC_HIGH = 1.0, 2.2
REC_SCALE = 65535.0 / (REC_HIGH - REC_LOW)
SUM_SCALE = 1.0 / 32.0
PIECES = (1024, 1024)
SUMS = pltpu.CompilerParams(vmem_limit_bytes=32 * 2**20)
SMALL = pltpu.CompilerParams(vmem_limit_bytes=12 * 2**20)
COST = pl.CostEstimate(flops=1000, bytes_accessed=1000, transcendentals=0)


def tr_of(z, x, c):
    return (z * NX + x) * NC + c


def sites():
    return [(z, x, c) for z in range(NZ) for x in range(NX) for c in range(NC)]


def swap(value, dz, dx, dc):
    return lax.ppermute(value, "tr", [(tr_of(z, x, c), tr_of(z ^ dz, x ^ dx, c ^ dc)) for z, x, c in sites()])


def send_y(value, k):
    return lax.ppermute(value, "fq", [(i, (i + k) % NY) for i in range(NY)])


def make_table(samples, y, width, after):
    part, cols = samples // NY, NY * 2 * width
    tile = 128
    quarter = samples // 4
    shift = quarter.bit_length() - 1

    def body(y_ref, *refs):
        y, out = y_ref[0], refs[-1]
        row = pl.program_id(0) * tile
        time = (y - row // part) % NY * part + row % part + lax.broadcasted_iota(jnp.int32, (tile, 1), 0)
        for k in range(NY):
            first = (y + k) % NY * width
            for half in range(2):
                freq = first + lax.broadcasted_iota(jnp.int32, (1, width), 1)
                phase = (time * freq + half * quarter) & (samples - 1)
                turn = lax.shift_right_logical(phase + quarter // 2, shift)
                rest = (phase - turn * quarter).astype(jnp.float32) * (2.0 * math.pi / samples)
                sq = rest * rest
                cos = 1.0 + sq * (-0.5 + sq * (1 / 24 + sq * (-1 / 720 + sq * (1 / 40320 - sq * (1 / 3628800)))))
                sin = rest * (1.0 + sq * (-1 / 6 + sq * (1 / 120 + sq * (-1 / 5040 + sq * (1 / 362880)))))
                value = jnp.where((turn & 1) == 1, sin, cos)
                value = jnp.where(((turn + 1) & 2) == 2, -value, value)
                out[:, pl.ds((2 * k + half) * width, width)] = value.astype(jnp.bfloat16)

    return pl.pallas_call(
        body,
        grid=(samples // tile,),
        in_specs=[pl.BlockSpec(memory_space=pltpu.SMEM)] + [pl.BlockSpec(memory_space=pl.ANY)] * len(after),
        out_specs=pl.BlockSpec((tile, cols), lambda i: (i, 0)),
        out_shape=jax.ShapeDtypeStruct((samples, cols), jnp.bfloat16),
        compiler_params=SMALL,
        cost_estimate=pl.CostEstimate(flops=2**30, bytes_accessed=2**25, transcendentals=0),
        name="make_table",
    )(y[None], *after)


def join(parts, after=()):
    size = parts[0].shape[0]

    def body(*refs):
        out = refs[-1]
        for k in range(len(parts)):
            out[pl.ds(k * size, size), :] = refs[k][...]

    vm = pl.BlockSpec(memory_space=pltpu.VMEM)
    return pl.pallas_call(
        body,
        in_specs=[vm] * len(parts) + [pl.BlockSpec(memory_space=pl.ANY)] * len(after),
        out_specs=vm,
        out_shape=jax.ShapeDtypeStruct((size * len(parts),) + parts[0].shape[1:], parts[0].dtype),
        compiler_params=SMALL,
        cost_estimate=COST,
        name="join",
    )(*parts, *after)


def encode_terms(terms, after):
    def body(a, *refs):
        b = refs[-1]
        code = jnp.clip((a[...] - REC_LOW) * REC_SCALE + 0.5, 0.0, 65535.0).astype(jnp.int32) - 32768
        b[...] = code.astype(jnp.int16)

    vm = pl.BlockSpec(memory_space=pltpu.VMEM)
    return pl.pallas_call(
        body,
        in_specs=[vm] + [pl.BlockSpec(memory_space=pl.ANY)] * len(after),
        out_specs=vm,
        out_shape=jax.ShapeDtypeStruct(terms.shape, jnp.int16),
        compiler_params=SMALL,
        cost_estimate=COST,
        name="encode_terms",
    )(terms, *after)


def spectra(blocks, table, width):
    rows, part = blocks[0].shape
    tile = 512

    def body(b0, b1, b2, b3, t, *outs):
        for k, out in enumerate(outs):
            cols = pl.ds(k * 2 * width, 2 * width)
            acc = None
            for j, b in enumerate((b0, b1, b2, b3)):
                one = jnp.dot(b[...], t[pl.ds(j * part, part), cols], preferred_element_type=jnp.float32)
                acc = one if acc is None else acc + one
            re, im = acc[:, :width], acc[:, width:]
            logamp = 0.5 * jnp.log(re * re + im * im + 1.0)
            code = jnp.minimum(logamp * LA_SCALE + 0.5, 65535.0).astype(jnp.int32) - 32768
            out[...] = code.astype(jnp.int16)

    return pl.pallas_call(
        body,
        grid=(rows // tile,),
        in_specs=[pl.BlockSpec((tile, part), lambda i: (i, 0))] * NY + [pl.BlockSpec(table.shape, lambda i: (0, 0))],
        out_specs=[pl.BlockSpec((tile, width), lambda i: (i, 0))] * NY,
        out_shape=[jax.ShapeDtypeStruct((rows, width), jnp.int16)] * NY,
        compiler_params=SMALL,
        cost_estimate=COST,
        name="spectra",
    )(*blocks, table)


def gather_shots(shot_near, shot_at, sizes):
    width = shot_near.shape[1]
    unroll = 64

    def body(shot_at, shot, *outs):
        for k, out in enumerate(outs):

            def step(b, _, out=out, first=sum(sizes[:k])):
                at = [b * unroll + u for u in range(unroll)]
                row = [shot[pl.ds(shot_at[first + i], 1), :] for i in at]
                for i, value in zip(at, row):
                    out[pl.ds(i, 1), :] = value
                return 0

            lax.fori_loop(0, sizes[k] // unroll, step, 0)

    vm, sm = pl.BlockSpec(memory_space=pltpu.VMEM), pl.BlockSpec(memory_space=pltpu.SMEM)
    return pl.pallas_call(
        body,
        in_specs=[sm, vm],
        out_specs=[vm] * len(sizes),
        out_shape=[jax.ShapeDtypeStruct((size, width), jnp.float32) for size in sizes],
        compiler_params=SMALL,
        cost_estimate=COST,
        name="gather_shots",
    )(shot_at, shot_near)


def sum_receivers(codes, shots, coded, live, rec_at, before):
    rows, width = shots.shape
    size, half = codes[0].shape[0], coded[0].shape[0]
    banks, unroll = 4, 32
    parts, held = len(codes), len(before)

    def body(*refs):
        rec_at, live, shots, own, other = refs[:5]
        codes, before = refs[5 : 5 + parts], refs[5 + parts : 5 + parts + held]
        near, far, res, rec = refs[5 + parts + held : 9 + parts + held]
        sums = refs[9 + parts + held :]
        halves = (pl.ds(0, half), pl.ds(half, half))
        for code, at in zip((own, other), halves):
            rec[at, :] = (code[...].astype(jnp.float32) + 32768.0) * (1.0 / REC_SCALE) + REC_LOW
        rec[pl.ds(2 * half, 8), :] = jnp.zeros((8, width), jnp.float32)
        for k, s in enumerate(sums):
            if k or not held:
                s[...] = jnp.zeros_like(s)
        for s, at in zip(before, halves):
            sums[0][at, :] = s[...]
        for k, code in enumerate(codes):
            at = pl.ds(k * size, size)
            logamp = (code[...].astype(jnp.float32) + 32768.0) * (1.0 / LA_SCALE)
            alive = lax.broadcasted_iota(jnp.int32, code.shape, 0) < live[k]
            res[at, :] = jnp.where(alive, logamp - shots[at, :], 0.0)

        def step(b, _):
            for u in range(unroll):
                s, row, at = sums[u % banks], pl.ds(b * unroll + u, 1), pl.ds(rec_at[b * unroll + u], 1)
                value = res[row, :] - rec[at, :]
                s[at, :] = s[at, :] + value
                res[row, :] = value
            return 0

        lax.fori_loop(0, rows // unroll, step, 0)
        for out, at in zip((near, far), halves):
            out[...] = (sums[0][at, :] + sums[1][at, :]) + (sums[2][at, :] + sums[3][at, :])

    vm, sm = pl.BlockSpec(memory_space=pltpu.VMEM), pl.BlockSpec(memory_space=pltpu.SMEM)
    sums = pltpu.VMEM((2 * half + 8, width), jnp.float32)
    return pl.pallas_call(
        body,
        in_specs=[sm, sm] + [vm] * (3 + parts + held),
        out_specs=[vm] * 3,
        out_shape=[jax.ShapeDtypeStruct((n, width), jnp.float32) for n in (half, half, rows)],
        scratch_shapes=[sums] * (1 + banks),
        compiler_params=SUMS,
        cost_estimate=COST,
        name="sum_receivers",
    )(rec_at, live, shots, *coded, *codes, *before)


def sum_shots(residuals, shot_at, count):
    width = residuals[0].shape[1]
    tile = 1024

    def body(shot_at, *refs):
        acc, first = jnp.zeros((count, 2 * width), jnp.float32), 0
        for res in refs[:-1]:
            for k in range(0, res.shape[0], tile):
                value = res[pl.ds(k, tile), :]
                high = value.astype(jnp.bfloat16)
                low = (value - high.astype(jnp.float32)).astype(jnp.bfloat16)
                both = jnp.concatenate([high, low], axis=1)
                hot = lax.broadcasted_iota(jnp.int32, (count, tile), 0) == shot_at[:, pl.ds(first + k, tile)]
                acc = acc + jnp.dot(hot.astype(jnp.bfloat16), both, preferred_element_type=jnp.float32)
            first += res.shape[0]
        refs[-1][...] = acc[:, :width] + acc[:, width:]

    vm = pl.BlockSpec(memory_space=pltpu.VMEM)
    return pl.pallas_call(
        body,
        in_specs=[vm] * (1 + len(residuals)),
        out_specs=vm,
        out_shape=jax.ShapeDtypeStruct((count, width), jnp.float32),
        compiler_params=SMALL,
        cost_estimate=COST,
        name="sum_shots",
    )(shot_at[None, :], *residuals)


def neighbour(value, by):
    size = NZ * NX * NC
    return lax.ppermute(value, "tr", [(i, i + by) for i in range(size) if 0 <= i + by < size])


def per_device(traces, shot_index, receiver_index, live_counts, shot_terms, receiver_terms):
    rows, part = traces.shape
    block, width = shot_terms.shape
    share = rows // NY
    first = [sum(PIECES[:h]) for h in range(len(PIECES))]
    owner, y = lax.axis_index("tr"), lax.axis_index("fq")
    z, x, c = owner // (NX * NC), owner // NC % NX, owner % NC

    got = []
    for at, size in zip(first, PIECES):
        mine = [lax.dynamic_slice_in_dim(traces, (y + k) % NY * share + at, size, 0) for k in range(NY)]
        come = {k: send_y(mine[k], k) for k in (1, 3, 2)}
        got.append([mine[0]] + [come[k] for k in range(1, NY)])
    table = make_table(part * NY, y, width, got[0][:1])
    codes, coded = [], []
    for blocks in got:
        coded.append(spectra(blocks, table, width))
        codes += [send_y(coded[-1][k], k) if k else coded[-1][k] for k in range(NY)]

    def ordered(v):
        v = v.reshape(NY, share)
        v = jnp.stack([lax.dynamic_index_in_dim(v, (y - k) % NY, 0, keepdims=False) for k in range(NY)])
        return jnp.concatenate([v[:, at : at + size].reshape(NY * size) for at, size in zip(first, PIECES)])

    near = receiver_index // block
    rz, rx, rc = near // (NX * NC), near // NC % NX, near % NC
    turn = rz ^ z
    place = (((rc ^ c) * NX + (rx ^ x)) * 2 + (turn & 1)) * (NZ // 2) + turn // 2
    place = place * block + receiver_index % block
    spare = block * NZ * NX * NC
    rec_at = ordered(jnp.where(jnp.arange(rows, dtype=jnp.int32) < live_counts[0], place, spare))
    shot_at = ordered(shot_index - (owner - 1) * block)
    live = live_counts[0] - jnp.stack([(y - k) % NY * share + at for at in first for k in range(NY)])

    shot_terms = join([shot_terms], (table,))
    shot_near = jnp.concatenate([neighbour(shot_terms, 1), shot_terms, neighbour(shot_terms, -1)])
    terms = encode_terms(receiver_terms, (table,))
    terms = join([terms, swap(terms, 2, 0, 0)])
    terms = join([terms, swap(terms, 4, 0, 0)], got[0][1:] + [shot_near])
    terms = join([terms, swap(terms, 1, 0, 0)])
    shots = gather_shots(shot_near, shot_at, [size * NY for size in PIECES])
    terms = join([terms, swap(terms, 0, 1, 0)], [coded[0][0]])
    terms = join([terms, swap(terms, 0, 2, 0)], [shots[0], rec_at] + got[1][1:])
    far_terms = swap(terms, 0, 0, 1)

    sums, residuals, done = (), [], 0
    for h, part_shots in enumerate(shots):
        some = slice(h * NY, (h + 1) * NY)
        at = rec_at[done : done + part_shots.shape[0]]
        done += part_shots.shape[0]
        *sums, resid = sum_receivers(codes[some], part_shots, [terms, far_terms], live[some], at, sums)
        residuals.append(resid)
    sums, far_sums = sums
    sums = (sums + swap(far_sums, 0, 0, 1)).reshape(NX, 2, NZ // 2, block, width)
    shots = sum_shots(residuals, shot_at, 3 * block)
    sent = (sums * SUM_SCALE).astype(jnp.float16)
    come = [swap(sent[k], 0, k, 0).astype(jnp.float32) for k in (1, 3, 2)]
    mine = join([sums[0].reshape(-1, width)], (shots,)).reshape(sums.shape[1:])
    sums = mine + (come[0] + come[1] + come[2]) * (1.0 / SUM_SCALE)
    shot_sums = shots[block : 2 * block] + neighbour(shots[2 * block :], 1) + neighbour(shots[:block], -1)
    sent = (sums[1] * SUM_SCALE).astype(jnp.float16)
    mine = join([sums[0].reshape(-1, width)], (shot_sums,)).reshape(sums.shape[1:])
    sums = mine + swap(sent, 1, 0, 0).astype(jnp.float32) * (1.0 / SUM_SCALE)
    sums = sums.reshape(2, 2, block, width)
    sent = (sums[:, 1] * SUM_SCALE).astype(jnp.float16)
    sums = sums[:, 0] + swap(sent, 2, 0, 0).astype(jnp.float32) * (1.0 / SUM_SCALE)
    sent = (sums[1] * SUM_SCALE).astype(jnp.float16)
    receiver_sums = sums[0] + swap(sent, 4, 0, 0).astype(jnp.float32) * (1.0 / SUM_SCALE)
    return (shot_sums, receiver_sums)


def solution(mesh):
    return jax.shard_map(
        per_device,
        mesh=mesh,
        in_specs=(P("tr", "fq"), P("tr"), P("tr"), P("tr"), P("tr", "fq"), P("tr", "fq")),
        out_specs=(P("tr", "fq"), P("tr", "fq")),
        check_vma=False,
    )
```

```python
import math

import jax
import jax.numpy as jnp
from jax import lax
from jax.experimental import pallas as pl
from jax.experimental.pallas import tpu as pltpu
from jax.sharding import PartitionSpec as P

NZ, NX, NC, NY = 8, 4, 2, 4
LA_TOP = 9.1
LA_SCALE = 65535.0 / LA_TOP
REC_LOW, REC_HIGH = 1.0, 2.2
REC_SCALE = 65535.0 / (REC_HIGH - REC_LOW)
SUM_SCALE = 1.0 / 32.0
PIECES = (1024, 1024)
SUMS = pltpu.CompilerParams(vmem_limit_bytes=32 * 2**20)
SMALL = pltpu.CompilerParams(vmem_limit_bytes=12 * 2**20)
COST = pl.CostEstimate(flops=1000, bytes_accessed=1000, transcendentals=0)


def tr_of(z, x, c):
    return (z * NX + x) * NC + c


def sites():
    return [(z, x, c) for z in range(NZ) for x in range(NX) for c in range(NC)]


def swap(value, dz, dx, dc):
    return lax.ppermute(value, "tr", [(tr_of(z, x, c), tr_of(z ^ dz, x ^ dx, c ^ dc)) for z, x, c in sites()])


def send_y(value, k):
    return lax.ppermute(value, "fq", [(i, (i + k) % NY) for i in range(NY)])


def make_table(samples, y, width, after):
    part, cols = samples // NY, NY * 2 * width
    tile = 128
    quarter = samples // 4
    shift = quarter.bit_length() - 1

    def body(y_ref, *refs):
        y, out = y_ref[0], refs[-1]
        row = pl.program_id(0) * tile
        time = (y - row // part) % NY * part + row % part + lax.broadcasted_iota(jnp.int32, (tile, 1), 0)
        for k in range(NY):
            first = (y + k) % NY * width
            for half in range(2):
                freq = first + lax.broadcasted_iota(jnp.int32, (1, width), 1)
                phase = (time * freq + half * quarter) & (samples - 1)
                turn = lax.shift_right_logical(phase + quarter // 2, shift)
                rest = (phase - turn * quarter).astype(jnp.float32) * (2.0 * math.pi / samples)
                sq = rest * rest
                cos = 1.0 + sq * (-0.5 + sq * (1 / 24 + sq * (-1 / 720 + sq * (1 / 40320 - sq * (1 / 3628800)))))
                sin = rest * (1.0 + sq * (-1 / 6 + sq * (1 / 120 + sq * (-1 / 5040 + sq * (1 / 362880)))))
                value = jnp.where((turn & 1) == 1, sin, cos)
                value = jnp.where(((turn + 1) & 2) == 2, -value, value)
                out[:, pl.ds((2 * k + half) * width, width)] = value.astype(jnp.bfloat16)

    return pl.pallas_call(
        body,
        grid=(samples // tile,),
        in_specs=[pl.BlockSpec(memory_space=pltpu.SMEM)] + [pl.BlockSpec(memory_space=pl.ANY)] * len(after),
        out_specs=pl.BlockSpec((tile, cols), lambda i: (i, 0)),
        out_shape=jax.ShapeDtypeStruct((samples, cols), jnp.bfloat16),
        compiler_params=SMALL,
        cost_estimate=pl.CostEstimate(flops=2**30, bytes_accessed=2**25, transcendentals=0),
        name="make_table",
    )(y[None], *after)


def join(parts, after=()):
    size = parts[0].shape[0]

    def body(*refs):
        out = refs[-1]
        for k in range(len(parts)):
            out[pl.ds(k * size, size), :] = refs[k][...]

    vm = pl.BlockSpec(memory_space=pltpu.VMEM)
    return pl.pallas_call(
        body,
        in_specs=[vm] * len(parts) + [pl.BlockSpec(memory_space=pl.ANY)] * len(after),
        out_specs=vm,
        out_shape=jax.ShapeDtypeStruct((size * len(parts),) + parts[0].shape[1:], parts[0].dtype),
        compiler_params=SMALL,
        cost_estimate=COST,
        name="join",
    )(*parts, *after)


def tie(values, after):
    hbm = pl.BlockSpec(memory_space=pl.ANY)
    return pl.pallas_call(
        lambda *refs: None,
        in_specs=[hbm] * (len(values) + len(after)),
        out_specs=[hbm] * len(values),
        out_shape=[jax.ShapeDtypeStruct(value.shape, value.dtype) for value in values],
        input_output_aliases={k: k for k in range(len(values))},
        compiler_params=SMALL,
        cost_estimate=COST,
        name="tie",
    )(*values, *after)


def encode_terms(terms, after):
    def body(a, *refs):
        b = refs[-1]
        code = jnp.clip((a[...] - REC_LOW) * REC_SCALE + 0.5, 0.0, 65535.0).astype(jnp.int32) - 32768
        b[...] = code.astype(jnp.int16)

    vm = pl.BlockSpec(memory_space=pltpu.VMEM)
    return pl.pallas_call(
        body,
        in_specs=[vm] + [pl.BlockSpec(memory_space=pl.ANY)] * len(after),
        out_specs=vm,
        out_shape=jax.ShapeDtypeStruct(terms.shape, jnp.int16),
        compiler_params=SMALL,
        cost_estimate=COST,
        name="encode_terms",
    )(terms, *after)


def spectra(blocks, table, width):
    rows, part = blocks[0].shape
    tile = 512

    def body(b0, b1, b2, b3, t, *outs):
        for k, out in enumerate(outs):
            cols = pl.ds(k * 2 * width, 2 * width)
            acc = None
            for j, b in enumerate((b0, b1, b2, b3)):
                one = jnp.dot(b[...], t[pl.ds(j * part, part), cols], preferred_element_type=jnp.float32)
                acc = one if acc is None else acc + one
            re, im = acc[:, :width], acc[:, width:]
            logamp = 0.5 * jnp.log(re * re + im * im + 1.0)
            code = jnp.minimum(logamp * LA_SCALE + 0.5, 65535.0).astype(jnp.int32) - 32768
            out[...] = code.astype(jnp.int16)

    return pl.pallas_call(
        body,
        grid=(rows // tile,),
        in_specs=[pl.BlockSpec((tile, part), lambda i: (i, 0))] * NY + [pl.BlockSpec(table.shape, lambda i: (0, 0))],
        out_specs=[pl.BlockSpec((tile, width), lambda i: (i, 0))] * NY,
        out_shape=[jax.ShapeDtypeStruct((rows, width), jnp.int16)] * NY,
        compiler_params=SMALL,
        cost_estimate=COST,
        name="spectra",
    )(*blocks, table)


def gather_shots(shot_near, shot_at, sizes):
    width = shot_near.shape[1]
    unroll = 64

    def body(shot_at, shot, *outs):
        for k, out in enumerate(outs):

            def step(b, _, out=out, first=sum(sizes[:k])):
                at = [b * unroll + u for u in range(unroll)]
                row = [shot[pl.ds(shot_at[first + i], 1), :] for i in at]
                for i, value in zip(at, row):
                    out[pl.ds(i, 1), :] = value
                return 0

            lax.fori_loop(0, sizes[k] // unroll, step, 0)

    vm, sm = pl.BlockSpec(memory_space=pltpu.VMEM), pl.BlockSpec(memory_space=pltpu.SMEM)
    return pl.pallas_call(
        body,
        in_specs=[sm, vm],
        out_specs=[vm] * len(sizes),
        out_shape=[jax.ShapeDtypeStruct((size, width), jnp.float32) for size in sizes],
        compiler_params=SMALL,
        cost_estimate=COST,
        name="gather_shots",
    )(shot_at, shot_near)


def sum_receivers(codes, shots, coded, live, rec_at, before):
    rows, width = shots.shape
    size, half = codes[0].shape[0], coded[0].shape[0]
    banks, unroll = 4, 32
    parts, held = len(codes), len(before)

    def body(*refs):
        rec_at, live, shots, own, other = refs[:5]
        codes, before = refs[5 : 5 + parts], refs[5 + parts : 5 + parts + held]
        near, far, res, rec = refs[5 + parts + held : 9 + parts + held]
        sums = refs[9 + parts + held :]
        halves = (pl.ds(0, half), pl.ds(half, half))
        for code, at in zip((own, other), halves):
            rec[at, :] = (code[...].astype(jnp.float32) + 32768.0) * (1.0 / REC_SCALE) + REC_LOW
        rec[pl.ds(2 * half, 8), :] = jnp.zeros((8, width), jnp.float32)
        for k, s in enumerate(sums):
            if k or not held:
                s[...] = jnp.zeros_like(s)
        for s, at in zip(before, halves):
            sums[0][at, :] = s[...]
        for k, code in enumerate(codes):
            at = pl.ds(k * size, size)
            logamp = (code[...].astype(jnp.float32) + 32768.0) * (1.0 / LA_SCALE)
            alive = lax.broadcasted_iota(jnp.int32, code.shape, 0) < live[k]
            res[at, :] = jnp.where(alive, logamp - shots[at, :], 0.0)

        def step(b, _):
            for u in range(unroll):
                s, row, at = sums[u % banks], pl.ds(b * unroll + u, 1), pl.ds(rec_at[b * unroll + u], 1)
                value = res[row, :] - rec[at, :]
                s[at, :] = s[at, :] + value
                res[row, :] = value
            return 0

        lax.fori_loop(0, rows // unroll, step, 0)
        for out, at in zip((near, far), halves):
            out[...] = (sums[0][at, :] + sums[1][at, :]) + (sums[2][at, :] + sums[3][at, :])

    vm, sm = pl.BlockSpec(memory_space=pltpu.VMEM), pl.BlockSpec(memory_space=pltpu.SMEM)
    sums = pltpu.VMEM((2 * half + 8, width), jnp.float32)
    return pl.pallas_call(
        body,
        in_specs=[sm, sm] + [vm] * (3 + parts + held),
        out_specs=[vm] * 3,
        out_shape=[jax.ShapeDtypeStruct((n, width), jnp.float32) for n in (half, half, rows)],
        scratch_shapes=[sums] * (1 + banks),
        compiler_params=SUMS,
        cost_estimate=COST,
        name="sum_receivers",
    )(rec_at, live, shots, *coded, *codes, *before)


def sum_shots(residuals, shot_at, count):
    width = residuals[0].shape[1]
    tile = 1024

    def body(shot_at, *refs):
        acc, first = jnp.zeros((count, 2 * width), jnp.float32), 0
        for res in refs[:-1]:
            for k in range(0, res.shape[0], tile):
                value = res[pl.ds(k, tile), :]
                high = value.astype(jnp.bfloat16)
                low = (value - high.astype(jnp.float32)).astype(jnp.bfloat16)
                both = jnp.concatenate([high, low], axis=1)
                hot = lax.broadcasted_iota(jnp.int32, (count, tile), 0) == shot_at[:, pl.ds(first + k, tile)]
                acc = acc + jnp.dot(hot.astype(jnp.bfloat16), both, preferred_element_type=jnp.float32)
            first += res.shape[0]
        refs[-1][...] = acc[:, :width] + acc[:, width:]

    vm = pl.BlockSpec(memory_space=pltpu.VMEM)
    return pl.pallas_call(
        body,
        in_specs=[vm] * (1 + len(residuals)),
        out_specs=vm,
        out_shape=jax.ShapeDtypeStruct((count, width), jnp.float32),
        compiler_params=SMALL,
        cost_estimate=COST,
        name="sum_shots",
    )(shot_at[None, :], *residuals)


def neighbour(value, by):
    size = NZ * NX * NC
    return lax.ppermute(value, "tr", [(i, i + by) for i in range(size) if 0 <= i + by < size])


def per_device(traces, shot_index, receiver_index, live_counts, shot_terms, receiver_terms):
    rows, part = traces.shape
    block, width = shot_terms.shape
    share = rows // NY
    first = [sum(PIECES[:h]) for h in range(len(PIECES))]
    owner, y = lax.axis_index("tr"), lax.axis_index("fq")
    z, x, c = owner // (NX * NC), owner // NC % NX, owner % NC

    got = []
    for at, size in zip(first, PIECES):
        mine = [lax.dynamic_slice_in_dim(traces, (y + k) % NY * share + at, size, 0) for k in range(NY)]
        if got:
            mine[1:] = tie(mine[1:], got[0][1:])
        come = {k: send_y(mine[k], k) for k in (1, 3, 2)}
        got.append([mine[0]] + [come[k] for k in range(1, NY)])
    table = make_table(part * NY, y, width, got[0][:1])
    codes, coded = [], []
    for blocks in got:
        coded.append(spectra(blocks, table, width))
        codes += [send_y(coded[-1][k], k) if k else coded[-1][k] for k in range(NY)]

    def ordered(v):
        v = v.reshape(NY, share)
        v = jnp.stack([lax.dynamic_index_in_dim(v, (y - k) % NY, 0, keepdims=False) for k in range(NY)])
        return jnp.concatenate([v[:, at : at + size].reshape(NY * size) for at, size in zip(first, PIECES)])

    near = receiver_index // block
    rz, rx, rc = near // (NX * NC), near // NC % NX, near % NC
    turn = rz ^ z
    place = (((rc ^ c) * NX + (rx ^ x)) * 2 + (turn & 1)) * (NZ // 2) + turn // 2
    place = place * block + receiver_index % block
    spare = block * NZ * NX * NC
    rec_at = ordered(jnp.where(jnp.arange(rows, dtype=jnp.int32) < live_counts[0], place, spare))
    shot_at = ordered(shot_index - (owner - 1) * block)
    live = live_counts[0] - jnp.stack([(y - k) % NY * share + at for at in first for k in range(NY)])

    shot_terms = join([shot_terms], (table,))
    shot_near = jnp.concatenate([neighbour(shot_terms, 1), shot_terms, neighbour(shot_terms, -1)])
    terms = encode_terms(receiver_terms, (table,))
    terms = join([terms, swap(terms, 2, 0, 0)])
    terms = join([terms, swap(terms, 4, 0, 0)], got[0][1:] + [shot_near])
    terms = join([terms, swap(terms, 1, 0, 0)])
    shots = gather_shots(shot_near, shot_at, [size * NY for size in PIECES])
    terms = join([terms, swap(terms, 0, 1, 0)], [coded[0][0], shots[0], rec_at] + got[1][1:])
    terms = join([terms, swap(terms, 0, 2, 0)], [coded[1][0]] + codes[1:NY])
    far_terms = swap(terms, 0, 0, 1)

    sums, residuals, done = (), [], 0
    for h, part_shots in enumerate(shots):
        some = slice(h * NY, (h + 1) * NY)
        at = rec_at[done : done + part_shots.shape[0]]
        done += part_shots.shape[0]
        *sums, resid = sum_receivers(codes[some], part_shots, [terms, far_terms], live[some], at, sums)
        residuals.append(resid)
    sums, far_sums = sums
    sums = (sums + swap(far_sums, 0, 0, 1)).reshape(NX, 2, NZ // 2, block, width)
    shots = sum_shots(residuals, shot_at, 3 * block)
    sent = (sums * SUM_SCALE).astype(jnp.float16)
    come = [swap(sent[k], 0, k, 0).astype(jnp.float32) for k in (1, 3, 2)]
    mine = join([sums[0].reshape(-1, width)], (shots,)).reshape(sums.shape[1:])
    sums = mine + (come[0] + come[1] + come[2]) * (1.0 / SUM_SCALE)
    shot_sums = shots[block : 2 * block] + neighbour(shots[2 * block :], 1) + neighbour(shots[:block], -1)
    sent = (sums[1] * SUM_SCALE).astype(jnp.float16)
    mine = join([sums[0].reshape(-1, width)], (shot_sums,)).reshape(sums.shape[1:])
    sums = mine + swap(sent, 1, 0, 0).astype(jnp.float32) * (1.0 / SUM_SCALE)
    sums = sums.reshape(2, 2, block, width)
    sent = (sums[:, 1] * SUM_SCALE).astype(jnp.float16)
    sums = sums[:, 0] + swap(sent, 2, 0, 0).astype(jnp.float32) * (1.0 / SUM_SCALE)
    sent = (sums[1] * SUM_SCALE).astype(jnp.float16)
    receiver_sums = sums[0] + swap(sent, 4, 0, 0).astype(jnp.float32) * (1.0 / SUM_SCALE)
    return (shot_sums, receiver_sums)


def solution(mesh):
    return jax.shard_map(
        per_device,
        mesh=mesh,
        in_specs=(P("tr", "fq"), P("tr"), P("tr"), P("tr"), P("tr", "fq"), P("tr", "fq")),
        out_specs=(P("tr", "fq"), P("tr", "fq")),
        check_vma=False,
    )
```

```python
import math

import jax
import jax.numpy as jnp
from jax import lax
from jax.experimental import pallas as pl
from jax.experimental.pallas import tpu as pltpu
from jax.sharding import PartitionSpec as P

NZ, NX, NC, NY = 8, 4, 2, 4
LA_TOP = 9.1
LA_SCALE = 65535.0 / LA_TOP
REC_LOW, REC_HIGH = 1.0, 2.2
REC_SCALE = 65535.0 / (REC_HIGH - REC_LOW)
SUM_SCALE = 1.0 / 32.0
PIECES = (1024, 1024)
SUMS = pltpu.CompilerParams(vmem_limit_bytes=24 * 2**20)
SMALL = pltpu.CompilerParams(vmem_limit_bytes=12 * 2**20)
COST = pl.CostEstimate(flops=1000, bytes_accessed=1000, transcendentals=0)


def tr_of(z, x, c):
    return (z * NX + x) * NC + c


def sites():
    return [(z, x, c) for z in range(NZ) for x in range(NX) for c in range(NC)]


def swap(value, dz, dx, dc):
    return lax.ppermute(value, "tr", [(tr_of(z, x, c), tr_of(z ^ dz, x ^ dx, c ^ dc)) for z, x, c in sites()])


def send_y(value, k):
    return lax.ppermute(value, "fq", [(i, (i + k) % NY) for i in range(NY)])


def make_table(samples, y, width, after):
    part, cols = samples // NY, NY * 2 * width
    tile = 128
    quarter = samples // 4
    shift = quarter.bit_length() - 1

    def body(y_ref, *refs):
        y, out = y_ref[0], refs[-1]
        row = pl.program_id(0) * tile
        time = (y - row // part) % NY * part + row % part + lax.broadcasted_iota(jnp.int32, (tile, 1), 0)
        for k in range(NY):
            first = (y + k) % NY * width
            for half in range(2):
                freq = first + lax.broadcasted_iota(jnp.int32, (1, width), 1)
                phase = (time * freq + half * quarter) & (samples - 1)
                turn = lax.shift_right_logical(phase + quarter // 2, shift)
                rest = (phase - turn * quarter).astype(jnp.float32) * (2.0 * math.pi / samples)
                sq = rest * rest
                cos = 1.0 + sq * (-0.5 + sq * (1 / 24 + sq * (-1 / 720 + sq * (1 / 40320 - sq * (1 / 3628800)))))
                sin = rest * (1.0 + sq * (-1 / 6 + sq * (1 / 120 + sq * (-1 / 5040 + sq * (1 / 362880)))))
                value = jnp.where((turn & 1) == 1, sin, cos)
                value = jnp.where(((turn + 1) & 2) == 2, -value, value)
                out[:, pl.ds((2 * k + half) * width, width)] = value.astype(jnp.bfloat16)

    return pl.pallas_call(
        body,
        grid=(samples // tile,),
        in_specs=[pl.BlockSpec(memory_space=pltpu.SMEM)] + [pl.BlockSpec(memory_space=pl.ANY)] * len(after),
        out_specs=pl.BlockSpec((tile, cols), lambda i: (i, 0)),
        out_shape=jax.ShapeDtypeStruct((samples, cols), jnp.bfloat16),
        compiler_params=SMALL,
        cost_estimate=pl.CostEstimate(flops=2**30, bytes_accessed=2**25, transcendentals=0),
        name="make_table",
    )(y[None], *after)


def join(parts, after=()):
    size = parts[0].shape[0]

    def body(*refs):
        out = refs[-1]
        for k in range(len(parts)):
            out[pl.ds(k * size, size), :] = refs[k][...]

    vm = pl.BlockSpec(memory_space=pltpu.VMEM)
    return pl.pallas_call(
        body,
        in_specs=[vm] * len(parts) + [pl.BlockSpec(memory_space=pl.ANY)] * len(after),
        out_specs=vm,
        out_shape=jax.ShapeDtypeStruct((size * len(parts),) + parts[0].shape[1:], parts[0].dtype),
        compiler_params=SMALL,
        cost_estimate=COST,
        name="join",
    )(*parts, *after)


def tie(values, after):
    hbm = pl.BlockSpec(memory_space=pl.ANY)
    return pl.pallas_call(
        lambda *refs: None,
        in_specs=[hbm] * (len(values) + len(after)),
        out_specs=[hbm] * len(values),
        out_shape=[jax.ShapeDtypeStruct(value.shape, value.dtype) for value in values],
        input_output_aliases={k: k for k in range(len(values))},
        compiler_params=SMALL,
        cost_estimate=COST,
        name="tie",
    )(*values, *after)


def encode_terms(terms, after):
    def body(a, *refs):
        b = refs[-1]
        code = jnp.clip((a[...] - REC_LOW) * REC_SCALE + 0.5, 0.0, 65535.0).astype(jnp.int32) - 32768
        b[...] = code.astype(jnp.int16)

    vm = pl.BlockSpec(memory_space=pltpu.VMEM)
    return pl.pallas_call(
        body,
        in_specs=[vm] + [pl.BlockSpec(memory_space=pl.ANY)] * len(after),
        out_specs=vm,
        out_shape=jax.ShapeDtypeStruct(terms.shape, jnp.int16),
        compiler_params=SMALL,
        cost_estimate=COST,
        name="encode_terms",
    )(terms, *after)


def spectra(blocks, table, width):
    rows, part = blocks[0].shape
    tile = 512

    def body(b0, b1, b2, b3, t, *outs):
        for k, out in enumerate(outs):
            cols = pl.ds(k * 2 * width, 2 * width)
            acc = None
            for j, b in enumerate((b0, b1, b2, b3)):
                one = jnp.dot(b[...], t[pl.ds(j * part, part), cols], preferred_element_type=jnp.float32)
                acc = one if acc is None else acc + one
            re, im = acc[:, :width], acc[:, width:]
            logamp = 0.5 * jnp.log(re * re + im * im + 1.0)
            code = jnp.minimum(logamp * LA_SCALE + 0.5, 65535.0).astype(jnp.int32) - 32768
            out[...] = code.astype(jnp.int16)

    return pl.pallas_call(
        body,
        grid=(rows // tile,),
        in_specs=[pl.BlockSpec((tile, part), lambda i: (i, 0))] * NY + [pl.BlockSpec(table.shape, lambda i: (0, 0))],
        out_specs=[pl.BlockSpec((tile, width), lambda i: (i, 0))] * NY,
        out_shape=[jax.ShapeDtypeStruct((rows, width), jnp.int16)] * NY,
        compiler_params=SMALL,
        cost_estimate=COST,
        name="spectra",
    )(*blocks, table)


def gather_shots(shot_near, shot_at, sizes):
    width = shot_near.shape[1]
    unroll = 64

    def body(shot_at, shot, *outs):
        for k, out in enumerate(outs):

            def step(b, _, out=out, first=sum(sizes[:k])):
                at = [b * unroll + u for u in range(unroll)]
                row = [shot[pl.ds(shot_at[first + i], 1), :] for i in at]
                for i, value in zip(at, row):
                    out[pl.ds(i, 1), :] = value
                return 0

            lax.fori_loop(0, sizes[k] // unroll, step, 0)

    vm, sm = pl.BlockSpec(memory_space=pltpu.VMEM), pl.BlockSpec(memory_space=pltpu.SMEM)
    return pl.pallas_call(
        body,
        in_specs=[sm, vm],
        out_specs=[vm] * len(sizes),
        out_shape=[jax.ShapeDtypeStruct((size, width), jnp.float32) for size in sizes],
        compiler_params=SMALL,
        cost_estimate=COST,
        name="gather_shots",
    )(shot_at, shot_near)


def sum_receivers(codes, shots, coded, live, rec_at, before):
    rows, width = shots.shape
    size, half = codes[0].shape[0], coded[0].shape[0]
    banks, unroll = 4, 32
    parts, held = len(codes), len(before)

    def body(*refs):
        rec_at, live, shots, own, other = refs[:5]
        codes, before = refs[5 : 5 + parts], refs[5 + parts : 5 + parts + held]
        near, far, res, rec = refs[5 + parts + held : 9 + parts + held]
        sums = refs[9 + parts + held :]
        halves = (pl.ds(0, half), pl.ds(half, half))
        for code, at in zip((own, other), halves):
            rec[at, :] = (code[...].astype(jnp.float32) + 32768.0) * (1.0 / REC_SCALE) + REC_LOW
        rec[pl.ds(2 * half, 8), :] = jnp.zeros((8, width), jnp.float32)
        for k, s in enumerate(sums):
            if k or not held:
                s[...] = jnp.zeros_like(s)
        for s, at in zip(before, halves):
            sums[0][at, :] = s[...]
        for k, code in enumerate(codes):
            at = pl.ds(k * size, size)
            logamp = (code[...].astype(jnp.float32) + 32768.0) * (1.0 / LA_SCALE)
            alive = lax.broadcasted_iota(jnp.int32, code.shape, 0) < live[k]
            res[at, :] = jnp.where(alive, logamp - shots[at, :], 0.0)

        def step(b, _):
            for u in range(unroll):
                s, row, at = sums[u % banks], pl.ds(b * unroll + u, 1), pl.ds(rec_at[b * unroll + u], 1)
                value = res[row, :] - rec[at, :]
                s[at, :] = s[at, :] + value
                res[row, :] = value
            return 0

        lax.fori_loop(0, rows // unroll, step, 0)
        for out, at in zip((near, far), halves):
            out[...] = (sums[0][at, :] + sums[1][at, :]) + (sums[2][at, :] + sums[3][at, :])

    vm, sm = pl.BlockSpec(memory_space=pltpu.VMEM), pl.BlockSpec(memory_space=pltpu.SMEM)
    sums = pltpu.VMEM((2 * half + 8, width), jnp.float32)
    return pl.pallas_call(
        body,
        in_specs=[sm, sm] + [vm] * (3 + parts + held),
        out_specs=[vm] * 3,
        out_shape=[jax.ShapeDtypeStruct((n, width), jnp.float32) for n in (half, half, rows)],
        scratch_shapes=[sums] * (1 + banks),
        compiler_params=SUMS,
        cost_estimate=COST,
        name="sum_receivers",
    )(rec_at, live, shots, *coded, *codes, *before)


def sum_shots(residuals, shot_at, count):
    width = residuals[0].shape[1]
    tile = 1024

    def body(shot_at, *refs):
        acc, first = jnp.zeros((count, 2 * width), jnp.float32), 0
        for res in refs[:-1]:
            for k in range(0, res.shape[0], tile):
                value = res[pl.ds(k, tile), :]
                high = value.astype(jnp.bfloat16)
                low = (value - high.astype(jnp.float32)).astype(jnp.bfloat16)
                both = jnp.concatenate([high, low], axis=1)
                hot = lax.broadcasted_iota(jnp.int32, (count, tile), 0) == shot_at[:, pl.ds(first + k, tile)]
                acc = acc + jnp.dot(hot.astype(jnp.bfloat16), both, preferred_element_type=jnp.float32)
            first += res.shape[0]
        refs[-1][...] = acc[:, :width] + acc[:, width:]

    vm = pl.BlockSpec(memory_space=pltpu.VMEM)
    return pl.pallas_call(
        body,
        in_specs=[vm] * (1 + len(residuals)),
        out_specs=vm,
        out_shape=jax.ShapeDtypeStruct((count, width), jnp.float32),
        compiler_params=SMALL,
        cost_estimate=COST,
        name="sum_shots",
    )(shot_at[None, :], *residuals)


def neighbour(value, by):
    size = NZ * NX * NC
    return lax.ppermute(value, "tr", [(i, i + by) for i in range(size) if 0 <= i + by < size])


def per_device(traces, shot_index, receiver_index, live_counts, shot_terms, receiver_terms):
    rows, part = traces.shape
    block, width = shot_terms.shape
    share = rows // NY
    first = [sum(PIECES[:h]) for h in range(len(PIECES))]
    owner, y = lax.axis_index("tr"), lax.axis_index("fq")
    z, x, c = owner // (NX * NC), owner // NC % NX, owner % NC

    got = []
    for at, size in zip(first, PIECES):
        mine = [lax.dynamic_slice_in_dim(traces, (y + k) % NY * share + at, size, 0) for k in range(NY)]
        if got:
            mine[1:] = tie(mine[1:], got[0][1:])
        come = {k: send_y(mine[k], k) for k in (1, 3, 2)}
        got.append([mine[0]] + [come[k] for k in range(1, NY)])
    table = make_table(part * NY, y, width, got[0][:1])
    codes, coded = [], []
    for blocks in got:
        coded.append(spectra(blocks, table, width))
        codes += [send_y(coded[-1][k], k) if k else coded[-1][k] for k in range(NY)]

    def ordered(v):
        v = v.reshape(NY, share)
        v = jnp.stack([lax.dynamic_index_in_dim(v, (y - k) % NY, 0, keepdims=False) for k in range(NY)])
        return jnp.concatenate([v[:, at : at + size].reshape(NY * size) for at, size in zip(first, PIECES)])

    near = receiver_index // block
    rz, rx, rc = near // (NX * NC), near // NC % NX, near % NC
    turn = rz ^ z
    place = (((rc ^ c) * NX + (rx ^ x)) * 2 + (turn & 1)) * (NZ // 2) + turn // 2
    place = place * block + receiver_index % block
    spare = block * NZ * NX * NC
    rec_at = ordered(jnp.where(jnp.arange(rows, dtype=jnp.int32) < live_counts[0], place, spare))
    shot_at = ordered(shot_index - (owner - 1) * block)
    live = live_counts[0] - jnp.stack([(y - k) % NY * share + at for at in first for k in range(NY)])

    shot_terms = join([shot_terms], (table,))
    shot_near = jnp.concatenate([neighbour(shot_terms, 1), shot_terms, neighbour(shot_terms, -1)])
    terms = encode_terms(receiver_terms, (table,))
    terms = join([terms, swap(terms, 2, 0, 0)])
    terms = join([terms, swap(terms, 4, 0, 0)], got[0][1:] + [shot_near])
    terms = join([terms, swap(terms, 1, 0, 0)])
    shots = gather_shots(shot_near, shot_at, [size * NY for size in PIECES])
    terms = join([terms, swap(terms, 0, 1, 0)], [codes[1], shots[0], rec_at] + got[1][1:])
    terms = join([terms, swap(terms, 0, 2, 0)], [coded[1][0]] + codes[2:NY])
    far_terms = swap(terms, 0, 0, 1)

    sums, residuals, done = (), [], 0
    for h, part_shots in enumerate(shots):
        some = slice(h * NY, (h + 1) * NY)
        at = rec_at[done : done + part_shots.shape[0]]
        done += part_shots.shape[0]
        *sums, resid = sum_receivers(codes[some], part_shots, [terms, far_terms], live[some], at, sums)
        residuals.append(resid)
    sums, far_sums = sums
    sums = (sums + swap(far_sums, 0, 0, 1)).reshape(NX, 2, NZ // 2, block, width)
    shots = sum_shots(residuals, shot_at, 3 * block)
    sent = (sums * SUM_SCALE).astype(jnp.float16)
    come = [swap(sent[k], 0, k, 0).astype(jnp.float32) for k in (1, 3, 2)]
    mine = join([sums[0].reshape(-1, width)], (shots,)).reshape(sums.shape[1:])
    sums = mine + (come[0] + come[1] + come[2]) * (1.0 / SUM_SCALE)
    shot_sums = shots[block : 2 * block] + neighbour(shots[2 * block :], 1) + neighbour(shots[:block], -1)
    sent = (sums[1] * SUM_SCALE).astype(jnp.float16)
    mine = join([sums[0].reshape(-1, width)], (shot_sums,)).reshape(sums.shape[1:])
    sums = mine + swap(sent, 1, 0, 0).astype(jnp.float32) * (1.0 / SUM_SCALE)
    sums = sums.reshape(2, 2, block, width)
    sent = (sums[:, 1] * SUM_SCALE).astype(jnp.float16)
    sums = sums[:, 0] + swap(sent, 2, 0, 0).astype(jnp.float32) * (1.0 / SUM_SCALE)
    sent = (sums[1] * SUM_SCALE).astype(jnp.float16)
    receiver_sums = sums[0] + swap(sent, 4, 0, 0).astype(jnp.float32) * (1.0 / SUM_SCALE)
    return (shot_sums, receiver_sums)


def solution(mesh):
    return jax.shard_map(
        per_device,
        mesh=mesh,
        in_specs=(P("tr", "fq"), P("tr"), P("tr"), P("tr"), P("tr", "fq"), P("tr", "fq")),
        out_specs=(P("tr", "fq"), P("tr", "fq")),
        check_vma=False,
    )
```

```python
import math

import jax
import jax.numpy as jnp
from jax import lax
from jax.experimental import pallas as pl
from jax.experimental.pallas import tpu as pltpu
from jax.sharding import PartitionSpec as P

NZ, NX, NC, NY = 8, 4, 2, 4
LA_TOP = 9.1
LA_SCALE = 65535.0 / LA_TOP
REC_LOW, REC_HIGH = 1.0, 2.2
REC_SCALE = 65535.0 / (REC_HIGH - REC_LOW)
SUM_SCALE = 1.0 / 32.0
PIECES = (1024, 1024)
SUMS = pltpu.CompilerParams(vmem_limit_bytes=32 * 2**20)
SMALL = pltpu.CompilerParams(vmem_limit_bytes=12 * 2**20)
COST = pl.CostEstimate(flops=1000, bytes_accessed=1000, transcendentals=0)


def tr_of(z, x, c):
    return (z * NX + x) * NC + c


def sites():
    return [(z, x, c) for z in range(NZ) for x in range(NX) for c in range(NC)]


def swap(value, dz, dx, dc):
    return lax.ppermute(value, "tr", [(tr_of(z, x, c), tr_of(z ^ dz, x ^ dx, c ^ dc)) for z, x, c in sites()])


def send_y(value, k):
    return lax.ppermute(value, "fq", [(i, (i + k) % NY) for i in range(NY)])


def make_table(samples, y, width, after):
    part, cols = samples // NY, NY * 2 * width
    tile = 128
    quarter = samples // 4
    shift = quarter.bit_length() - 1

    def body(y_ref, *refs):
        y, out = y_ref[0], refs[-1]
        row = pl.program_id(0) * tile
        time = (y - row // part) % NY * part + row % part + lax.broadcasted_iota(jnp.int32, (tile, 1), 0)
        for k in range(NY):
            first = (y + k) % NY * width
            for half in range(2):
                freq = first + lax.broadcasted_iota(jnp.int32, (1, width), 1)
                phase = (time * freq + half * quarter) & (samples - 1)
                turn = lax.shift_right_logical(phase + quarter // 2, shift)
                rest = (phase - turn * quarter).astype(jnp.float32) * (2.0 * math.pi / samples)
                sq = rest * rest
                cos = 1.0 + sq * (-0.5 + sq * (1 / 24 + sq * (-1 / 720 + sq * (1 / 40320 - sq * (1 / 3628800)))))
                sin = rest * (1.0 + sq * (-1 / 6 + sq * (1 / 120 + sq * (-1 / 5040 + sq * (1 / 362880)))))
                value = jnp.where((turn & 1) == 1, sin, cos)
                value = jnp.where(((turn + 1) & 2) == 2, -value, value)
                out[:, pl.ds((2 * k + half) * width, width)] = value.astype(jnp.bfloat16)

    return pl.pallas_call(
        body,
        grid=(samples // tile,),
        in_specs=[pl.BlockSpec(memory_space=pltpu.SMEM)] + [pl.BlockSpec(memory_space=pl.ANY)] * len(after),
        out_specs=pl.BlockSpec((tile, cols), lambda i: (i, 0)),
        out_shape=jax.ShapeDtypeStruct((samples, cols), jnp.bfloat16),
        compiler_params=SMALL,
        cost_estimate=pl.CostEstimate(flops=2**30, bytes_accessed=2**25, transcendentals=0),
        name="make_table",
    )(y[None], *after)


def join(parts, after=()):
    size = parts[0].shape[0]

    def body(*refs):
        out = refs[-1]
        for k in range(len(parts)):
            out[pl.ds(k * size, size), :] = refs[k][...]

    vm = pl.BlockSpec(memory_space=pltpu.VMEM)
    return pl.pallas_call(
        body,
        in_specs=[vm] * len(parts) + [pl.BlockSpec(memory_space=pl.ANY)] * len(after),
        out_specs=vm,
        out_shape=jax.ShapeDtypeStruct((size * len(parts),) + parts[0].shape[1:], parts[0].dtype),
        compiler_params=SMALL,
        cost_estimate=COST,
        name="join",
    )(*parts, *after)


def tie(values, after):
    hbm = pl.BlockSpec(memory_space=pl.ANY)
    return pl.pallas_call(
        lambda *refs: None,
        in_specs=[hbm] * (len(values) + len(after)),
        out_specs=[hbm] * len(values),
        out_shape=[jax.ShapeDtypeStruct(value.shape, value.dtype) for value in values],
        input_output_aliases={k: k for k in range(len(values))},
        compiler_params=SMALL,
        cost_estimate=COST,
        name="tie",
    )(*values, *after)


def encode_terms(terms, after):
    def body(a, *refs):
        b = refs[-1]
        code = jnp.clip((a[...] - REC_LOW) * REC_SCALE + 0.5, 0.0, 65535.0).astype(jnp.int32) - 32768
        b[...] = code.astype(jnp.int16)

    vm = pl.BlockSpec(memory_space=pltpu.VMEM)
    return pl.pallas_call(
        body,
        in_specs=[vm] + [pl.BlockSpec(memory_space=pl.ANY)] * len(after),
        out_specs=vm,
        out_shape=jax.ShapeDtypeStruct(terms.shape, jnp.int16),
        compiler_params=SMALL,
        cost_estimate=COST,
        name="encode_terms",
    )(terms, *after)


def spectra(blocks, table, width):
    rows, part = blocks[0].shape
    tile = 512

    def body(b0, b1, b2, b3, t, *outs):
        for k, out in enumerate(outs):
            cols = pl.ds(k * 2 * width, 2 * width)
            acc = None
            for j, b in enumerate((b0, b1, b2, b3)):
                one = jnp.dot(b[...], t[pl.ds(j * part, part), cols], preferred_element_type=jnp.float32)
                acc = one if acc is None else acc + one
            re, im = acc[:, :width], acc[:, width:]
            logamp = 0.5 * jnp.log(re * re + im * im + 1.0)
            code = jnp.minimum(logamp * LA_SCALE + 0.5, 65535.0).astype(jnp.int32) - 32768
            out[...] = code.astype(jnp.int16)

    return pl.pallas_call(
        body,
        grid=(rows // tile,),
        in_specs=[pl.BlockSpec((tile, part), lambda i: (i, 0))] * NY + [pl.BlockSpec(table.shape, lambda i: (0, 0))],
        out_specs=[pl.BlockSpec((tile, width), lambda i: (i, 0))] * NY,
        out_shape=[jax.ShapeDtypeStruct((rows, width), jnp.int16)] * NY,
        compiler_params=SMALL,
        cost_estimate=COST,
        name="spectra",
    )(*blocks, table)


def gather_shots(shot_near, shot_at, sizes):
    width = shot_near.shape[1]
    unroll = 64

    def body(shot_at, shot, *outs):
        for k, out in enumerate(outs):

            def step(b, _, out=out, first=sum(sizes[:k])):
                at = [b * unroll + u for u in range(unroll)]
                row = [shot[pl.ds(shot_at[first + i], 1), :] for i in at]
                for i, value in zip(at, row):
                    out[pl.ds(i, 1), :] = value
                return 0

            lax.fori_loop(0, sizes[k] // unroll, step, 0)

    vm, sm = pl.BlockSpec(memory_space=pltpu.VMEM), pl.BlockSpec(memory_space=pltpu.SMEM)
    return pl.pallas_call(
        body,
        in_specs=[sm, vm],
        out_specs=[vm] * len(sizes),
        out_shape=[jax.ShapeDtypeStruct((size, width), jnp.float32) for size in sizes],
        compiler_params=SMALL,
        cost_estimate=COST,
        name="gather_shots",
    )(shot_at, shot_near)


def sum_receivers(codes, shots, coded, live, rec_at, before):
    rows, width = shots.shape
    size, half = codes[0].shape[0], coded[0].shape[0]
    banks, unroll = 4, 32
    parts, held = len(codes), len(before)

    def body(*refs):
        rec_at, live, shots, own, other = refs[:5]
        codes, before = refs[5 : 5 + parts], refs[5 + parts : 5 + parts + held]
        near, far, res, rec = refs[5 + parts + held : 9 + parts + held]
        sums = refs[9 + parts + held :]
        halves = (pl.ds(0, half), pl.ds(half, half))
        for code, at in zip((own, other), halves):
            rec[at, :] = (code[...].astype(jnp.float32) + 32768.0) * (1.0 / REC_SCALE) + REC_LOW
        rec[pl.ds(2 * half, 8), :] = jnp.zeros((8, width), jnp.float32)
        for k, s in enumerate(sums):
            if k or not held:
                s[...] = jnp.zeros_like(s)
        for s, at in zip(before, halves):
            sums[0][at, :] = s[...]
        for k, code in enumerate(codes):
            at = pl.ds(k * size, size)
            logamp = (code[...].astype(jnp.float32) + 32768.0) * (1.0 / LA_SCALE)
            alive = lax.broadcasted_iota(jnp.int32, code.shape, 0) < live[k]
            res[at, :] = jnp.where(alive, logamp - shots[at, :], 0.0)

        def step(b, _):
            for u in range(unroll):
                s, row, at = sums[u % banks], pl.ds(b * unroll + u, 1), pl.ds(rec_at[b * unroll + u], 1)
                value = res[row, :] - rec[at, :]
                s[at, :] = s[at, :] + value
                res[row, :] = value
            return 0

        lax.fori_loop(0, rows // unroll, step, 0)
        for out, at in zip((near, far), halves):
            out[...] = (sums[0][at, :] + sums[1][at, :]) + (sums[2][at, :] + sums[3][at, :])

    vm, sm = pl.BlockSpec(memory_space=pltpu.VMEM), pl.BlockSpec(memory_space=pltpu.SMEM)
    sums = pltpu.VMEM((2 * half + 8, width), jnp.float32)
    return pl.pallas_call(
        body,
        in_specs=[sm, sm] + [vm] * (3 + parts + held),
        out_specs=[vm] * 3,
        out_shape=[jax.ShapeDtypeStruct((n, width), jnp.float32) for n in (half, half, rows)],
        scratch_shapes=[sums] * (1 + banks),
        compiler_params=SUMS,
        cost_estimate=COST,
        name="sum_receivers",
    )(rec_at, live, shots, *coded, *codes, *before)


def sum_shots(residuals, shot_at, count):
    width = residuals[0].shape[1]
    tile = 1024

    def body(shot_at, *refs):
        acc, first = jnp.zeros((count, 2 * width), jnp.float32), 0
        for res in refs[:-1]:
            for k in range(0, res.shape[0], tile):
                value = res[pl.ds(k, tile), :]
                high = value.astype(jnp.bfloat16)
                low = (value - high.astype(jnp.float32)).astype(jnp.bfloat16)
                both = jnp.concatenate([high, low], axis=1)
                hot = lax.broadcasted_iota(jnp.int32, (count, tile), 0) == shot_at[:, pl.ds(first + k, tile)]
                acc = acc + jnp.dot(hot.astype(jnp.bfloat16), both, preferred_element_type=jnp.float32)
            first += res.shape[0]
        refs[-1][...] = acc[:, :width] + acc[:, width:]

    vm = pl.BlockSpec(memory_space=pltpu.VMEM)
    return pl.pallas_call(
        body,
        in_specs=[vm] * (1 + len(residuals)),
        out_specs=vm,
        out_shape=jax.ShapeDtypeStruct((count, width), jnp.float32),
        compiler_params=SMALL,
        cost_estimate=COST,
        name="sum_shots",
    )(shot_at[None, :], *residuals)


def neighbour(value, by):
    size = NZ * NX * NC
    return lax.ppermute(value, "tr", [(i, i + by) for i in range(size) if 0 <= i + by < size])


def per_device(traces, shot_index, receiver_index, live_counts, shot_terms, receiver_terms):
    rows, part = traces.shape
    block, width = shot_terms.shape
    share = rows // NY
    first = [sum(PIECES[:h]) for h in range(len(PIECES))]
    owner, y = lax.axis_index("tr"), lax.axis_index("fq")
    z, x, c = owner // (NX * NC), owner // NC % NX, owner % NC

    got = []
    for at, size in zip(first, PIECES):
        mine = [lax.dynamic_slice_in_dim(traces, (y + k) % NY * share + at, size, 0) for k in range(NY)]
        if got:
            mine[1:] = tie(mine[1:], got[0][1:])
        come = {k: send_y(mine[k], k) for k in (1, 3, 2)}
        got.append([mine[0]] + [come[k] for k in range(1, NY)])
    table = make_table(part * NY, y, width, got[0][:1])
    codes, coded = [], []
    for blocks in got:
        coded.append(spectra(blocks, table, width))
        codes += [send_y(coded[-1][k], k) if k else coded[-1][k] for k in range(NY)]

    def ordered(v):
        v = v.reshape(NY, share)
        v = jnp.stack([lax.dynamic_index_in_dim(v, (y - k) % NY, 0, keepdims=False) for k in range(NY)])
        return jnp.concatenate([v[:, at : at + size].reshape(NY * size) for at, size in zip(first, PIECES)])

    near = receiver_index // block
    rz, rx, rc = near // (NX * NC), near // NC % NX, near % NC
    turn = rz ^ z
    place = (((rc ^ c) * NX + (rx ^ x)) * 2 + (turn & 1)) * (NZ // 2) + turn // 2
    place = place * block + receiver_index % block
    spare = block * NZ * NX * NC
    rec_at = ordered(jnp.where(jnp.arange(rows, dtype=jnp.int32) < live_counts[0], place, spare))
    shot_at = ordered(shot_index - (owner - 1) * block)
    live = live_counts[0] - jnp.stack([(y - k) % NY * share + at for at in first for k in range(NY)])

    shot_terms = join([shot_terms], (table,))
    shot_near = jnp.concatenate([neighbour(shot_terms, 1), shot_terms, neighbour(shot_terms, -1)])
    terms = encode_terms(receiver_terms, (table,))
    terms = join([terms, swap(terms, 2, 0, 0)])
    terms = join([terms, swap(terms, 4, 0, 0)], got[0][1:] + [shot_near])
    terms = join([terms, swap(terms, 1, 0, 0)])
    shots = gather_shots(shot_near, shot_at, [size * NY for size in PIECES])
    terms = join([terms, swap(terms, 0, 1, 0)], [coded[0][0], got[1][1], got[1][3]])
    terms = join([terms, swap(terms, 0, 2, 0)], [shots[0], rec_at, got[1][2], coded[1][0], codes[1]])
    far_terms = swap(terms, 0, 0, 1)

    sums, residuals, done = (), [], 0
    for h, part_shots in enumerate(shots):
        some = slice(h * NY, (h + 1) * NY)
        at = rec_at[done : done + part_shots.shape[0]]
        done += part_shots.shape[0]
        *sums, resid = sum_receivers(codes[some], part_shots, [terms, far_terms], live[some], at, sums)
        residuals.append(resid)
    sums, far_sums = sums
    sums = (sums + swap(far_sums, 0, 0, 1)).reshape(NX, 2, NZ // 2, block, width)
    shots = sum_shots(residuals, shot_at, 3 * block)
    sent = (sums * SUM_SCALE).astype(jnp.float16)
    come = [swap(sent[k], 0, k, 0).astype(jnp.float32) for k in (1, 3, 2)]
    mine = join([sums[0].reshape(-1, width)], (shots,)).reshape(sums.shape[1:])
    sums = mine + (come[0] + come[1] + come[2]) * (1.0 / SUM_SCALE)
    shot_sums = shots[block : 2 * block] + neighbour(shots[2 * block :], 1) + neighbour(shots[:block], -1)
    sent = (sums[1] * SUM_SCALE).astype(jnp.float16)
    mine = join([sums[0].reshape(-1, width)], (shot_sums,)).reshape(sums.shape[1:])
    sums = mine + swap(sent, 1, 0, 0).astype(jnp.float32) * (1.0 / SUM_SCALE)
    sums = sums.reshape(2, 2, block, width)
    sent = (sums[:, 1] * SUM_SCALE).astype(jnp.float16)
    sums = sums[:, 0] + swap(sent, 2, 0, 0).astype(jnp.float32) * (1.0 / SUM_SCALE)
    sent = (sums[1] * SUM_SCALE).astype(jnp.float16)
    receiver_sums = sums[0] + swap(sent, 4, 0, 0).astype(jnp.float32) * (1.0 / SUM_SCALE)
    return (shot_sums, receiver_sums)


def solution(mesh):
    return jax.shard_map(
        per_device,
        mesh=mesh,
        in_specs=(P("tr", "fq"), P("tr"), P("tr"), P("tr"), P("tr", "fq"), P("tr", "fq")),
        out_specs=(P("tr", "fq"), P("tr", "fq")),
        check_vma=False,
    )
```

```python
import math

import jax
import jax.numpy as jnp
from jax import lax
from jax.experimental import pallas as pl
from jax.experimental.pallas import tpu as pltpu
from jax.sharding import PartitionSpec as P

NZ, NX, NC, NY = 8, 4, 2, 4
LA_TOP = 9.1
LA_SCALE = 65535.0 / LA_TOP
REC_LOW, REC_HIGH = 1.0, 2.2
REC_SCALE = 65535.0 / (REC_HIGH - REC_LOW)
SUM_SCALE = 1.0 / 32.0
PIECES = (1024, 1024)
LARGE = pltpu.CompilerParams(vmem_limit_bytes=60 * 2**20)
SUMS = pltpu.CompilerParams(vmem_limit_bytes=20 * 2**20)
SMALL = pltpu.CompilerParams(vmem_limit_bytes=12 * 2**20)
COST = pl.CostEstimate(flops=1000, bytes_accessed=1000, transcendentals=0)
MEDIUM = pltpu.CompilerParams(vmem_limit_bytes=18 * 2**20)


def tr_of(z, x, c):
    return (z * NX + x) * NC + c


def sites():
    return [(z, x, c) for z in range(NZ) for x in range(NX) for c in range(NC)]


def swap(value, dz, dx, dc):
    return lax.ppermute(value, "tr", [(tr_of(z, x, c), tr_of(z ^ dz, x ^ dx, c ^ dc)) for z, x, c in sites()])


def send_y(value, k):
    return lax.ppermute(value, "fq", [(i, (i + k) % NY) for i in range(NY)])


def make_table(samples, y, width, after):
    part, cols = samples // NY, NY * 2 * width
    tile = 128
    quarter = samples // 4
    shift = quarter.bit_length() - 1

    def body(y_ref, *refs):
        y, out = y_ref[0], refs[-1]
        row = pl.program_id(0) * tile
        time = (y - row // part) % NY * part + row % part + lax.broadcasted_iota(jnp.int32, (tile, 1), 0)
        for k in range(NY):
            first = (y + k) % NY * width
            for half in range(2):
                freq = first + lax.broadcasted_iota(jnp.int32, (1, width), 1)
                phase = (time * freq + half * quarter) & (samples - 1)
                turn = lax.shift_right_logical(phase + quarter // 2, shift)
                rest = (phase - turn * quarter).astype(jnp.float32) * (2.0 * math.pi / samples)
                sq = rest * rest
                cos = 1.0 + sq * (-0.5 + sq * (1 / 24 + sq * (-1 / 720 + sq * (1 / 40320 - sq * (1 / 3628800)))))
                sin = rest * (1.0 + sq * (-1 / 6 + sq * (1 / 120 + sq * (-1 / 5040 + sq * (1 / 362880)))))
                value = jnp.where((turn & 1) == 1, sin, cos)
                value = jnp.where(((turn + 1) & 2) == 2, -value, value)
                out[:, pl.ds((2 * k + half) * width, width)] = value.astype(jnp.bfloat16)

    return pl.pallas_call(
        body,
        grid=(samples // tile,),
        in_specs=[pl.BlockSpec(memory_space=pltpu.SMEM)] + [pl.BlockSpec(memory_space=pl.ANY)] * len(after),
        out_specs=pl.BlockSpec((tile, cols), lambda i: (i, 0)),
        out_shape=jax.ShapeDtypeStruct((samples, cols), jnp.bfloat16),
        compiler_params=SMALL,
        cost_estimate=pl.CostEstimate(flops=2**30, bytes_accessed=2**25, transcendentals=0),
        name="make_table",
    )(y[None], *after)


def join(parts, after=()):
    size = parts[0].shape[0]

    def body(*refs):
        out = refs[-1]
        for k in range(len(parts)):
            out[pl.ds(k * size, size), :] = refs[k][...]

    vm = pl.BlockSpec(memory_space=pltpu.VMEM)
    return pl.pallas_call(
        body,
        in_specs=[vm] * len(parts) + [pl.BlockSpec(memory_space=pl.ANY)] * len(after),
        out_specs=vm,
        out_shape=jax.ShapeDtypeStruct((size * len(parts),) + parts[0].shape[1:], parts[0].dtype),
        compiler_params=SMALL,
        cost_estimate=COST,
        name="join",
    )(*parts, *after)


def take_rows(traces, y, first, size, after=()):
    rows, part = traces.shape

    def body(y_ref, traces, *refs):
        outs, sems = refs[len(after) : len(after) + NY], refs[len(after) + NY :]
        copies = []
        for k in range(NY):
            at = pl.multiple_of((y_ref[0] + k) % NY * (rows // NY) + first, 16)
            copies.append(pltpu.make_async_copy(traces.at[pl.ds(at, size), :], outs[k], sems[k]))
        for copy in copies:
            copy.start()
        for copy in copies:
            copy.wait()

    hbm, vm = pl.BlockSpec(memory_space=pl.ANY), pl.BlockSpec(memory_space=pltpu.VMEM)
    return pl.pallas_call(
        body,
        in_specs=[pl.BlockSpec(memory_space=pltpu.SMEM), hbm] + [hbm] * len(after),
        out_specs=[vm] * NY,
        out_shape=[jax.ShapeDtypeStruct((size, part), traces.dtype)] * NY,
        scratch_shapes=[pltpu.SemaphoreType.DMA] * NY,
        compiler_params=SMALL,
        cost_estimate=COST,
        name="take_rows",
    )(y[None], traces, *after)


def encode_terms(terms, after):
    def body(a, *refs):
        b = refs[-1]
        code = jnp.clip((a[...] - REC_LOW) * REC_SCALE + 0.5, 0.0, 65535.0).astype(jnp.int32) - 32768
        b[...] = code.astype(jnp.int16)

    vm = pl.BlockSpec(memory_space=pltpu.VMEM)
    return pl.pallas_call(
        body,
        in_specs=[vm] + [pl.BlockSpec(memory_space=pl.ANY)] * len(after),
        out_specs=vm,
        out_shape=jax.ShapeDtypeStruct(terms.shape, jnp.int16),
        compiler_params=SMALL,
        cost_estimate=COST,
        name="encode_terms",
    )(terms, *after)


def spectra(blocks, table, width):
    rows, part = blocks[0].shape
    tile = 512

    def body(b0, b1, b2, b3, t, *outs):
        for k, out in enumerate(outs):
            cols = pl.ds(k * 2 * width, 2 * width)
            acc = None
            for j, b in enumerate((b0, b1, b2, b3)):
                one = jnp.dot(b[...], t[pl.ds(j * part, part), cols], preferred_element_type=jnp.float32)
                acc = one if acc is None else acc + one
            re, im = acc[:, :width], acc[:, width:]
            logamp = 0.5 * jnp.log(re * re + im * im + 1.0)
            code = jnp.minimum(logamp * LA_SCALE + 0.5, 65535.0).astype(jnp.int32) - 32768
            out[...] = code.astype(jnp.int16)

    return pl.pallas_call(
        body,
        grid=(rows // tile,),
        in_specs=[pl.BlockSpec((tile, part), lambda i: (i, 0))] * NY + [pl.BlockSpec(table.shape, lambda i: (0, 0))],
        out_specs=[pl.BlockSpec((tile, width), lambda i: (i, 0))] * NY,
        out_shape=[jax.ShapeDtypeStruct((rows, width), jnp.int16)] * NY,
        compiler_params=MEDIUM,
        cost_estimate=COST,
        name="spectra",
    )(*blocks, table)


def gather_shots(shot_near, shot_at, sizes):
    width = shot_near.shape[1]
    unroll = 64

    def body(shot_at, shot, *outs):
        for k, out in enumerate(outs):

            def step(b, _, out=out, first=sum(sizes[:k])):
                at = [b * unroll + u for u in range(unroll)]
                row = [shot[pl.ds(shot_at[first + i], 1), :] for i in at]
                for i, value in zip(at, row):
                    out[pl.ds(i, 1), :] = value
                return 0

            lax.fori_loop(0, sizes[k] // unroll, step, 0)

    vm, sm = pl.BlockSpec(memory_space=pltpu.VMEM), pl.BlockSpec(memory_space=pltpu.SMEM)
    return pl.pallas_call(
        body,
        in_specs=[sm, vm],
        out_specs=[vm] * len(sizes),
        out_shape=[jax.ShapeDtypeStruct((size, width), jnp.float32) for size in sizes],
        compiler_params=MEDIUM,
        cost_estimate=COST,
        name="gather_shots",
    )(shot_at, shot_near)


def sum_receivers(codes, shots, coded, live, rec_at, held, last):
    rows, width = shots.shape
    size, half = codes[0].shape[0], coded[0].shape[0]
    banks, unroll = 4, 32
    parts, first = len(codes), not held
    given = list(coded) if first else list(held)

    def body(*refs):
        rec_at, live, shots = refs[:3]
        codes, given = refs[3 : 3 + parts], refs[3 + parts :]
        res, outs = given[2 if first else banks + 1], given[3 if first else banks + 2 :]
        rec, sums = outs[0], outs[1 : 1 + banks]
        halves = (pl.ds(0, half), pl.ds(half, half))
        if first:
            for code, at in zip(given[:2], halves):
                rec[at, :] = (code[...].astype(jnp.float32) + 32768.0) * (1.0 / REC_SCALE) + REC_LOW
            rec[pl.ds(2 * half, 8), :] = jnp.zeros((8, width), jnp.float32)
            for s in sums:
                s[...] = jnp.zeros_like(s)
        for k, code in enumerate(codes):
            at = pl.ds(k * size, size)
            logamp = (code[...].astype(jnp.float32) + 32768.0) * (1.0 / LA_SCALE)
            alive = lax.broadcasted_iota(jnp.int32, code.shape, 0) < live[k]
            res[at, :] = jnp.where(alive, logamp - shots[at, :], 0.0)

        def step(b, _):
            for u in range(unroll):
                s, row, at = sums[u % banks], pl.ds(b * unroll + u, 1), pl.ds(rec_at[b * unroll + u], 1)
                value = res[row, :] - rec[at, :]
                s[at, :] = s[at, :] + value
                res[row, :] = value
            return 0

        lax.fori_loop(0, rows // unroll, step, 0)
        if last:
            for out, at in zip(outs[1 + banks :], halves):
                out[...] = (sums[0][at, :] + sums[1][at, :]) + (sums[2][at, :] + sums[3][at, :])

    vm, sm = pl.BlockSpec(memory_space=pltpu.VMEM), pl.BlockSpec(memory_space=pltpu.SMEM)
    shapes = [(rows, width)] + [(2 * half + 8, width)] * (1 + banks) + [(half, width)] * (2 if last else 0)
    return pl.pallas_call(
        body,
        in_specs=[sm, sm] + [vm] * (1 + parts + len(given)),
        out_specs=[vm] * len(shapes),
        out_shape=[jax.ShapeDtypeStruct(shape, jnp.float32) for shape in shapes],
        input_output_aliases={} if first else {3 + parts + k: 1 + k for k in range(1 + banks)},
        compiler_params=SUMS,
        cost_estimate=COST,
        name="sum_receivers",
    )(rec_at, live, shots, *codes, *given)


def sum_shots(residuals, shot_at, count):
    width = residuals[0].shape[1]
    tile = 1024

    def body(shot_at, *refs):
        acc, first = jnp.zeros((count, 2 * width), jnp.float32), 0
        for res in refs[:-1]:
            for k in range(0, res.shape[0], tile):
                value = res[pl.ds(k, tile), :]
                high = value.astype(jnp.bfloat16)
                low = (value - high.astype(jnp.float32)).astype(jnp.bfloat16)
                both = jnp.concatenate([high, low], axis=1)
                hot = lax.broadcasted_iota(jnp.int32, (count, tile), 0) == shot_at[:, pl.ds(first + k, tile)]
                acc = acc + jnp.dot(hot.astype(jnp.bfloat16), both, preferred_element_type=jnp.float32)
            first += res.shape[0]
        refs[-1][...] = acc[:, :width] + acc[:, width:]

    vm = pl.BlockSpec(memory_space=pltpu.VMEM)
    return pl.pallas_call(
        body,
        in_specs=[vm] * (1 + len(residuals)),
        out_specs=vm,
        out_shape=jax.ShapeDtypeStruct((count, width), jnp.float32),
        compiler_params=MEDIUM,
        cost_estimate=COST,
        name="sum_shots",
    )(shot_at[None, :], *residuals)


def neighbour(value, by):
    size = NZ * NX * NC
    return lax.ppermute(value, "tr", [(i, i + by) for i in range(size) if 0 <= i + by < size])


def per_device(traces, shot_index, receiver_index, live_counts, shot_terms, receiver_terms):
    rows, part = traces.shape
    block, width = shot_terms.shape
    share = rows // NY
    first = [sum(PIECES[:h]) for h in range(len(PIECES))]
    owner, y = lax.axis_index("tr"), lax.axis_index("fq")
    z, x, c = owner // (NX * NC), owner // NC % NX, owner % NC

    got, after = [], ()
    for at, size in zip(first, PIECES):
        if after:
            mine = take_rows(traces, y, at, size, after)
        else:
            mine = [lax.dynamic_slice_in_dim(traces, (y + k) % NY * share + at, size, 0) for k in range(NY)]
        come = {k: send_y(mine[k], k) for k in (1, 3, 2)}
        after = [come[k] for k in range(1, NY)]
        got.append([mine[0]] + after)
    table = make_table(part * NY, y, width, got[0][:1])
    codes, coded = [], []
    for blocks in got:
        coded.append(spectra(blocks, table, width))
        codes += [send_y(coded[-1][k], k) if k else coded[-1][k] for k in range(NY)]

    def ordered(v):
        v = v.reshape(NY, share)
        v = jnp.stack([lax.dynamic_index_in_dim(v, (y - k) % NY, 0, keepdims=False) for k in range(NY)])
        return jnp.concatenate([v[:, at : at + size].reshape(NY * size) for at, size in zip(first, PIECES)])

    near = receiver_index // block
    rz, rx, rc = near // (NX * NC), near // NC % NX, near % NC
    turn = rz ^ z
    place = (((rc ^ c) * NX + (rx ^ x)) * 2 + (turn & 1)) * (NZ // 2) + turn // 2
    place = place * block + receiver_index % block
    spare = block * NZ * NX * NC
    rec_at = ordered(jnp.where(jnp.arange(rows, dtype=jnp.int32) < live_counts[0], place, spare))
    shot_at = ordered(shot_index - (owner - 1) * block)
    live = live_counts[0] - jnp.stack([(y - k) % NY * share + at for at in first for k in range(NY)])

    shot_terms = join([shot_terms], (table,))
    shot_near = jnp.concatenate([neighbour(shot_terms, 1), shot_terms, neighbour(shot_terms, -1)])
    terms = encode_terms(receiver_terms, (table,))
    terms = join([terms, swap(terms, 2, 0, 0)])
    terms = join([terms, swap(terms, 4, 0, 0)], got[0][1:] + [shot_near])
    terms = join([terms, swap(terms, 1, 0, 0)], got[1][:1])
    shots = gather_shots(shot_near, shot_at, [size * NY for size in PIECES])
    terms = join([terms, swap(terms, 0, 1, 0)], [coded[0][0]])
    terms = join([terms, swap(terms, 0, 2, 0)], [shots[0], rec_at] + got[1][1:])
    far_terms = swap(terms, 0, 0, 1)

    held, residuals, done = [], [], 0
    for h, part_shots in enumerate(shots):
        some, last = slice(h * NY, (h + 1) * NY), h == len(shots) - 1
        at = rec_at[done : done + part_shots.shape[0]]
        done += part_shots.shape[0]
        resid, *held = sum_receivers(codes[some], part_shots, [terms, far_terms], live[some], at, held, last)
        residuals.append(resid)
    sums, far_sums = held[-2:]
    sums = (sums + swap(far_sums, 0, 0, 1)).reshape(NX, 2, NZ // 2, block, width)
    shots = sum_shots(residuals, shot_at, 3 * block)
    sent = (sums * SUM_SCALE).astype(jnp.float16)
    come = [swap(sent[k], 0, k, 0).astype(jnp.float32) for k in (1, 3, 2)]
    mine = join([sums[0].reshape(-1, width)], (shots,)).reshape(sums.shape[1:])
    sums = mine + (come[0] + come[1] + come[2]) * (1.0 / SUM_SCALE)
    shot_sums = shots[block : 2 * block] + neighbour(shots[2 * block :], 1) + neighbour(shots[:block], -1)
    sent = (sums[1] * SUM_SCALE).astype(jnp.float16)
    mine = join([sums[0].reshape(-1, width)], (shot_sums,)).reshape(sums.shape[1:])
    sums = mine + swap(sent, 1, 0, 0).astype(jnp.float32) * (1.0 / SUM_SCALE)
    sums = sums.reshape(2, 2, block, width)
    sent = (sums[:, 1] * SUM_SCALE).astype(jnp.float16)
    sums = sums[:, 0] + swap(sent, 2, 0, 0).astype(jnp.float32) * (1.0 / SUM_SCALE)
    sent = (sums[1] * SUM_SCALE).astype(jnp.float16)
    receiver_sums = sums[0] + swap(sent, 4, 0, 0).astype(jnp.float32) * (1.0 / SUM_SCALE)
    return (shot_sums, receiver_sums)


def solution(mesh):
    return jax.shard_map(
        per_device,
        mesh=mesh,
        in_specs=(P("tr", "fq"), P("tr"), P("tr"), P("tr"), P("tr", "fq"), P("tr", "fq")),
        out_specs=(P("tr", "fq"), P("tr", "fq")),
        check_vma=False,
    )
```

```python
import math

import jax
import jax.numpy as jnp
from jax import lax
from jax.experimental import pallas as pl
from jax.experimental.pallas import tpu as pltpu
from jax.sharding import PartitionSpec as P

NZ, NX, NC, NY = 8, 4, 2, 4
LA_TOP = 9.1
LA_SCALE = 65535.0 / LA_TOP
REC_LOW, REC_HIGH = 1.0, 2.2
REC_SCALE = 65535.0 / (REC_HIGH - REC_LOW)
SUM_SCALE = 1.0 / 32.0
PIECES = (1024, 1024)
LARGE = pltpu.CompilerParams(vmem_limit_bytes=60 * 2**20)
SUMS = pltpu.CompilerParams(vmem_limit_bytes=20 * 2**20)
SMALL = pltpu.CompilerParams(vmem_limit_bytes=12 * 2**20)
COST = pl.CostEstimate(flops=1000, bytes_accessed=1000, transcendentals=0)
MEDIUM = pltpu.CompilerParams(vmem_limit_bytes=18 * 2**20)


def tr_of(z, x, c):
    return (z * NX + x) * NC + c


def sites():
    return [(z, x, c) for z in range(NZ) for x in range(NX) for c in range(NC)]


def swap(value, dz, dx, dc):
    return lax.ppermute(value, "tr", [(tr_of(z, x, c), tr_of(z ^ dz, x ^ dx, c ^ dc)) for z, x, c in sites()])


def send_y(value, k):
    return lax.ppermute(value, "fq", [(i, (i + k) % NY) for i in range(NY)])


def make_table(samples, y, width, after):
    part, cols = samples // NY, NY * 2 * width
    tile = 128
    quarter = samples // 4
    shift = quarter.bit_length() - 1

    def body(y_ref, *refs):
        y, out = y_ref[0], refs[-1]
        row = pl.program_id(0) * tile
        time = (y - row // part) % NY * part + row % part + lax.broadcasted_iota(jnp.int32, (tile, 1), 0)
        for k in range(NY):
            first = (y + k) % NY * width
            for half in range(2):
                freq = first + lax.broadcasted_iota(jnp.int32, (1, width), 1)
                phase = (time * freq + half * quarter) & (samples - 1)
                turn = lax.shift_right_logical(phase + quarter // 2, shift)
                rest = (phase - turn * quarter).astype(jnp.float32) * (2.0 * math.pi / samples)
                sq = rest * rest
                cos = 1.0 + sq * (-0.5 + sq * (1 / 24 + sq * (-1 / 720 + sq * (1 / 40320 - sq * (1 / 3628800)))))
                sin = rest * (1.0 + sq * (-1 / 6 + sq * (1 / 120 + sq * (-1 / 5040 + sq * (1 / 362880)))))
                value = jnp.where((turn & 1) == 1, sin, cos)
                value = jnp.where(((turn + 1) & 2) == 2, -value, value)
                out[:, pl.ds((2 * k + half) * width, width)] = value.astype(jnp.bfloat16)

    return pl.pallas_call(
        body,
        grid=(samples // tile,),
        in_specs=[pl.BlockSpec(memory_space=pltpu.SMEM)] + [pl.BlockSpec(memory_space=pl.ANY)] * len(after),
        out_specs=pl.BlockSpec((tile, cols), lambda i: (i, 0)),
        out_shape=jax.ShapeDtypeStruct((samples, cols), jnp.bfloat16),
        compiler_params=SMALL,
        cost_estimate=pl.CostEstimate(flops=2**30, bytes_accessed=2**25, transcendentals=0),
        name="make_table",
    )(y[None], *after)


def join(parts, after=()):
    size = parts[0].shape[0]

    def body(*refs):
        out = refs[-1]
        for k in range(len(parts)):
            out[pl.ds(k * size, size), :] = refs[k][...]

    vm = pl.BlockSpec(memory_space=pltpu.VMEM)
    return pl.pallas_call(
        body,
        in_specs=[vm] * len(parts) + [pl.BlockSpec(memory_space=pl.ANY)] * len(after),
        out_specs=vm,
        out_shape=jax.ShapeDtypeStruct((size * len(parts),) + parts[0].shape[1:], parts[0].dtype),
        compiler_params=SMALL,
        cost_estimate=COST,
        name="join",
    )(*parts, *after)


def take_rows(traces, y, first, size, after=()):
    rows, part = traces.shape

    def body(y_ref, traces, *refs):
        outs, sems = refs[len(after) : len(after) + NY], refs[len(after) + NY :]
        copies = []
        for k in range(NY):
            at = pl.multiple_of((y_ref[0] + k) % NY * (rows // NY) + first, 16)
            copies.append(pltpu.make_async_copy(traces.at[pl.ds(at, size), :], outs[k], sems[k]))
        for copy in copies:
            copy.start()
        for copy in copies:
            copy.wait()

    hbm, vm = pl.BlockSpec(memory_space=pl.ANY), pl.BlockSpec(memory_space=pltpu.VMEM)
    return pl.pallas_call(
        body,
        in_specs=[pl.BlockSpec(memory_space=pltpu.SMEM), hbm] + [hbm] * len(after),
        out_specs=[vm] * NY,
        out_shape=[jax.ShapeDtypeStruct((size, part), traces.dtype)] * NY,
        scratch_shapes=[pltpu.SemaphoreType.DMA] * NY,
        compiler_params=SMALL,
        cost_estimate=COST,
        name="take_rows",
    )(y[None], traces, *after)


def encode_terms(terms, after):
    def body(a, *refs):
        b = refs[-1]
        code = jnp.clip((a[...] - REC_LOW) * REC_SCALE + 0.5, 0.0, 65535.0).astype(jnp.int32) - 32768
        b[...] = code.astype(jnp.int16)

    vm = pl.BlockSpec(memory_space=pltpu.VMEM)
    return pl.pallas_call(
        body,
        in_specs=[vm] + [pl.BlockSpec(memory_space=pl.ANY)] * len(after),
        out_specs=vm,
        out_shape=jax.ShapeDtypeStruct(terms.shape, jnp.int16),
        compiler_params=SMALL,
        cost_estimate=COST,
        name="encode_terms",
    )(terms, *after)


def spectra(blocks, table, width):
    rows, part = blocks[0].shape
    tile = 512

    def body(b0, b1, b2, b3, t, *outs):
        for k, out in enumerate(outs):
            cols = pl.ds(k * 2 * width, 2 * width)
            acc = None
            for j, b in enumerate((b0, b1, b2, b3)):
                one = jnp.dot(b[...], t[pl.ds(j * part, part), cols], preferred_element_type=jnp.float32)
                acc = one if acc is None else acc + one
            re, im = acc[:, :width], acc[:, width:]
            logamp = 0.5 * jnp.log(re * re + im * im + 1.0)
            code = jnp.minimum(logamp * LA_SCALE + 0.5, 65535.0).astype(jnp.int32) - 32768
            out[...] = code.astype(jnp.int16)

    return pl.pallas_call(
        body,
        grid=(rows // tile,),
        in_specs=[pl.BlockSpec((tile, part), lambda i: (i, 0))] * NY + [pl.BlockSpec(table.shape, lambda i: (0, 0))],
        out_specs=[pl.BlockSpec((tile, width), lambda i: (i, 0))] * NY,
        out_shape=[jax.ShapeDtypeStruct((rows, width), jnp.int16)] * NY,
        compiler_params=MEDIUM,
        cost_estimate=COST,
        name="spectra",
    )(*blocks, table)


def gather_shots(shot_near, shot_at, sizes):
    width = shot_near.shape[1]
    unroll = 64

    def body(shot_at, shot, *outs):
        for k, out in enumerate(outs):

            def step(b, _, out=out, first=sum(sizes[:k])):
                at = [b * unroll + u for u in range(unroll)]
                row = [shot[pl.ds(shot_at[first + i], 1), :] for i in at]
                for i, value in zip(at, row):
                    out[pl.ds(i, 1), :] = value
                return 0

            lax.fori_loop(0, sizes[k] // unroll, step, 0)

    vm, sm = pl.BlockSpec(memory_space=pltpu.VMEM), pl.BlockSpec(memory_space=pltpu.SMEM)
    return pl.pallas_call(
        body,
        in_specs=[sm, vm],
        out_specs=[vm] * len(sizes),
        out_shape=[jax.ShapeDtypeStruct((size, width), jnp.float32) for size in sizes],
        compiler_params=MEDIUM,
        cost_estimate=COST,
        name="gather_shots",
    )(shot_at, shot_near)


def sum_receivers(codes, shots, coded, live, rec_at, held, last):
    rows, width = shots.shape
    size, half = codes[0].shape[0], coded[0].shape[0]
    banks, unroll = 4, 32
    parts, first = len(codes), not held
    given = list(coded) if first else list(held)

    def body(*refs):
        rec_at, live, shots = refs[:3]
        codes, given = refs[3 : 3 + parts], refs[3 + parts :]
        res, outs = given[2 if first else banks + 1], given[3 if first else banks + 2 :]
        rec, sums = outs[0], outs[1 : 1 + banks]
        halves = (pl.ds(0, half), pl.ds(half, half))
        if first:
            for code, at in zip(given[:2], halves):
                rec[at, :] = (code[...].astype(jnp.float32) + 32768.0) * (1.0 / REC_SCALE) + REC_LOW
            rec[pl.ds(2 * half, 8), :] = jnp.zeros((8, width), jnp.float32)
            for s in sums:
                s[...] = jnp.zeros_like(s)
        for k, code in enumerate(codes):
            at = pl.ds(k * size, size)
            logamp = (code[...].astype(jnp.float32) + 32768.0) * (1.0 / LA_SCALE)
            alive = lax.broadcasted_iota(jnp.int32, code.shape, 0) < live[k]
            res[at, :] = jnp.where(alive, logamp - shots[at, :], 0.0)

        def step(b, _):
            for u in range(unroll):
                s, row, at = sums[u % banks], pl.ds(b * unroll + u, 1), pl.ds(rec_at[b * unroll + u], 1)
                value = res[row, :] - rec[at, :]
                s[at, :] = s[at, :] + value
                res[row, :] = value
            return 0

        lax.fori_loop(0, rows // unroll, step, 0)
        if last:
            for out, at in zip(outs[1 + banks :], halves):
                out[...] = (sums[0][at, :] + sums[1][at, :]) + (sums[2][at, :] + sums[3][at, :])

    vm, sm = pl.BlockSpec(memory_space=pltpu.VMEM), pl.BlockSpec(memory_space=pltpu.SMEM)
    shapes = [(rows, width)] + [(2 * half + 8, width)] * (1 + banks) + [(half, width)] * (2 if last else 0)
    return pl.pallas_call(
        body,
        in_specs=[sm, sm] + [vm] * (1 + parts + len(given)),
        out_specs=[vm] * len(shapes),
        out_shape=[jax.ShapeDtypeStruct(shape, jnp.float32) for shape in shapes],
        input_output_aliases={} if first else {3 + parts + k: 1 + k for k in range(1 + banks)},
        compiler_params=SUMS,
        cost_estimate=COST,
        name="sum_receivers",
    )(rec_at, live, shots, *codes, *given)


def sum_shots(residuals, shot_at, count):
    width = residuals[0].shape[1]
    tile = 1024

    def body(shot_at, *refs):
        acc, first = jnp.zeros((count, 2 * width), jnp.float32), 0
        for res in refs[:-1]:
            for k in range(0, res.shape[0], tile):
                value = res[pl.ds(k, tile), :]
                high = value.astype(jnp.bfloat16)
                low = (value - high.astype(jnp.float32)).astype(jnp.bfloat16)
                both = jnp.concatenate([high, low], axis=1)
                hot = lax.broadcasted_iota(jnp.int32, (count, tile), 0) == shot_at[:, pl.ds(first + k, tile)]
                acc = acc + jnp.dot(hot.astype(jnp.bfloat16), both, preferred_element_type=jnp.float32)
            first += res.shape[0]
        refs[-1][...] = acc[:, :width] + acc[:, width:]

    vm = pl.BlockSpec(memory_space=pltpu.VMEM)
    return pl.pallas_call(
        body,
        in_specs=[vm] * (1 + len(residuals)),
        out_specs=vm,
        out_shape=jax.ShapeDtypeStruct((count, width), jnp.float32),
        compiler_params=MEDIUM,
        cost_estimate=COST,
        name="sum_shots",
    )(shot_at[None, :], *residuals)


def neighbour(value, by):
    size = NZ * NX * NC
    return lax.ppermute(value, "tr", [(i, i + by) for i in range(size) if 0 <= i + by < size])


def per_device(traces, shot_index, receiver_index, live_counts, shot_terms, receiver_terms):
    rows, part = traces.shape
    block, width = shot_terms.shape
    share = rows // NY
    first = [sum(PIECES[:h]) for h in range(len(PIECES))]
    owner, y = lax.axis_index("tr"), lax.axis_index("fq")
    z, x, c = owner // (NX * NC), owner // NC % NX, owner % NC

    got, after = [], ()
    for at, size in zip(first, PIECES):
        if after:
            mine = take_rows(traces, y, at, size, after)
        else:
            mine = [lax.dynamic_slice_in_dim(traces, (y + k) % NY * share + at, size, 0) for k in range(NY)]
        come = {k: send_y(mine[k], k) for k in (1, 3, 2)}
        after = [come[k] for k in range(1, NY)]
        got.append([mine[0]] + after)
    table = make_table(part * NY, y, width, got[0][:1])
    codes, coded = [], []
    for blocks in got:
        coded.append(spectra(blocks, table, width))
        codes += [send_y(coded[-1][k], k) if k else coded[-1][k] for k in range(NY)]

    def ordered(v):
        v = v.reshape(NY, share)
        v = jnp.stack([lax.dynamic_index_in_dim(v, (y - k) % NY, 0, keepdims=False) for k in range(NY)])
        return jnp.concatenate([v[:, at : at + size].reshape(NY * size) for at, size in zip(first, PIECES)])

    near = receiver_index // block
    rz, rx, rc = near // (NX * NC), near // NC % NX, near % NC
    turn = rz ^ z
    place = (((rc ^ c) * NX + (rx ^ x)) * 2 + (turn & 1)) * (NZ // 2) + turn // 2
    place = place * block + receiver_index % block
    spare = block * NZ * NX * NC
    rec_at = ordered(jnp.where(jnp.arange(rows, dtype=jnp.int32) < live_counts[0], place, spare))
    shot_at = ordered(shot_index - (owner - 1) * block)
    live = live_counts[0] - jnp.stack([(y - k) % NY * share + at for at in first for k in range(NY)])

    shot_terms = join([shot_terms], (table,))
    shot_near = jnp.concatenate([neighbour(shot_terms, 1), shot_terms, neighbour(shot_terms, -1)])
    terms = encode_terms(receiver_terms, (table,))
    terms = join([terms, swap(terms, 2, 0, 0)])
    terms = join([terms, swap(terms, 4, 0, 0)], got[0][1:] + [shot_near])
    terms = join([terms, swap(terms, 1, 0, 0)], got[1][:1])
    shots = gather_shots(shot_near, shot_at, [size * NY for size in PIECES])
    terms = join([terms, swap(terms, 0, 1, 0)], [coded[0][0]])
    terms = join([terms, swap(terms, 0, 2, 0)], [shots[0], rec_at] + got[1][1:])
    far_terms = swap(terms, 0, 0, 1)

    held, residuals, done = [], [], 0
    for h, part_shots in enumerate(shots):
        some, last = slice(h * NY, (h + 1) * NY), h == len(shots) - 1
        at = rec_at[done : done + part_shots.shape[0]]
        done += part_shots.shape[0]
        resid, *held = sum_receivers(codes[some], part_shots, [terms, far_terms], live[some], at, held, last)
        residuals.append(resid)
    sums, far_sums = held[-2:]
    sums = (sums + swap(far_sums, 0, 0, 1)).reshape(NX, 2, NZ // 2 * block, width)
    shots = sum_shots(residuals, shot_at, 3 * block)
    sent = (sums * SUM_SCALE).astype(jnp.float16)
    halves = [None, None]
    for h in (1, 0):
        come = [swap(sent[k, h], 0, k, 0).astype(jnp.float32) for k in (1, 3, 2)]
        mine = join([sums[0, h]], (shots,)) if h else sums[0, h]
        halves[h] = mine + (come[0] + come[1] + come[2]) * (1.0 / SUM_SCALE)
    shot_sums = shots[block : 2 * block] + neighbour(shots[2 * block :], 1) + neighbour(shots[:block], -1)
    sent = (halves[1] * SUM_SCALE).astype(jnp.float16)
    sums = halves[0] + swap(sent, 1, 0, 0).astype(jnp.float32) * (1.0 / SUM_SCALE)
    sums = sums.reshape(2, 2, block, width)
    sent = (sums[:, 1] * SUM_SCALE).astype(jnp.float16)
    sums = sums[:, 0] + swap(sent, 2, 0, 0).astype(jnp.float32) * (1.0 / SUM_SCALE)
    sent = (sums[1] * SUM_SCALE).astype(jnp.float16)
    receiver_sums = sums[0] + swap(sent, 4, 0, 0).astype(jnp.float32) * (1.0 / SUM_SCALE)
    return (shot_sums, receiver_sums)


def solution(mesh):
    return jax.shard_map(
        per_device,
        mesh=mesh,
        in_specs=(P("tr", "fq"), P("tr"), P("tr"), P("tr"), P("tr", "fq"), P("tr", "fq")),
        out_specs=(P("tr", "fq"), P("tr", "fq")),
        check_vma=False,
    )
```

```python
import math

import jax
import jax.numpy as jnp
from jax import lax
from jax.experimental import pallas as pl
from jax.experimental.pallas import tpu as pltpu
from jax.sharding import PartitionSpec as P

NZ, NX, NC, NY = 8, 4, 2, 4
LA_TOP = 9.1
LA_SCALE = 65535.0 / LA_TOP
REC_LOW, REC_HIGH = 1.0, 2.2
REC_SCALE = 65535.0 / (REC_HIGH - REC_LOW)
SUM_SCALE = 1.0 / 32.0
PIECES = (1024, 1024)
LARGE = pltpu.CompilerParams(vmem_limit_bytes=60 * 2**20)
SUMS = pltpu.CompilerParams(vmem_limit_bytes=20 * 2**20)
SMALL = pltpu.CompilerParams(vmem_limit_bytes=12 * 2**20)
COST = pl.CostEstimate(flops=1000, bytes_accessed=1000, transcendentals=0)
MEDIUM = pltpu.CompilerParams(vmem_limit_bytes=18 * 2**20)


def tr_of(z, x, c):
    return (z * NX + x) * NC + c


def sites():
    return [(z, x, c) for z in range(NZ) for x in range(NX) for c in range(NC)]


def swap(value, dz, dx, dc):
    return lax.ppermute(value, "tr", [(tr_of(z, x, c), tr_of(z ^ dz, x ^ dx, c ^ dc)) for z, x, c in sites()])


def send_y(value, k):
    return lax.ppermute(value, "fq", [(i, (i + k) % NY) for i in range(NY)])


def make_table(samples, y, width, after):
    part, cols = samples // NY, NY * 2 * width
    tile = 128
    quarter = samples // 4
    shift = quarter.bit_length() - 1

    def body(y_ref, *refs):
        y, out = y_ref[0], refs[-1]
        row = pl.program_id(0) * tile
        time = (y - row // part) % NY * part + row % part + lax.broadcasted_iota(jnp.int32, (tile, 1), 0)
        for k in range(NY):
            first = (y + k) % NY * width
            for half in range(2):
                freq = first + lax.broadcasted_iota(jnp.int32, (1, width), 1)
                phase = (time * freq + half * quarter) & (samples - 1)
                turn = lax.shift_right_logical(phase + quarter // 2, shift)
                rest = (phase - turn * quarter).astype(jnp.float32) * (2.0 * math.pi / samples)
                sq = rest * rest
                cos = 1.0 + sq * (-0.5 + sq * (1 / 24 + sq * (-1 / 720 + sq * (1 / 40320 - sq * (1 / 3628800)))))
                sin = rest * (1.0 + sq * (-1 / 6 + sq * (1 / 120 + sq * (-1 / 5040 + sq * (1 / 362880)))))
                value = jnp.where((turn & 1) == 1, sin, cos)
                value = jnp.where(((turn + 1) & 2) == 2, -value, value)
                out[:, pl.ds((2 * k + half) * width, width)] = value.astype(jnp.bfloat16)

    return pl.pallas_call(
        body,
        grid=(samples // tile,),
        in_specs=[pl.BlockSpec(memory_space=pltpu.SMEM)] + [pl.BlockSpec(memory_space=pl.ANY)] * len(after),
        out_specs=pl.BlockSpec((tile, cols), lambda i: (i, 0)),
        out_shape=jax.ShapeDtypeStruct((samples, cols), jnp.bfloat16),
        compiler_params=SMALL,
        cost_estimate=pl.CostEstimate(flops=2**30, bytes_accessed=2**25, transcendentals=0),
        name="make_table",
    )(y[None], *after)


def join(parts, after=()):
    size = parts[0].shape[0]

    def body(*refs):
        out = refs[-1]
        for k in range(len(parts)):
            out[pl.ds(k * size, size), :] = refs[k][...]

    vm = pl.BlockSpec(memory_space=pltpu.VMEM)
    return pl.pallas_call(
        body,
        in_specs=[vm] * len(parts) + [pl.BlockSpec(memory_space=pl.ANY)] * len(after),
        out_specs=vm,
        out_shape=jax.ShapeDtypeStruct((size * len(parts),) + parts[0].shape[1:], parts[0].dtype),
        compiler_params=SMALL,
        cost_estimate=COST,
        name="join",
    )(*parts, *after)


def take_rows(traces, y, first, size, after=()):
    rows, part = traces.shape

    def body(y_ref, traces, *refs):
        outs, sems = refs[len(after) : len(after) + NY], refs[len(after) + NY :]
        copies = []
        for k in range(NY):
            at = pl.multiple_of((y_ref[0] + k) % NY * (rows // NY) + first, 16)
            copies.append(pltpu.make_async_copy(traces.at[pl.ds(at, size), :], outs[k], sems[k]))
        for copy in copies:
            copy.start()
        for copy in copies:
            copy.wait()

    hbm, vm = pl.BlockSpec(memory_space=pl.ANY), pl.BlockSpec(memory_space=pltpu.VMEM)
    return pl.pallas_call(
        body,
        in_specs=[pl.BlockSpec(memory_space=pltpu.SMEM), hbm] + [hbm] * len(after),
        out_specs=[vm] * NY,
        out_shape=[jax.ShapeDtypeStruct((size, part), traces.dtype)] * NY,
        scratch_shapes=[pltpu.SemaphoreType.DMA] * NY,
        compiler_params=SMALL,
        cost_estimate=COST,
        name="take_rows",
    )(y[None], traces, *after)


def encode_terms(terms, after):
    def body(a, *refs):
        b = refs[-1]
        code = jnp.clip((a[...] - REC_LOW) * REC_SCALE + 0.5, 0.0, 65535.0).astype(jnp.int32) - 32768
        b[...] = code.astype(jnp.int16)

    vm = pl.BlockSpec(memory_space=pltpu.VMEM)
    return pl.pallas_call(
        body,
        in_specs=[vm] + [pl.BlockSpec(memory_space=pl.ANY)] * len(after),
        out_specs=vm,
        out_shape=jax.ShapeDtypeStruct(terms.shape, jnp.int16),
        compiler_params=SMALL,
        cost_estimate=COST,
        name="encode_terms",
    )(terms, *after)


def spectra(blocks, table, width):
    rows, part = blocks[0].shape
    tile = 512

    def body(b0, b1, b2, b3, t, *outs):
        for k, out in enumerate(outs):
            cols = pl.ds(k * 2 * width, 2 * width)
            acc = None
            for j, b in enumerate((b0, b1, b2, b3)):
                one = jnp.dot(b[...], t[pl.ds(j * part, part), cols], preferred_element_type=jnp.float32)
                acc = one if acc is None else acc + one
            re, im = acc[:, :width], acc[:, width:]
            logamp = 0.5 * jnp.log(re * re + im * im + 1.0)
            code = jnp.minimum(logamp * LA_SCALE + 0.5, 65535.0).astype(jnp.int32) - 32768
            out[...] = code.astype(jnp.int16)

    return pl.pallas_call(
        body,
        grid=(rows // tile,),
        in_specs=[pl.BlockSpec((tile, part), lambda i: (i, 0))] * NY + [pl.BlockSpec(table.shape, lambda i: (0, 0))],
        out_specs=[pl.BlockSpec((tile, width), lambda i: (i, 0))] * NY,
        out_shape=[jax.ShapeDtypeStruct((rows, width), jnp.int16)] * NY,
        compiler_params=MEDIUM,
        cost_estimate=COST,
        name="spectra",
    )(*blocks, table)


def gather_shots(shot_near, shot_at, sizes):
    width = shot_near.shape[1]
    unroll = 64

    def body(shot_at, shot, *outs):
        for k, out in enumerate(outs):

            def step(b, _, out=out, first=sum(sizes[:k])):
                at = [b * unroll + u for u in range(unroll)]
                row = [shot[pl.ds(shot_at[first + i], 1), :] for i in at]
                for i, value in zip(at, row):
                    out[pl.ds(i, 1), :] = value
                return 0

            lax.fori_loop(0, sizes[k] // unroll, step, 0)

    vm, sm = pl.BlockSpec(memory_space=pltpu.VMEM), pl.BlockSpec(memory_space=pltpu.SMEM)
    return pl.pallas_call(
        body,
        in_specs=[sm, vm],
        out_specs=[vm] * len(sizes),
        out_shape=[jax.ShapeDtypeStruct((size, width), jnp.float32) for size in sizes],
        compiler_params=MEDIUM,
        cost_estimate=COST,
        name="gather_shots",
    )(shot_at, shot_near)


def sum_receivers(codes, shots, coded, live, rec_at, held, last):
    rows, width = shots.shape
    size, half = codes[0].shape[0], coded[0].shape[0]
    banks, unroll = 4, 32
    parts, first = len(codes), not held
    given = list(coded) if first else list(held)

    def body(*refs):
        rec_at, live, shots = refs[:3]
        codes, given = refs[3 : 3 + parts], refs[3 + parts :]
        res, outs = given[2 if first else banks + 1], given[3 if first else banks + 2 :]
        rec, sums = outs[0], outs[1 : 1 + banks]
        halves = (pl.ds(0, half), pl.ds(half, half))
        if first:
            for code, at in zip(given[:2], halves):
                rec[at, :] = (code[...].astype(jnp.float32) + 32768.0) * (1.0 / REC_SCALE) + REC_LOW
            rec[pl.ds(2 * half, 8), :] = jnp.zeros((8, width), jnp.float32)
            for s in sums:
                s[...] = jnp.zeros_like(s)
        for k, code in enumerate(codes):
            at = pl.ds(k * size, size)
            logamp = (code[...].astype(jnp.float32) + 32768.0) * (1.0 / LA_SCALE)
            alive = lax.broadcasted_iota(jnp.int32, code.shape, 0) < live[k]
            res[at, :] = jnp.where(alive, logamp - shots[at, :], 0.0)

        def step(b, _):
            for u in range(unroll):
                s, row, at = sums[u % banks], pl.ds(b * unroll + u, 1), pl.ds(rec_at[b * unroll + u], 1)
                value = res[row, :] - rec[at, :]
                s[at, :] = s[at, :] + value
                res[row, :] = value
            return 0

        lax.fori_loop(0, rows // unroll, step, 0)
        if last:
            for out, at in zip(outs[1 + banks :], halves):
                out[...] = (sums[0][at, :] + sums[1][at, :]) + (sums[2][at, :] + sums[3][at, :])

    vm, sm = pl.BlockSpec(memory_space=pltpu.VMEM), pl.BlockSpec(memory_space=pltpu.SMEM)
    shapes = [(rows, width)] + [(2 * half + 8, width)] * (1 + banks) + [(half, width)] * (2 if last else 0)
    return pl.pallas_call(
        body,
        in_specs=[sm, sm] + [vm] * (1 + parts + len(given)),
        out_specs=[vm] * len(shapes),
        out_shape=[jax.ShapeDtypeStruct(shape, jnp.float32) for shape in shapes],
        input_output_aliases={} if first else {3 + parts + k: 1 + k for k in range(1 + banks)},
        compiler_params=SUMS,
        cost_estimate=COST,
        name="sum_receivers",
    )(rec_at, live, shots, *codes, *given)


def sum_shots(residuals, shot_at, count):
    width = residuals[0].shape[1]
    tile = 1024

    def body(shot_at, *refs):
        acc, first = jnp.zeros((count, 2 * width), jnp.float32), 0
        for res in refs[:-1]:
            for k in range(0, res.shape[0], tile):
                value = res[pl.ds(k, tile), :]
                high = value.astype(jnp.bfloat16)
                low = (value - high.astype(jnp.float32)).astype(jnp.bfloat16)
                both = jnp.concatenate([high, low], axis=1)
                hot = lax.broadcasted_iota(jnp.int32, (count, tile), 0) == shot_at[:, pl.ds(first + k, tile)]
                acc = acc + jnp.dot(hot.astype(jnp.bfloat16), both, preferred_element_type=jnp.float32)
            first += res.shape[0]
        refs[-1][...] = acc[:, :width] + acc[:, width:]

    vm = pl.BlockSpec(memory_space=pltpu.VMEM)
    return pl.pallas_call(
        body,
        in_specs=[vm] * (1 + len(residuals)),
        out_specs=vm,
        out_shape=jax.ShapeDtypeStruct((count, width), jnp.float32),
        compiler_params=MEDIUM,
        cost_estimate=COST,
        name="sum_shots",
    )(shot_at[None, :], *residuals)


def neighbour(value, by):
    size = NZ * NX * NC
    return lax.ppermute(value, "tr", [(i, i + by) for i in range(size) if 0 <= i + by < size])


def per_device(traces, shot_index, receiver_index, live_counts, shot_terms, receiver_terms):
    rows, part = traces.shape
    block, width = shot_terms.shape
    share = rows // NY
    first = [sum(PIECES[:h]) for h in range(len(PIECES))]
    owner, y = lax.axis_index("tr"), lax.axis_index("fq")
    z, x, c = owner // (NX * NC), owner // NC % NX, owner % NC

    got, after = [], ()
    for at, size in zip(first, PIECES):
        if after:
            mine = take_rows(traces, y, at, size, after)
        else:
            mine = [lax.dynamic_slice_in_dim(traces, (y + k) % NY * share + at, size, 0) for k in range(NY)]
        come = {k: send_y(mine[k], k) for k in (1, 3, 2)}
        after = [come[k] for k in range(1, NY)]
        got.append([mine[0]] + after)
    table = make_table(part * NY, y, width, got[0][:1])
    codes, coded = [], []
    for blocks in got:
        coded.append(spectra(blocks, table, width))
        codes += [send_y(coded[-1][k], k) if k else coded[-1][k] for k in range(NY)]

    def ordered(v):
        v = v.reshape(NY, share)
        v = jnp.stack([lax.dynamic_index_in_dim(v, (y - k) % NY, 0, keepdims=False) for k in range(NY)])
        return jnp.concatenate([v[:, at : at + size].reshape(NY * size) for at, size in zip(first, PIECES)])

    near = receiver_index // block
    rz, rx, rc = near // (NX * NC), near // NC % NX, near % NC
    turn = rz ^ z
    place = (((rc ^ c) * NX + (rx ^ x)) * 2 + (turn & 1)) * (NZ // 2) + turn // 2
    place = place * block + receiver_index % block
    spare = block * NZ * NX * NC
    rec_at = ordered(jnp.where(jnp.arange(rows, dtype=jnp.int32) < live_counts[0], place, spare))
    shot_at = ordered(shot_index - (owner - 1) * block)
    live = live_counts[0] - jnp.stack([(y - k) % NY * share + at for at in first for k in range(NY)])

    shot_terms = join([shot_terms], (table,))
    shot_near = jnp.concatenate([neighbour(shot_terms, 1), shot_terms, neighbour(shot_terms, -1)])
    terms = encode_terms(receiver_terms, (table,))
    terms = join([terms, swap(terms, 2, 0, 0)])
    terms = join([terms, swap(terms, 4, 0, 0)], got[0][1:] + [shot_near])
    terms = join([terms, swap(terms, 1, 0, 0)], got[1][:1])
    shots = gather_shots(shot_near, shot_at, [size * NY for size in PIECES])
    terms = join([terms, swap(terms, 0, 1, 0)], [coded[0][0]])
    terms = join([terms, swap(terms, 0, 2, 0)], [shots[0], rec_at] + got[1][1:])
    far_terms = swap(terms, 0, 0, 1)

    held, residuals, done = [], [], 0
    for h, part_shots in enumerate(shots):
        some, last = slice(h * NY, (h + 1) * NY), h == len(shots) - 1
        at = rec_at[done : done + part_shots.shape[0]]
        done += part_shots.shape[0]
        resid, *held = sum_receivers(codes[some], part_shots, [terms, far_terms], live[some], at, held, last)
        residuals.append(resid)
    sums, far_sums = held[-2:]
    sums = (sums + swap(far_sums, 0, 0, 1)).reshape(NX, 2, NZ // 2 * block, width)
    shots = sum_shots(residuals, shot_at, 3 * block)
    sent = (sums * SUM_SCALE).astype(jnp.float16)
    halves = [None, None]
    for h in (1, 0):
        come = [swap(sent[k, h], 0, k, 0).astype(jnp.float32) for k in (1, 3, 2)]
        mine = join([sums[0, h]], (shots,)) if h else sums[0, h]
        halves[h] = mine + (come[0] + come[1] + come[2]) * (1.0 / SUM_SCALE)
    shots = join([shots], (halves[1],))
    shot_sums = shots[block : 2 * block] + neighbour(shots[2 * block :], 1) + neighbour(shots[:block], -1)
    sent = (halves[1] * SUM_SCALE).astype(jnp.float16)
    sums = join(halves[:1], (shot_sums,)) + swap(sent, 1, 0, 0).astype(jnp.float32) * (1.0 / SUM_SCALE)
    sums = sums.reshape(2, 2, block, width)
    sent = (sums[:, 1] * SUM_SCALE).astype(jnp.float16)
    sums = sums[:, 0] + swap(sent, 2, 0, 0).astype(jnp.float32) * (1.0 / SUM_SCALE)
    sent = (sums[1] * SUM_SCALE).astype(jnp.float16)
    receiver_sums = sums[0] + swap(sent, 4, 0, 0).astype(jnp.float32) * (1.0 / SUM_SCALE)
    return (shot_sums, receiver_sums)


def solution(mesh):
    return jax.shard_map(
        per_device,
        mesh=mesh,
        in_specs=(P("tr", "fq"), P("tr"), P("tr"), P("tr"), P("tr", "fq"), P("tr", "fq")),
        out_specs=(P("tr", "fq"), P("tr", "fq")),
        check_vma=False,
    )
```

```python
import math

import jax
import jax.numpy as jnp
from jax import lax
from jax.experimental import pallas as pl
from jax.experimental.pallas import tpu as pltpu
from jax.sharding import PartitionSpec as P

NZ, NX, NC, NY = 8, 4, 2, 4
LA_TOP = 9.1
LA_SCALE = 65535.0 / LA_TOP
REC_LOW, REC_HIGH = 1.0, 2.2
REC_SCALE = 65535.0 / (REC_HIGH - REC_LOW)
SUM_SCALE = 1.0 / 32.0
PIECES = (1024, 1024)
LARGE = pltpu.CompilerParams(vmem_limit_bytes=60 * 2**20)
SUMS = pltpu.CompilerParams(vmem_limit_bytes=20 * 2**20)
SMALL = pltpu.CompilerParams(vmem_limit_bytes=12 * 2**20)
COST = pl.CostEstimate(flops=1000, bytes_accessed=1000, transcendentals=0)
MEDIUM = pltpu.CompilerParams(vmem_limit_bytes=18 * 2**20)


def tr_of(z, x, c):
    return (z * NX + x) * NC + c


def sites():
    return [(z, x, c) for z in range(NZ) for x in range(NX) for c in range(NC)]


def swap(value, dz, dx, dc):
    return lax.ppermute(value, "tr", [(tr_of(z, x, c), tr_of(z ^ dz, x ^ dx, c ^ dc)) for z, x, c in sites()])


def send_y(value, k):
    return lax.ppermute(value, "fq", [(i, (i + k) % NY) for i in range(NY)])


def make_table(samples, y, width, after):
    part, cols = samples // NY, NY * 2 * width
    tile = 128
    quarter = samples // 4
    shift = quarter.bit_length() - 1

    def body(y_ref, *refs):
        y, out = y_ref[0], refs[-1]
        row = pl.program_id(0) * tile
        time = (y - row // part) % NY * part + row % part + lax.broadcasted_iota(jnp.int32, (tile, 1), 0)
        for k in range(NY):
            first = (y + k) % NY * width
            for half in range(2):
                freq = first + lax.broadcasted_iota(jnp.int32, (1, width), 1)
                phase = (time * freq + half * quarter) & (samples - 1)
                turn = lax.shift_right_logical(phase + quarter // 2, shift)
                rest = (phase - turn * quarter).astype(jnp.float32) * (2.0 * math.pi / samples)
                sq = rest * rest
                cos = 1.0 + sq * (-0.5 + sq * (1 / 24 + sq * (-1 / 720 + sq * (1 / 40320 - sq * (1 / 3628800)))))
                sin = rest * (1.0 + sq * (-1 / 6 + sq * (1 / 120 + sq * (-1 / 5040 + sq * (1 / 362880)))))
                value = jnp.where((turn & 1) == 1, sin, cos)
                value = jnp.where(((turn + 1) & 2) == 2, -value, value)
                out[:, pl.ds((2 * k + half) * width, width)] = value.astype(jnp.bfloat16)

    return pl.pallas_call(
        body,
        grid=(samples // tile,),
        in_specs=[pl.BlockSpec(memory_space=pltpu.SMEM)] + [pl.BlockSpec(memory_space=pl.ANY)] * len(after),
        out_specs=pl.BlockSpec((tile, cols), lambda i: (i, 0)),
        out_shape=jax.ShapeDtypeStruct((samples, cols), jnp.bfloat16),
        compiler_params=SMALL,
        cost_estimate=pl.CostEstimate(flops=2**30, bytes_accessed=2**25, transcendentals=0),
        name="make_table",
    )(y[None], *after)


def join(parts, after=()):
    size = parts[0].shape[0]

    def body(*refs):
        out = refs[-1]
        for k in range(len(parts)):
            out[pl.ds(k * size, size), :] = refs[k][...]

    vm = pl.BlockSpec(memory_space=pltpu.VMEM)
    return pl.pallas_call(
        body,
        in_specs=[vm] * len(parts) + [pl.BlockSpec(memory_space=pl.ANY)] * len(after),
        out_specs=vm,
        out_shape=jax.ShapeDtypeStruct((size * len(parts),) + parts[0].shape[1:], parts[0].dtype),
        compiler_params=SMALL,
        cost_estimate=COST,
        name="join",
    )(*parts, *after)


def tie(values, after):
    hbm = pl.BlockSpec(memory_space=pl.ANY)
    return pl.pallas_call(
        lambda *refs: None,
        in_specs=[hbm] * (len(values) + len(after)),
        out_specs=[hbm] * len(values),
        out_shape=[jax.ShapeDtypeStruct(value.shape, value.dtype) for value in values],
        input_output_aliases={k: k for k in range(len(values))},
        compiler_params=SMALL,
        cost_estimate=COST,
        name="tie",
    )(*values, *after)


def encode_terms(terms, after):
    def body(a, *refs):
        b = refs[-1]
        code = jnp.clip((a[...] - REC_LOW) * REC_SCALE + 0.5, 0.0, 65535.0).astype(jnp.int32) - 32768
        b[...] = code.astype(jnp.int16)

    vm = pl.BlockSpec(memory_space=pltpu.VMEM)
    return pl.pallas_call(
        body,
        in_specs=[vm] + [pl.BlockSpec(memory_space=pl.ANY)] * len(after),
        out_specs=vm,
        out_shape=jax.ShapeDtypeStruct(terms.shape, jnp.int16),
        compiler_params=SMALL,
        cost_estimate=COST,
        name="encode_terms",
    )(terms, *after)


def spectra(blocks, table, width):
    rows, part = blocks[0].shape
    tile = 512

    def body(b0, b1, b2, b3, t, *outs):
        for k, out in enumerate(outs):
            cols = pl.ds(k * 2 * width, 2 * width)
            acc = None
            for j, b in enumerate((b0, b1, b2, b3)):
                one = jnp.dot(b[...], t[pl.ds(j * part, part), cols], preferred_element_type=jnp.float32)
                acc = one if acc is None else acc + one
            re, im = acc[:, :width], acc[:, width:]
            logamp = 0.5 * jnp.log(re * re + im * im + 1.0)
            code = jnp.minimum(logamp * LA_SCALE + 0.5, 65535.0).astype(jnp.int32) - 32768
            out[...] = code.astype(jnp.int16)

    return pl.pallas_call(
        body,
        grid=(rows // tile,),
        in_specs=[pl.BlockSpec((tile, part), lambda i: (i, 0))] * NY + [pl.BlockSpec(table.shape, lambda i: (0, 0))],
        out_specs=[pl.BlockSpec((tile, width), lambda i: (i, 0))] * NY,
        out_shape=[jax.ShapeDtypeStruct((rows, width), jnp.int16)] * NY,
        compiler_params=MEDIUM,
        cost_estimate=COST,
        name="spectra",
    )(*blocks, table)


def gather_shots(shot_near, shot_at, sizes):
    width = shot_near.shape[1]
    unroll = 64

    def body(shot_at, shot, *outs):
        for k, out in enumerate(outs):

            def step(b, _, out=out, first=sum(sizes[:k])):
                at = [b * unroll + u for u in range(unroll)]
                row = [shot[pl.ds(shot_at[first + i], 1), :] for i in at]
                for i, value in zip(at, row):
                    out[pl.ds(i, 1), :] = value
                return 0

            lax.fori_loop(0, sizes[k] // unroll, step, 0)

    vm, sm = pl.BlockSpec(memory_space=pltpu.VMEM), pl.BlockSpec(memory_space=pltpu.SMEM)
    return pl.pallas_call(
        body,
        in_specs=[sm, vm],
        out_specs=[vm] * len(sizes),
        out_shape=[jax.ShapeDtypeStruct((size, width), jnp.float32) for size in sizes],
        compiler_params=MEDIUM,
        cost_estimate=COST,
        name="gather_shots",
    )(shot_at, shot_near)


def sum_receivers(codes, shots, coded, live, rec_at, held, last):
    rows, width = shots.shape
    size, half = codes[0].shape[0], coded[0].shape[0]
    banks, unroll = 4, 32
    parts, first = len(codes), not held
    given = list(coded) if first else list(held)

    def body(*refs):
        rec_at, live, shots = refs[:3]
        codes, given = refs[3 : 3 + parts], refs[3 + parts :]
        res, outs = given[2 if first else banks + 1], given[3 if first else banks + 2 :]
        rec, sums = outs[0], outs[1 : 1 + banks]
        halves = (pl.ds(0, half), pl.ds(half, half))
        if first:
            for code, at in zip(given[:2], halves):
                rec[at, :] = (code[...].astype(jnp.float32) + 32768.0) * (1.0 / REC_SCALE) + REC_LOW
            rec[pl.ds(2 * half, 8), :] = jnp.zeros((8, width), jnp.float32)
            for s in sums:
                s[...] = jnp.zeros_like(s)
        for k, code in enumerate(codes):
            at = pl.ds(k * size, size)
            logamp = (code[...].astype(jnp.float32) + 32768.0) * (1.0 / LA_SCALE)
            alive = lax.broadcasted_iota(jnp.int32, code.shape, 0) < live[k]
            res[at, :] = jnp.where(alive, logamp - shots[at, :], 0.0)

        def step(b, _):
            for u in range(unroll):
                s, row, at = sums[u % banks], pl.ds(b * unroll + u, 1), pl.ds(rec_at[b * unroll + u], 1)
                value = res[row, :] - rec[at, :]
                s[at, :] = s[at, :] + value
                res[row, :] = value
            return 0

        lax.fori_loop(0, rows // unroll, step, 0)
        if last:
            for out, at in zip(outs[1 + banks :], halves):
                out[...] = (sums[0][at, :] + sums[1][at, :]) + (sums[2][at, :] + sums[3][at, :])

    vm, sm = pl.BlockSpec(memory_space=pltpu.VMEM), pl.BlockSpec(memory_space=pltpu.SMEM)
    shapes = [(rows, width)] + [(2 * half + 8, width)] * (1 + banks) + [(half, width)] * (2 if last else 0)
    return pl.pallas_call(
        body,
        in_specs=[sm, sm] + [vm] * (1 + parts + len(given)),
        out_specs=[vm] * len(shapes),
        out_shape=[jax.ShapeDtypeStruct(shape, jnp.float32) for shape in shapes],
        input_output_aliases={} if first else {3 + parts + k: 1 + k for k in range(1 + banks)},
        compiler_params=SUMS,
        cost_estimate=COST,
        name="sum_receivers",
    )(rec_at, live, shots, *codes, *given)


def sum_shots(residuals, shot_at, count):
    width = residuals[0].shape[1]
    tile = 1024

    def body(shot_at, *refs):
        acc, first = jnp.zeros((count, 2 * width), jnp.float32), 0
        for res in refs[:-1]:
            for k in range(0, res.shape[0], tile):
                value = res[pl.ds(k, tile), :]
                high = value.astype(jnp.bfloat16)
                low = (value - high.astype(jnp.float32)).astype(jnp.bfloat16)
                both = jnp.concatenate([high, low], axis=1)
                hot = lax.broadcasted_iota(jnp.int32, (count, tile), 0) == shot_at[:, pl.ds(first + k, tile)]
                acc = acc + jnp.dot(hot.astype(jnp.bfloat16), both, preferred_element_type=jnp.float32)
            first += res.shape[0]
        refs[-1][...] = acc[:, :width] + acc[:, width:]

    vm = pl.BlockSpec(memory_space=pltpu.VMEM)
    return pl.pallas_call(
        body,
        in_specs=[vm] * (1 + len(residuals)),
        out_specs=vm,
        out_shape=jax.ShapeDtypeStruct((count, width), jnp.float32),
        compiler_params=MEDIUM,
        cost_estimate=COST,
        name="sum_shots",
    )(shot_at[None, :], *residuals)


def neighbour(value, by):
    size = NZ * NX * NC
    return lax.ppermute(value, "tr", [(i, i + by) for i in range(size) if 0 <= i + by < size])


def per_device(traces, shot_index, receiver_index, live_counts, shot_terms, receiver_terms):
    rows, part = traces.shape
    block, width = shot_terms.shape
    share = rows // NY
    first = [sum(PIECES[:h]) for h in range(len(PIECES))]
    owner, y = lax.axis_index("tr"), lax.axis_index("fq")
    z, x, c = owner // (NX * NC), owner // NC % NX, owner % NC

    got = []
    for at, size in zip(first, PIECES):
        mine = [lax.dynamic_slice_in_dim(traces, (y + k) % NY * share + at, size, 0) for k in range(NY)]
        if got:
            mine[1:] = tie(mine[1:], got[0][1:])
        come = {k: send_y(mine[k], k) for k in (1, 3, 2)}
        got.append([mine[0]] + [come[k] for k in range(1, NY)])
    table = make_table(part * NY, y, width, got[0][:1])
    codes, coded = [], []
    for blocks in got:
        coded.append(spectra(blocks, table, width))
        codes += [send_y(coded[-1][k], k) if k else coded[-1][k] for k in range(NY)]

    def ordered(v):
        v = v.reshape(NY, share)
        v = jnp.stack([lax.dynamic_index_in_dim(v, (y - k) % NY, 0, keepdims=False) for k in range(NY)])
        return jnp.concatenate([v[:, at : at + size].reshape(NY * size) for at, size in zip(first, PIECES)])

    near = receiver_index // block
    rz, rx, rc = near // (NX * NC), near // NC % NX, near % NC
    turn = rz ^ z
    place = (((rc ^ c) * NX + (rx ^ x)) * 2 + (turn & 1)) * (NZ // 2) + turn // 2
    place = place * block + receiver_index % block
    spare = block * NZ * NX * NC
    rec_at = ordered(jnp.where(jnp.arange(rows, dtype=jnp.int32) < live_counts[0], place, spare))
    shot_at = ordered(shot_index - (owner - 1) * block)
    live = live_counts[0] - jnp.stack([(y - k) % NY * share + at for at in first for k in range(NY)])

    shot_terms = join([shot_terms], (table,))
    shot_near = jnp.concatenate([neighbour(shot_terms, 1), shot_terms, neighbour(shot_terms, -1)])
    terms = encode_terms(receiver_terms, (table,))
    terms = join([terms, swap(terms, 2, 0, 0)])
    terms = join([terms, swap(terms, 4, 0, 0)], got[0][1:] + [shot_near])
    terms = join([terms, swap(terms, 1, 0, 0)])
    shots = gather_shots(shot_near, shot_at, [size * NY for size in PIECES])
    terms = join([terms, swap(terms, 0, 1, 0)], [coded[0][0]])
    terms = join([terms, swap(terms, 0, 2, 0)], [shots[0], rec_at] + got[1][1:])
    far_terms = swap(terms, 0, 0, 1)

    held, residuals, done = [], [], 0
    for h, part_shots in enumerate(shots):
        some, last = slice(h * NY, (h + 1) * NY), h == len(shots) - 1
        at = rec_at[done : done + part_shots.shape[0]]
        done += part_shots.shape[0]
        resid, *held = sum_receivers(codes[some], part_shots, [terms, far_terms], live[some], at, held, last)
        residuals.append(resid)
    sums, far_sums = held[-2:]
    sums = (sums + swap(far_sums, 0, 0, 1)).reshape(NX, 2, NZ // 2, block, width)
    shots = sum_shots(residuals, shot_at, 3 * block)
    sent = (sums * SUM_SCALE).astype(jnp.float16)
    come = [swap(sent[k], 0, k, 0).astype(jnp.float32) for k in (1, 3, 2)]
    mine = join([sums[0].reshape(-1, width)], (shots,)).reshape(sums.shape[1:])
    sums = mine + (come[0] + come[1] + come[2]) * (1.0 / SUM_SCALE)
    shot_sums = shots[block : 2 * block] + neighbour(shots[2 * block :], 1) + neighbour(shots[:block], -1)
    sent = (sums[1] * SUM_SCALE).astype(jnp.float16)
    mine = join([sums[0].reshape(-1, width)], (shot_sums,)).reshape(sums.shape[1:])
    sums = mine + swap(sent, 1, 0, 0).astype(jnp.float32) * (1.0 / SUM_SCALE)
    sums = sums.reshape(2, 2, block, width)
    sent = (sums[:, 1] * SUM_SCALE).astype(jnp.float16)
    sums = sums[:, 0] + swap(sent, 2, 0, 0).astype(jnp.float32) * (1.0 / SUM_SCALE)
    sent = (sums[1] * SUM_SCALE).astype(jnp.float16)
    receiver_sums = sums[0] + swap(sent, 4, 0, 0).astype(jnp.float32) * (1.0 / SUM_SCALE)
    return (shot_sums, receiver_sums)


def solution(mesh):
    return jax.shard_map(
        per_device,
        mesh=mesh,
        in_specs=(P("tr", "fq"), P("tr"), P("tr"), P("tr"), P("tr", "fq"), P("tr", "fq")),
        out_specs=(P("tr", "fq"), P("tr", "fq")),
        check_vma=False,
    )
```
